256 devices in a mesh: sp: 64 (over z, x, core), dp: 4 (over y).
Axes of the slice: x: 4, y: 4, z: 8, core: 2. Of those that a mesh axis runs over, the one named last changes fastest.
Arguments:
- grid_tokens: bfloat16 [4, 64, 128, 1024], P('dp', 'sp'), may hold values from -6 to 6
- cotangent: bfloat16 [4, 64, 128, 1024], P('dp', 'sp'), may hold values from -6 to 6
- obs_pairs: bfloat16 [4, 64, 96, 2048], P('dp', 'sp'), may hold values from -6 to 6
- obs_route: int32 [4, 64, 96, 1], P('dp', 'sp'), may hold values from 0 to 63; in each aligned block of 96 rows (0 to 95, 96 to 191, ..., all dimensions but the last counted through in order) at most 3 rows name the same one
- obs_patch: int32 [4, 64, 96], P('dp', 'sp'), may hold values from 0 to 3
- w_query: bfloat16 [1024, 1024], P('dp'), may hold values from -0.1875 to 0.1875
- w_cross_out: bfloat16 [1024, 1024], P('dp'), may hold values from -0.1875 to 0.1875
- w_qkv: bfloat16 [1024, 3072], P('dp'), may hold values from -0.1875 to 0.1875
- w_axial_out: bfloat16 [1024, 1024], P('dp'), may hold values from -0.1875 to 0.1875
- w_in: bfloat16 [1024, 2048], replicated, may hold values from -0.1875 to 0.1875
- w_out: bfloat16 [2048, 1024], replicated, may hold values from -0.125 to 0.125
Outputs:
- grad_w_in: float32 [1024, 2048], P(('sp', 'dp'))
- grad_w_out: float32 [2048, 1024], P(('sp', 'dp'))
The draws below stay inside these ranges and needn't reach their ends.
Inputs may be any that keep to these rules, and one draw needn't show every extreme that they name: `obs_route`: at most 3 of the 96 observations of one device fall in one latitude row, and in every draw some device sends exactly 3 to some row.
All inputs are finite; a program needn't handle non-finite values.
Results may differ from the reference program's by a relative error of at most 0.024.
Values may be sent and summed in bfloat16 or wider, within the bound.
A program may use at most 128 MiB of HBM per device.

```python
import math
import jax
import jax.numpy as jnp
import numpy as np
from jax import lax

D = 1024
HEADS = 16
FF = 2048
LONP = 128
PATCH = 32
PATCHES = 4
OBS_DEV = 96
CAP = 3
NLAT = 64
MEMBERS = 4
N_SP = 64


def draw_grid_tokens(key, part):
    noise_part = jax.random.normal(jax.random.fold_in(key, 11), (MEMBERS, NLAT, LONP, D), jnp.float32)
    values = noise_part
    return jnp.clip(values, -6.0, 6.0).astype(jnp.bfloat16)


def draw_obs_pairs(key, part):
    noise_part = jax.random.normal(jax.random.fold_in(key, 21), (MEMBERS, NLAT, OBS_DEV, 2 * D), jnp.float32)
    values = noise_part
    return jnp.clip(values, -6.0, 6.0).astype(jnp.bfloat16)


def draw_w_query(key, part):
    weight_scale = D ** (-0.5)
    base_part = jax.random.normal(jax.random.fold_in(key, 31), (D, D), jnp.float32) * weight_scale
    return jnp.clip(base_part, -6.0 * weight_scale, 6.0 * weight_scale).astype(jnp.bfloat16)


def draw_w_qkv(key, part):
    weight_scale = D ** (-0.5)
    base_part = jax.random.normal(jax.random.fold_in(key, 41), (D, 3 * D), jnp.float32) * weight_scale
    return jnp.clip(base_part, -6.0 * weight_scale, 6.0 * weight_scale).astype(jnp.bfloat16)


def plant(drawn, own_key, low, largest):
    longest = drawn.shape.index(max(drawn.shape))
    spots = []
    for shift in (0, 1):
        where = [jax.random.randint(jax.random.fold_in(own_key, axis), (), 0, length) for axis, length in enumerate(drawn.shape)]
        where[longest] = (where[longest] + shift) % drawn.shape[longest]
        spots.append(tuple(where))
    return drawn.at[spots[0]].set(low).at[spots[1]].set(largest)


def block_scale(rng, shape, shards, low, largest):
    def one(axis_at, parts):
        heights = jax.random.uniform(jax.random.fold_in(jax.random.fold_in(rng, 6), axis_at), (parts,), jnp.float32, low / len(shards), largest / len(shards))
        return jnp.repeat(jnp.exp(heights), shape[axis_at] // parts).reshape((-1,) + (1,) * (len(shape) - axis_at - 1))

    factor_of = one(*shards[0])
    for cut in shards[1:]:
        factor_of = factor_of * one(*cut)
    return factor_of


def assign_block(own_key, own, number, rows, number_of, top, reach, lean):
    order = jax.random.permutation(own_key, number_of)
    packed, common = load_shares(number_of, rows * top, reach, lean, True), load_shares(number_of, rows * top, reach, lean, False)
    places = jnp.arange(number_of)

    def named(lengths, offset_by):
        used = int((lengths > 0).sum())
        fixed = max(1, used // 4)
        passed = fixed + (places - fixed + offset_by * (used - fixed)) % max(1, number_of - fixed)
        return jnp.zeros((number_of,), jnp.int32).at[order[jnp.where(places < fixed, places, passed)]].set(jnp.asarray(lengths, jnp.int32))

    lengths = jnp.where(number % 4 == 0, named(packed, number // 4), named(common, number - number // 4 - 1))
    mixed = jax.random.permutation(jax.random.fold_in(own, 3), number_of)
    giver, sink = mixed[0:number_of // 2 * 2:2], mixed[1:number_of // 2 * 2:2]
    margin = jnp.minimum(lengths[giver] - 1, reach - lengths[sink]) // 2
    margin = jnp.where((giver == order[0]) | (sink == order[0]) | (lengths[sink] == 0), 0, jnp.maximum(margin, 0))
    passed = jax.random.randint(jax.random.fold_in(own, 4), (number_of // 2,), 0, 1 << 20) % (margin + 1)
    lengths = lengths.at[giver].add(-passed).at[sink].add(passed)
    labels = jnp.searchsorted(jnp.cumsum(lengths), jnp.arange(rows * top), side="right").astype(jnp.int32)
    table = labels.reshape(top, rows).T
    table = table[jax.random.permutation(jax.random.fold_in(own, 1), rows)]
    offset_by = jax.random.randint(jax.random.fold_in(own, 2), (rows, 1), 0, top)
    return jnp.take_along_axis(table, (jnp.arange(top)[None, :] + offset_by) % top, axis=1)


def load_shares(amount, total, reach, skew, full):
    weights = [(1 << 20) // math.isqrt(rank ** skew) + 1 for rank in range(1, amount + 1)]
    largest = reach if full else min(reach, max(-(-total // amount), total * weights[0] // sum(weights)))
    least = 1 if total - largest >= amount - 1 else 0
    given, surplus = [largest] + [least] * (amount - 1), total - largest - least * (amount - 1)
    while surplus > 0:
        movable = [i for i in range(1, amount) if given[i] < largest] or [i for i in range(1, amount) if given[i] < reach]
        mass, budget = sum([weights[i] for i in movable]), surplus
        for i in movable:
            extra = min(reach - given[i], max(1, budget * weights[i] // mass), surplus)
            given[i] = given[i] + extra
            surplus = surplus - extra
    return np.array(given)


def normal_values(own_key, shape, scale, reach, cuts=(), kind=jnp.bfloat16):
    drawn = jax.random.normal(own_key, shape, jnp.float32) * scale
    if len(cuts) > 0:
        drawn = block_scale(own_key, shape, cuts, -0.22, 0.18) * drawn
    return jnp.clip(drawn, min=-reach, max=reach).astype(kind)


def setup_inputs(seed: int = 0) -> dict:
    keys = jax.random.split(jax.random.key(seed), 12)
    grid_tokens = draw_grid_tokens(jax.random.fold_in(keys[11], 71), 0)
    cotangent = normal_values(keys[1], (MEMBERS, NLAT, LONP, D), 1.0, 6.0, ((0, 4), (1, 64)))
    obs_pairs = draw_obs_pairs(jax.random.fold_in(keys[11], 71), 0)
    obs_route_keys = jax.random.split(jax.random.fold_in(keys[3], 1), MEMBERS * NLAT * OBS_DEV // OBS_DEV)
    obs_route_turns = jax.random.permutation(jax.random.fold_in(keys[3], 3), MEMBERS * NLAT * OBS_DEV // OBS_DEV)
    obs_route = jax.vmap(lambda own, number: assign_block(jax.random.fold_in(keys[3], 2), own, number, OBS_DEV, N_SP, 1, CAP, 2))(obs_route_keys, obs_route_turns).reshape((MEMBERS, NLAT, OBS_DEV, 1))
    obs_patch = plant(jax.random.randint(keys[4], (MEMBERS, NLAT, OBS_DEV), 0, PATCHES), jax.random.fold_in(keys[4], 1), 0, PATCHES - 1).astype(jnp.int32)
    w_query = draw_w_query(jax.random.fold_in(keys[11], 71), 0)
    w_cross_out = normal_values(keys[6], (D, D), D ** -0.5, 0.1875, ((0, 4),))
    w_qkv = draw_w_qkv(jax.random.fold_in(keys[11], 71), 0)
    w_axial_out = normal_values(keys[8], (D, D), D ** -0.5, 0.1875, ((0, 4),))
    w_in = normal_values(keys[9], (D, FF), D ** -0.5, 0.1875)
    w_out = normal_values(keys[10], (FF, D), FF ** -0.5, 0.125)
    return dict(grid_tokens=grid_tokens, cotangent=cotangent, obs_pairs=obs_pairs, obs_route=obs_route, obs_patch=obs_patch, w_query=w_query, w_cross_out=w_cross_out, w_qkv=w_qkv, w_axial_out=w_axial_out, w_in=w_in, w_out=w_out)


norm_epsilon = 1e-06
root_half = 0.7071067811865476
inv_root_two_pi = 0.3989422804014327

def normalize(values):
    values = values.astype(jnp.float32)
    return values * lax.rsqrt(lax.optimization_barrier(jnp.mean(values * values, axis=-1, keepdims=True)) + norm_epsilon)

def gelu_exact(pre_act):
    return 0.5 * pre_act * (1.0 + jax.scipy.special.erf(pre_act * root_half))

def gelu_slope(pre_act):
    return 0.5 * (1.0 + jax.scipy.special.erf(pre_act * root_half)) + pre_act * jnp.exp(-0.5 * pre_act * pre_act) * inv_root_two_pi

def slot_ranks(destination):
    onehot = (destination[:, None] == jnp.arange(N_SP, dtype=jnp.int32)[None, :]).astype(jnp.int32)
    return lax.optimization_barrier(jnp.sum(jnp.cumsum(onehot, axis=0) * onehot, axis=1)) - 1

def softmax_rows(scores):
    row_max = lax.optimization_barrier(jnp.max(scores, axis=-1, keepdims=True))
    exp_terms = jnp.exp(scores - row_max)
    return exp_terms / lax.optimization_barrier(jnp.sum(exp_terms, axis=-1, keepdims=True))

def cross_block(tokens, received, received_patch, w_query, w_cross_out):
    head_size = D // HEADS
    normed = normalize(tokens).astype(jnp.bfloat16)
    queries = jnp.dot(normed, w_query, preferred_element_type=jnp.float32).astype(jnp.bfloat16)
    query_heads = queries.reshape(LONP, HEADS, head_size).astype(jnp.float32)
    key_heads = received[:, :D].reshape(-1, HEADS, head_size).astype(jnp.float32)
    value_heads = received[:, D:].reshape(-1, HEADS, head_size).astype(jnp.float32)
    scores = jnp.einsum('lhe,she->hls', query_heads, key_heads) * head_size ** (-0.5)
    cell_patch = jnp.arange(LONP, dtype=jnp.int32) // PATCH
    same_patch = received_patch[None, None, :] == cell_patch[None, :, None]
    masked = jnp.where(same_patch, scores, -1e+30)
    row_max = jnp.maximum(lax.optimization_barrier(jnp.max(masked, axis=-1, keepdims=True)), 0.0)
    exp_terms = jnp.where(same_patch, jnp.exp(masked - row_max), 0.0)
    denominator = jnp.exp(-row_max) + lax.optimization_barrier(jnp.sum(exp_terms, axis=-1, keepdims=True))
    weights = (exp_terms / denominator).astype(jnp.bfloat16)
    context = jnp.einsum('hls,she->lhe', weights.astype(jnp.float32), value_heads)
    context = context.reshape(LONP, D).astype(jnp.bfloat16)
    return (tokens.astype(jnp.float32) + jnp.dot(context, w_cross_out, preferred_element_type=jnp.float32)).astype(jnp.bfloat16)

def member_grads(grid_member, cot_member, pairs_member, route_member, patch_member, w_query, w_cross_out, w_qkv, w_axial_out, w_in, w_out):
    head_size = D // HEADS
    half_width = D // 2
    groups = HEADS // 4
    destination = route_member[:, :, 0]
    source_ids = jnp.arange(N_SP, dtype=jnp.int32)[:, None]
    ranks = jax.vmap(slot_ranks)(destination)
    slot_global = (destination * (N_SP * CAP) + source_ids * CAP + ranks).reshape(-1)
    received = jnp.zeros((N_SP * N_SP * CAP, 2 * D), jnp.bfloat16).at[slot_global].set(pairs_member.reshape(-1, 2 * D))
    received = received.reshape(N_SP, N_SP * CAP, 2 * D)
    received_patch = jnp.full((N_SP * N_SP * CAP,), -1, jnp.int32).at[slot_global].set(patch_member.reshape(-1))
    received_patch = received_patch.reshape(N_SP, N_SP * CAP)

    def one_row(triple):
        return cross_block(triple[0], triple[1], triple[2], w_query, w_cross_out)
    after_cross = lax.map(one_row, (grid_member, received, received_patch))
    normed = normalize(after_cross).astype(jnp.bfloat16)
    axial = jnp.dot(normed.reshape(-1, D), w_qkv, preferred_element_type=jnp.float32).astype(jnp.bfloat16)
    axial = axial.reshape(N_SP, LONP, 3 * D)
    lat_part = axial[..., :3 * half_width].reshape(N_SP, LONP, groups, 3, 2, head_size).astype(jnp.float32)
    lat_scores = jnp.einsum('alghe,blghe->lghab', lat_part[:, :, :, 0], lat_part[:, :, :, 1]) * head_size ** (-0.5)
    lat_weights = softmax_rows(lat_scores).astype(jnp.bfloat16).astype(jnp.float32)
    lat_context = jnp.einsum('lghab,blghe->alghe', lat_weights, lat_part[:, :, :, 2])
    lat_context = lat_context.reshape(N_SP, LONP, half_width).astype(jnp.bfloat16)
    lon_part = axial[..., 3 * half_width:].reshape(N_SP, LONP, 3, HEADS // 2, head_size).astype(jnp.float32)
    lon_scores = jnp.einsum('alhe,amhe->ahlm', lon_part[:, :, 0], lon_part[:, :, 1]) * head_size ** (-0.5)
    lon_weights = softmax_rows(lon_scores).astype(jnp.bfloat16).astype(jnp.float32)
    lon_context = jnp.einsum('ahlm,amhe->alhe', lon_weights, lon_part[:, :, 2])
    lon_context = lon_context.reshape(N_SP, LONP, half_width).astype(jnp.bfloat16)
    context = jnp.concatenate([lat_context, lon_context], axis=-1).reshape(-1, D)
    after_axial = (after_cross.reshape(-1, D).astype(jnp.float32) + jnp.dot(context, w_axial_out, preferred_element_type=jnp.float32)).astype(jnp.bfloat16)
    normed_ff = normalize(after_axial).astype(jnp.bfloat16)
    pre_act = jnp.dot(normed_ff, w_in, preferred_element_type=jnp.float32)
    hidden = gelu_exact(pre_act).astype(jnp.bfloat16)
    cot_rows = cot_member.reshape(-1, D)
    grad_out_term = lax.dot_general(hidden, cot_rows, (((0,), (0,)), ((), ())), preferred_element_type=jnp.float32)
    hidden_grad = lax.dot_general(cot_rows, w_out, (((1,), (1,)), ((), ())), preferred_element_type=jnp.float32)
    pre_grad = (hidden_grad * gelu_slope(pre_act)).astype(jnp.bfloat16)
    grad_in_term = lax.dot_general(normed_ff, pre_grad, (((0,), (0,)), ((), ())), preferred_element_type=jnp.float32)
    return (grad_in_term, grad_out_term)

def reference(grid_tokens, cotangent, obs_pairs, obs_route, obs_patch, w_query, w_cross_out, w_qkv, w_axial_out, w_in, w_out):

    def one_member(inputs):
        return member_grads(inputs[0], inputs[1], inputs[2], inputs[3], inputs[4], w_query, w_cross_out, w_qkv, w_axial_out, w_in, w_out)
    grad_in_all, grad_out_all = lax.map(one_member, (grid_tokens, cotangent, obs_pairs, obs_route, obs_patch))
    return (lax.optimization_barrier(jnp.sum(grad_in_all, axis=0)), lax.optimization_barrier(jnp.sum(grad_out_all, axis=0)))
```

```python
import jax
import jax.numpy as jnp
from jax import lax
from jax.experimental import pallas as pl
from jax.experimental.pallas import tpu as pltpu
from jax.sharding import PartitionSpec as P

BF = jnp.bfloat16
F32 = jnp.float32
EPS = 1e-06
ROOT_HALF = 0.7071067811865476
INV_ROOT_TWO_PI = 0.3989422804014327
SCALE = 0.125


def normalize(values):
    values = values.astype(F32)
    return values * lax.rsqrt(jnp.mean(values * values, axis=-1, keepdims=True) + EPS)


def dot(a, b):
    return jnp.dot(a, b, preferred_element_type=F32)


def dot_t(a, b):
    return lax.dot_general(a, b, (((1,), (1,)), ((), ())), preferred_element_type=F32)


def mult(value, by):
    return pl.multiple_of(value, by)


def push(src, dst, send, recv, sp, dp):
    pltpu.make_async_remote_copy(
        src_ref=src,
        dst_ref=dst,
        send_sem=send,
        recv_sem=recv,
        device_id={"sp": sp, "dp": dp},
        device_id_type=pl.DeviceIdType.MESH,
    ).start()


def await_bytes(ref, sem):
    pltpu.make_async_copy(ref, ref, sem).wait()


def kernel(
    src_index,
    tokens,
    cot,
    pairs,
    slot_patch,
    wq_hbm,
    wc_hbm,
    wkv_hbm,
    wa_hbm,
    wi_hbm,
    wo_hbm,
    out_in,
    out_out,
    wq,
    wc,
    wkv,
    wa,
    wi,
    wo,
    obs_send,
    obs_recv,
    obs_wide,
    patch_recv,
    queries,
    context,
    after_cross,
    axial,
    lat_own,
    lat_sib,
    q_wide,
    k_wide,
    v_wide,
    ks_wide,
    vs_wide,
    o_wide,
    lat_out,
    lat_context,
    lon_context,
    normed_all,
    cot_all,
    hidden_t,
    pre_grad_t,
    gin_send,
    gout_send,
    gin_recv,
    gout_recv,
    fin_in_send,
    fin_in_recv,
    fin_out_send,
    fin_out_recv,
    local_sem,
    w_send,
    w_recv,
    f_send,
    f_recv,
    gather_send,
    gather_recv,
    share_send,
    share_recv,
    bulk_send,
    bulk_recv,
    last_send,
    last_in,
    last_out,
):
    sp = lax.axis_index("sp")
    y = lax.axis_index("dp")
    core = sp % 2
    sib = sp + 1 - 2 * core
    chip = sp // 2
    x = chip % 4
    z = chip // 4
    part = sp % 8

    pieces = (
        (wq_hbm, wq, 0, 1024),
        (wc_hbm, wc, 0, 1024),
        (wkv_hbm, wkv, 0, 1536),
        (wkv_hbm, wkv, 1536, 1536),
        (wa_hbm, wa, 0, 1024),
    )

    def start_piece(i):
        hbm, full, col, width = pieces[i]
        for k in range(1, 4):
            push(
                hbm.at[pl.ds(mult(core * 128, 128), 128), pl.ds(col, width)],
                full.at[pl.ds(mult(y * 256 + core * 128, 128), 128), pl.ds(col, width)],
                w_send.at[i],
                w_recv.at[i, k - 1],
                sp,
                (y + k) % 4,
            )

    def own_piece(i):
        hbm, full, col, width = pieces[i]
        return pltpu.make_async_copy(
            hbm.at[:, pl.ds(col, width)],
            full.at[pl.ds(mult(y * 256, 256), 256), pl.ds(col, width)],
            local_sem.at[i],
        )

    def forward_piece(i):
        hbm, full, col, width = pieces[i]
        for k in range(1, 4):
            rows = full.at[
                pl.ds(mult(((y - k + 4) % 4) * 256 + core * 128, 128), 128), pl.ds(col, width)
            ]
            await_bytes(rows, w_recv.at[i, k - 1])
            push(rows, rows, f_send.at[i], f_recv.at[i], sib, y)

    def finish_piece(i):
        hbm, full, col, width = pieces[i]
        await_bytes(full.at[pl.ds(0, 384), pl.ds(col, width)], f_recv.at[i])
        own_piece(i).wait()

    def drain_piece(i):
        hbm, full, col, width = pieces[i]
        await_bytes(full.at[pl.ds(0, 384), pl.ds(col, width)], w_send.at[i])
        await_bytes(full.at[pl.ds(0, 384), pl.ds(col, width)], f_send.at[i])

    start_piece(0)
    for i in range(5):
        own_piece(i).start()
    wi_copy = pltpu.make_async_copy(
        wi_hbm.at[:, pl.ds(mult(part * 256, 256), 256)], wi, local_sem.at[5]
    )
    wo_copy = pltpu.make_async_copy(
        wo_hbm.at[pl.ds(mult(part * 256, 256), 256), :], wo, local_sem.at[6]
    )
    wi_copy.start()
    wo_copy.start()

    def place(s, carry):
        obs_send[s] = pairs[src_index[s]]
        return carry

    lax.fori_loop(0, 192, place, 0, unroll=8)

    def send_obs(k, carry):
        to = (sp + k) % 64
        push(
            obs_send.at[pl.ds(to * 3, 3)],
            obs_recv.at[pl.ds(sp * 3, 3)],
            bulk_send.at[0],
            bulk_recv.at[0],
            to,
            y,
        )
        push(slot_patch.at[to], patch_recv.at[sp], bulk_send.at[1], bulk_recv.at[1], to, y)
        return carry

    lax.fori_loop(1, 64, send_obs, 0)
    obs_recv[pl.ds(sp * 3, 3)] = obs_send[pl.ds(sp * 3, 3)]
    patch_recv[sp] = slot_patch[sp]
    start_piece(1)

    def share_start(j, source, full):
        rows = full.at[pl.ds(mult(part * 128, 128), 128), :]
        push(source, rows, gather_send.at[j], gather_recv.at[j, 0], sib, y)
        for k in range(1, 4):
            push(
                source,
                rows,
                gather_send.at[j],
                gather_recv.at[j, k],
                z * 8 + ((x + k) % 4) * 2 + core,
                y,
            )

    def share_forward(j, full):
        for k in range(1, 4):
            rows = full.at[pl.ds(mult((((x - k + 4) % 4) * 2 + core) * 128, 128), 128), :]
            await_bytes(rows, gather_recv.at[j, k])
            push(rows, rows, share_send.at[j], share_recv.at[j], sib, y)

    def share_finish(j, full):
        await_bytes(full.at[pl.ds(0, 128), :], gather_recv.at[j, 0])
        await_bytes(full.at[pl.ds(0, 384), :], share_recv.at[j])

    def share_drain(j, full):
        await_bytes(full.at[pl.ds(0, 512), :], gather_send.at[j])
        await_bytes(full.at[pl.ds(0, 384), :], share_send.at[j])

    start_piece(2)
    share_start(0, cot, cot_all)
    cot_all[pl.ds(mult(part * 128, 128), 128), :] = cot[...]
    start_piece(3)
    start_piece(4)

    normed = normalize(tokens[...]).astype(BF)
    forward_piece(0)
    finish_piece(0)

    def columns(count, width, source, weight, target, offset):
        def step(n, carry):
            cols = pl.ds(mult(offset + n * width, width), width)
            target[:, cols] = dot(source, weight[:, cols]).astype(BF)
            return carry

        lax.fori_loop(0, count, step, 0)

    columns(4, 256, normed, wq, queries, 0)

    await_bytes(obs_recv.at[pl.ds(0, 189)], bulk_recv.at[0])
    await_bytes(patch_recv.at[pl.ds(0, 63)], bulk_recv.at[1])
    obs_wide[...] = obs_recv[...].astype(F32).reshape(3072, 128)
    patches = patch_recv[...].reshape(64, 128)
    slot_lane = lax.broadcasted_iota(jnp.int32, (64, 192), 1)
    slot_from = lax.broadcasted_iota(jnp.int32, (64, 192), 0) * 3
    slot_row = jnp.zeros((1, 192), F32)
    for r in range(3):
        slot_row += jnp.sum(
            jnp.where(slot_lane == slot_from + r, patches[:, r : r + 1], 0.0),
            axis=0,
            keepdims=True,
        )
    cell_patch = (lax.broadcasted_iota(jnp.int32, (128, 192), 0) // 32).astype(F32)
    same_patch = cell_patch == slot_row
    low = lax.broadcasted_iota(jnp.int32, (128, 128), 1) < 64
    zero = jnp.zeros((128, 128), BF)

    def cross_pair(g, carry):
        cols = pl.ds(mult(g * 128, 128), 128)
        keys = obs_wide[pl.ds(g, 192, stride=16), :].astype(BF)
        values = obs_wide[pl.ds(g + 8, 192, stride=16), :].astype(BF)
        both = queries[:, cols]
        found = []
        for half in (jnp.where(low, both, zero), jnp.where(low, zero, both)):
            masked = jnp.where(same_patch, dot_t(half, keys) * SCALE, -1e30)
            top = jnp.maximum(jnp.max(masked, axis=-1, keepdims=True), 0.0)
            terms = jnp.where(same_patch, jnp.exp(masked - top), 0.0)
            total = jnp.exp(-top) + jnp.sum(terms, axis=-1, keepdims=True)
            found.append(dot((terms / total).astype(BF), values))
        context[:, cols] = jnp.where(low, found[0], found[1]).astype(BF)
        return carry

    lax.fori_loop(0, 8, cross_pair, 0)

    forward_piece(1)
    finish_piece(1)

    def cross_out(n, carry):
        cols = pl.ds(mult(n * 256, 256), 256)
        after_cross[:, cols] = (
            tokens[:, cols].astype(F32) + dot(context[...], wc[:, cols])
        ).astype(BF)
        return carry

    lax.fori_loop(0, 4, cross_out, 0)
    normed_axial = normalize(after_cross[...]).astype(BF)
    forward_piece(2)
    finish_piece(2)
    columns(6, 256, normed_axial, wkv, axial, 0)

    cell_at, group_at = z, x

    def send_lat(k, carry):
        to = (chip + k) % 32
        push(
            axial.at[pl.ds(mult((to // 4) * 16, 16), 16), pl.ds(mult((to % 4) * 384, 128), 384)],
            lat_own.at[chip],
            bulk_send.at[2],
            bulk_recv.at[2],
            to * 2 + core,
            y,
        )
        return carry

    lax.fori_loop(1, 32, send_lat, 0)
    lat_own[chip] = axial[pl.ds(mult(cell_at * 16, 16), 16), pl.ds(mult(group_at * 384, 128), 384)]

    share_forward(0, cot_all)

    forward_piece(3)
    finish_piece(3)
    columns(6, 256, normed_axial, wkv, axial, 1536)

    def lon_pair(p, carry):
        both = axial[:, pl.ds(mult(1536 + p * 128, 128), 128)]
        keys = axial[:, pl.ds(mult(2048 + p * 128, 128), 128)]
        values = axial[:, pl.ds(mult(2560 + p * 128, 128), 128)]
        found = []
        for half in (jnp.where(low, both, zero), jnp.where(low, zero, both)):
            scores = dot_t(half, keys) * SCALE
            terms = jnp.exp(scores - jnp.max(scores, axis=-1, keepdims=True))
            weights = (terms / jnp.sum(terms, axis=-1, keepdims=True)).astype(BF)
            found.append(dot(weights, values))
        lon_context[:, pl.ds(mult(p * 128, 128), 128)] = jnp.where(low, found[0], found[1]).astype(
            BF
        )
        return carry

    lat_kv = lat_own.at[:, :, pl.ds(128, 256)]
    await_bytes(lat_own.at[pl.ds(0, 31)], bulk_recv.at[2])
    push(lat_kv, lat_sib, bulk_send.at[3], bulk_recv.at[3], sib, y)
    lax.fori_loop(0, 4, lon_pair, 0)
    q_wide[...] = lat_own[:, :, 0:128].astype(F32).reshape(512, 128)
    k_wide[...] = lat_own[:, :, 128:256].astype(F32).reshape(512, 128)
    v_wide[...] = lat_own[:, :, 256:384].astype(F32).reshape(512, 128)
    await_bytes(lat_sib, bulk_recv.at[3])
    ks_wide[...] = lat_sib[:, :, 0:128].astype(F32).reshape(512, 128)
    vs_wide[...] = lat_sib[:, :, 128:256].astype(F32).reshape(512, 128)
    low_rows = lax.broadcasted_iota(jnp.int32, (32, 128), 1) < 64

    def lat_cell(l, carry):
        rows = pl.ds(l, 32, stride=16)
        q = q_wide[rows, :]
        both = jnp.concatenate(
            [jnp.where(low_rows, q, 0.0), jnp.where(low_rows, 0.0, q)], axis=0
        ).astype(BF)
        keys = jnp.concatenate([k_wide[rows, :], ks_wide[rows, :]], axis=0).astype(BF)
        values = jnp.concatenate([v_wide[rows, :], vs_wide[rows, :]], axis=0).astype(BF)
        scores = dot_t(both, keys) * SCALE
        terms = jnp.exp(scores - jnp.max(scores, axis=-1, keepdims=True))
        weights = (terms / jnp.sum(terms, axis=-1, keepdims=True)).astype(BF)
        found = dot(weights, values)
        o_wide[rows, :] = jnp.where(low_rows, found[:32], found[32:])
        return carry

    lax.fori_loop(0, 16, lat_cell, 0, unroll=4)
    lat_out[...] = o_wide[...].reshape(32, 16, 128).astype(BF)
    home = (pl.ds(mult(cell_at * 16, 16), 16), pl.ds(mult(group_at * 128, 128), 128))

    def send_back(k, carry):
        to = (chip + k) % 32
        push(
            lat_out.at[to],
            lat_context.at[home],
            bulk_send.at[4],
            bulk_recv.at[4],
            to * 2 + core,
            y,
        )
        return carry

    lax.fori_loop(1, 32, send_back, 0)
    lat_context[home] = lat_out[chip]
    forward_piece(4)
    finish_piece(4)
    await_bytes(lat_out.at[pl.ds(0, 31)], bulk_recv.at[4])

    mine = pl.ds(mult(part * 128, 128), 128)

    def axial_out(n, carry):
        cols = pl.ds(mult(n * 256, 256), 256)
        context[:, cols] = (
            after_cross[:, cols].astype(F32)
            + dot(lat_context[...], wa[pl.ds(0, 512), cols])
            + dot(lon_context[...], wa[pl.ds(512, 512), cols])
        ).astype(BF)
        return carry

    lax.fori_loop(0, 4, axial_out, 0)
    normed_all[mine, :] = normalize(context[...]).astype(BF)
    share_start(1, normed_all.at[mine, :], normed_all)
    share_finish(0, cot_all)
    wi_copy.wait()
    wo_copy.wait()
    share_forward(1, normed_all)
    share_finish(1, normed_all)

    def ff_rows(n, carry):
        rows = pl.ds(mult(n * 256, 256), 256)
        pre_act = dot(normed_all[rows, :], wi[...])
        hidden_grad = dot_t(cot_all[rows, :], wo[...])
        cdf = 0.5 * (1.0 + lax.erf(pre_act * ROOT_HALF))
        slope = cdf + pre_act * jnp.exp(-0.5 * pre_act * pre_act) * INV_ROOT_TWO_PI
        hidden_t[:, rows] = (pre_act * cdf).astype(BF).T
        pre_grad_t[:, rows] = (hidden_grad * slope).astype(BF).T
        return carry

    lax.fori_loop(0, 4, ff_rows, 0)

    def grad_cols(n, carry):
        cols = pl.ds(mult(n * 256, 256), 256)
        gout_send[:, cols] = dot(hidden_t[...], cot_all[:, cols]).astype(BF)
        gin_send[cols, :] = dot(pre_grad_t[...], normed_all[:, cols]).astype(BF).T
        return carry

    lax.fori_loop(0, 4, grad_cols, 0)

    place_at = z * 4 + y

    def blocks(to):
        return (
            (pl.ds(mult(to * 32, 32), 32), slice(None)),
            (pl.ds(mult((to // 2) * 16, 16), 16), pl.ds(mult((to % 2) * 512, 512), 512)),
        )

    def send_grads(k, carry):
        to = (place_at + k) % 32
        at_in, at_out = blocks(to)
        to_sp, to_dp = (to // 4) * 8 + part, to % 4
        push(
            gin_send.at[at_in],
            gin_recv.at[place_at],
            bulk_send.at[5],
            bulk_recv.at[5],
            to_sp,
            to_dp,
        )
        push(
            gout_send.at[at_out],
            gout_recv.at[place_at],
            bulk_send.at[6],
            bulk_recv.at[6],
            to_sp,
            to_dp,
        )
        return carry

    lax.fori_loop(1, 32, send_grads, 0)
    at_in, at_out = blocks(place_at)
    gin_recv[place_at] = gin_send[at_in]
    gout_recv[place_at] = gout_send[at_out]
    await_bytes(gin_recv.at[pl.ds(0, 31)], bulk_recv.at[5])
    await_bytes(gout_recv.at[pl.ds(0, 31)], bulk_recv.at[6])

    def add_in(n, total):
        return total + gin_recv[n].astype(F32)

    def add_out(n, total):
        return total + gout_recv[n].astype(F32)

    sum_in = lax.fori_loop(0, 32, add_in, jnp.zeros((32, 256), F32), unroll=4)
    sum_out = lax.fori_loop(0, 32, add_out, jnp.zeros((16, 512), F32), unroll=4)
    for n in range(8):
        fin_in_send[n] = sum_in[n * 4 : n * 4 + 4]
    for n in range(2):
        fin_out_send[n] = sum_out[n * 8 : n * 8 + 8]

    for n in range(8):
        to_sp, to_dp = z * 8 + y * 2 + n // 4, n % 4
        here = (to_sp == sp) & (to_dp == y)

        @pl.when(here)
        def _():
            fin_in_recv[part] = fin_in_send[n]

        @pl.when(jnp.logical_not(here))
        def _():
            push(
                fin_in_send.at[n],
                fin_in_recv.at[part],
                last_send.at[n],
                last_in.at[part],
                to_sp,
                to_dp,
            )

    for n in range(2):
        to_sp, to_dp = part * 8 + z, (y // 2) * 2 + n
        here = (to_sp == sp) & (to_dp == y)

        @pl.when(here)
        def _():
            fin_out_recv[y % 2] = fin_out_send[n]

        @pl.when(jnp.logical_not(here))
        def _():
            push(
                fin_out_send.at[n],
                fin_out_recv.at[y % 2],
                last_send.at[8 + n],
                last_out.at[y % 2],
                to_sp,
                to_dp,
            )

    for n in range(8):
        from_sp, from_dp = z * 8 + n, part // 2

        @pl.when(jnp.logical_not((from_sp == sp) & (from_dp == y)))
        def _():
            await_bytes(fin_in_recv.at[n], last_in.at[n])

        out_in[:, n * 256 : (n + 1) * 256] = fin_in_recv[n]
    for n in range(2):
        from_sp, from_dp = part * 8 + z, (y // 2) * 2 + n

        @pl.when(jnp.logical_not((from_sp == sp) & (from_dp == y)))
        def _():
            await_bytes(fin_out_recv.at[n], last_out.at[n])

        out_out[:, n * 512 : (n + 1) * 512] = fin_out_recv[n]

    for i in range(5):
        drain_piece(i)
    share_drain(0, cot_all)
    share_drain(1, normed_all)
    await_bytes(obs_recv.at[pl.ds(0, 189)], bulk_send.at[0])
    await_bytes(patch_recv.at[pl.ds(0, 63)], bulk_send.at[1])
    await_bytes(lat_own.at[pl.ds(0, 31)], bulk_send.at[2])
    await_bytes(lat_sib, bulk_send.at[3])
    await_bytes(lat_out.at[pl.ds(0, 31)], bulk_send.at[4])
    await_bytes(gin_recv.at[pl.ds(0, 31)], bulk_send.at[5])
    await_bytes(gout_recv.at[pl.ds(0, 31)], bulk_send.at[6])
    for n in range(8):
        to_sp, to_dp = z * 8 + y * 2 + n // 4, n % 4

        @pl.when(jnp.logical_not((to_sp == sp) & (to_dp == y)))
        def _():
            await_bytes(fin_in_send.at[n], last_send.at[n])

    for n in range(2):
        to_sp, to_dp = part * 8 + z, (y // 2) * 2 + n

        @pl.when(jnp.logical_not((to_sp == sp) & (to_dp == y)))
        def _():
            await_bytes(fin_out_send.at[n], last_send.at[8 + n])


def scratch():
    vmem = pltpu.VMEM
    dma = pltpu.SemaphoreType.DMA
    return [
        vmem((1024, 1024), BF),
        vmem((1024, 1024), BF),
        vmem((1024, 3072), BF),
        vmem((1024, 1024), BF),
        vmem((1024, 256), BF),
        vmem((256, 1024), BF),
        vmem((192, 16, 128), BF),
        vmem((192, 16, 128), BF),
        vmem((3072, 128), F32),
        vmem((64, 1, 128), F32),
        vmem((128, 1024), BF),
        vmem((128, 1024), BF),
        vmem((128, 1024), BF),
        vmem((128, 3072), BF),
        vmem((32, 16, 384), BF),
        vmem((32, 16, 256), BF),
        vmem((512, 128), F32),
        vmem((512, 128), F32),
        vmem((512, 128), F32),
        vmem((512, 128), F32),
        vmem((512, 128), F32),
        vmem((512, 128), F32),
        vmem((32, 16, 128), BF),
        vmem((128, 512), BF),
        vmem((128, 512), BF),
        vmem((1024, 1024), BF),
        vmem((1024, 1024), BF),
        vmem((256, 1024), BF),
        vmem((256, 1024), BF),
        vmem((1024, 256), BF),
        vmem((256, 1024), BF),
        vmem((32, 32, 256), BF),
        vmem((32, 16, 512), BF),
        vmem((8, 4, 256), F32),
        vmem((8, 4, 256), F32),
        vmem((2, 8, 512), F32),
        vmem((2, 8, 512), F32),
        dma((7,)),
        dma((5,)),
        dma((5, 3)),
        dma((5,)),
        dma((5,)),
        dma((2,)),
        dma((2, 4)),
        dma((2,)),
        dma((2,)),
        dma((7,)),
        dma((7,)),
        dma((10,)),
        dma((8,)),
        dma((2,)),
    ]


def local(
    grid_tokens,
    cotangent,
    obs_pairs,
    obs_route,
    obs_patch,
    w_query,
    w_cross_out,
    w_qkv,
    w_axial_out,
    w_in,
    w_out,
):
    row = obs_route.reshape(96)
    order = jnp.arange(96, dtype=jnp.int32)
    earlier = (row[:, None] == row[None, :]) & (order[None, :] < order[:, None])
    slot = row * 3 + jnp.sum(earlier.astype(jnp.int32), axis=1)
    hit = slot[None, :] == jnp.arange(192, dtype=jnp.int32)[:, None]
    src_index = jnp.sum(jnp.where(hit, order[None, :], 0), axis=1)
    patch = jnp.sum(jnp.where(hit, obs_patch.reshape(1, 96) + 1, 0), axis=1) - 1
    slot_patch = jnp.pad(patch.astype(F32).reshape(64, 1, 3), ((0, 0), (0, 0), (0, 125)))
    vmem = pl.BlockSpec(memory_space=pltpu.VMEM)
    hbm = pl.BlockSpec(memory_space=pl.ANY)
    return pl.pallas_call(
        kernel,
        out_shape=(
            jax.ShapeDtypeStruct((4, 2048), F32),
            jax.ShapeDtypeStruct((8, 1024), F32),
        ),
        in_specs=[pl.BlockSpec(memory_space=pltpu.SMEM)] + [vmem] * 4 + [hbm] * 6,
        out_specs=(vmem, vmem),
        scratch_shapes=scratch(),
        compiler_params=pltpu.CompilerParams(
            has_side_effects=True, vmem_limit_bytes=50 * 1024 * 1024
        ),
    )(
        src_index,
        grid_tokens.reshape(128, 1024),
        cotangent.reshape(128, 1024),
        obs_pairs.reshape(96, 16, 128),
        slot_patch,
        w_query,
        w_cross_out,
        w_qkv,
        w_axial_out,
        w_in,
        w_out,
    )


def solution(mesh):
    return jax.shard_map(
        local,
        mesh=mesh,
        in_specs=(
            P("dp", "sp", None, None),
            P("dp", "sp", None, None),
            P("dp", "sp", None, None),
            P("dp", "sp", None, None),
            P("dp", "sp", None),
            P("dp", None),
            P("dp", None),
            P("dp", None),
            P("dp", None),
            P(),
            P(),
        ),
        out_specs=(P(("sp", "dp"), None), P(("sp", "dp"), None)),
        check_vma=False,
    )
```

```python
import jax
import jax.numpy as jnp
from jax import lax
from jax.experimental import pallas as pl
from jax.experimental.pallas import tpu as pltpu
from jax.sharding import PartitionSpec as P

BF = jnp.bfloat16
F32 = jnp.float32
EPS = 1e-06
ROOT_HALF = 0.7071067811865476
INV_ROOT_TWO_PI = 0.3989422804014327
SCALE = 0.125


def normalize(values):
    values = values.astype(F32)
    return values * lax.rsqrt(jnp.mean(values * values, axis=-1, keepdims=True) + EPS)


def dot(a, b):
    return jnp.dot(a, b, preferred_element_type=F32)


def dot_t(a, b):
    return lax.dot_general(a, b, (((1,), (1,)), ((), ())), preferred_element_type=F32)


def mult(value, by):
    return pl.multiple_of(value, by)


def push(src, dst, send, recv, sp, dp):
    pltpu.make_async_remote_copy(
        src_ref=src,
        dst_ref=dst,
        send_sem=send,
        recv_sem=recv,
        device_id={"sp": sp, "dp": dp},
        device_id_type=pl.DeviceIdType.MESH,
    ).start()


def await_bytes(ref, sem):
    pltpu.make_async_copy(ref, ref, sem).wait()


def kernel(
    tokens_hbm,
    cot_hbm,
    pairs_hbm,
    route_hbm,
    patch_hbm,
    wq_hbm,
    wc_hbm,
    wkv_hbm,
    wa_hbm,
    wi_hbm,
    wo_hbm,
    out_in,
    out_out,
    tokens,
    cot,
    pairs,
    route,
    patch,
    pairs_wide,
    pairs_tiles,
    index_row,
    src_index,
    slot_patch,
    wq,
    wc,
    wkv,
    wa,
    wi,
    wo,
    obs_send,
    obs_recv,
    obs_wide,
    patch_recv,
    queries,
    context,
    after_cross,
    axial,
    lat_own,
    lat_sib,
    q_wide,
    k_wide,
    v_wide,
    ks_wide,
    vs_wide,
    o_wide,
    lat_out,
    lat_context,
    lon_context,
    normed_all,
    cot_all,
    hidden_t,
    pre_grad_t,
    gin_send,
    gout_send,
    gin_recv,
    gout_recv,
    fin_in_send,
    fin_in_recv,
    fin_out_send,
    fin_out_recv,
    local_sem,
    w_send,
    w_recv,
    gather_send,
    gather_recv,
    share_send,
    share_recv,
    bulk_send,
    bulk_recv,
    last_send,
    last_in,
    last_out,
):
    sp = lax.axis_index("sp")
    y = lax.axis_index("dp")
    core = sp % 2
    sib = sp + 1 - 2 * core
    chip = sp // 2
    x = chip % 4
    z = chip // 4
    part = sp % 8

    barrier = pltpu.get_barrier_semaphore()

    def greet(to_sp, to_dp):
        pl.semaphore_signal(
            barrier,
            inc=1,
            device_id={"sp": to_sp, "dp": to_dp},
            device_id_type=pl.DeviceIdType.MESH,
        )

    def greet_row(k, carry):
        greet((sp + k) % 64, y)
        return carry

    def greet_member(k, carry):
        for other in range(1, 4):
            greet(k * 8 + part, (y + other) % 4)
        return carry

    lax.fori_loop(1, 64, greet_row, 0)
    lax.fori_loop(0, 8, greet_member, 0)
    greet(part * 8 + z, y + 1 - 2 * (y % 2))

    loads = [
        pltpu.make_async_copy(source, target, local_sem.at[7 + i])
        for i, (source, target) in enumerate(
            (
                (route_hbm, route),
                (patch_hbm, patch),
                (pairs_hbm, pairs),
                (tokens_hbm, tokens),
                (cot_hbm, cot),
            )
        )
    ]
    for load in loads:
        load.start()

    pieces = (
        (wq_hbm, wq, 0, 1024),
        (wc_hbm, wc, 0, 1024),
        (wkv_hbm, wkv, 0, 1536),
        (wkv_hbm, wkv, 1536, 1536),
        (wa_hbm, wa, 0, 1024),
    )
    pos_x = (x + core) % 2
    pos_z = (z + core) % 2
    mate_x = z * 8 + ((x + 5 - 2 * pos_x) % 4) * 2 + core
    mate_z = ((z + 9 - 2 * pos_z) % 8) * 8 + x * 2 + core
    quarter = core * 128 + pos_x * 64 + pos_z * 32
    spans = (
        (quarter, 32, None),
        (quarter, 32, mate_z),
        (core * 128 + pos_x * 64, 64, mate_x),
        (core * 128, 128, sib),
    )

    def start_piece(i):
        hbm, full, col, width = pieces[i]
        for k in range(1, 4):
            push(
                hbm.at[pl.ds(mult(quarter, 32), 32), pl.ds(col, width)],
                full.at[pl.ds(mult(y * 256 + quarter, 32), 32), pl.ds(col, width)],
                w_send.at[i, 0],
                w_recv.at[i, 0],
                sp,
                (y + k) % 4,
            )

    def own_piece(i):
        hbm, full, col, width = pieces[i]
        return pltpu.make_async_copy(
            hbm.at[:, pl.ds(col, width)],
            full.at[pl.ds(mult(y * 256, 256), 256), pl.ds(col, width)],
            local_sem.at[i],
        )

    def arrive(i, stage):
        hbm, full, col, width = pieces[i]
        rows = (96, 96, 192, 384)[stage]
        await_bytes(full.at[pl.ds(0, rows), pl.ds(col, width)], w_recv.at[i, stage])

    def advance(i, stage):
        hbm, full, col, width = pieces[i]
        arrive(i, stage - 1)
        first, count, mate = spans[stage]
        for k in range(1, 4):
            rows = full.at[
                pl.ds(mult(((y + k) % 4) * 256 + first, 32), count), pl.ds(col, width)
            ]
            push(rows, rows, w_send.at[i, stage], w_recv.at[i, stage], mate, y)

    def finish_piece(i):
        arrive(i, 3)
        own_piece(i).wait()

    def drain_piece(i):
        hbm, full, col, width = pieces[i]
        for stage in range(4):
            rows = (96, 96, 192, 384)[stage]
            await_bytes(full.at[pl.ds(0, rows), pl.ds(col, width)], w_send.at[i, stage])

    for i in range(5):
        own_piece(i).start()
    wi_copy = pltpu.make_async_copy(
        wi_hbm.at[:, pl.ds(mult(part * 256, 256), 256)], wi, local_sem.at[5]
    )
    wo_copy = pltpu.make_async_copy(
        wo_hbm.at[pl.ds(mult(part * 256, 256), 256), :], wo, local_sem.at[6]
    )
    wi_copy.start()
    wo_copy.start()

    loads[0].wait()
    loads[1].wait()
    line = lax.broadcasted_iota(jnp.int32, (96, 96), 0)
    lane = lax.broadcasted_iota(jnp.int32, (96, 96), 1)

    def upright(row):
        return jnp.sum(jnp.where(line == lane, row, 0), axis=1, keepdims=True)

    row_across = route[...]
    row_down = upright(row_across)
    patch_across = patch[...] + 1
    same = row_across == row_down
    rank_across = jnp.sum(jnp.where(same & (line < lane), 1, 0), axis=0, keepdims=True)
    rank_down = jnp.sum(jnp.where(same & (lane < line), 1, 0), axis=1, keepdims=True)
    slot_across = row_across * 3 + rank_across
    slot_down = row_down * 3 + rank_down
    hit = slot_down == lax.broadcasted_iota(jnp.int32, (96, 256), 1)
    index_row[...] = jnp.sum(
        jnp.where(hit, lax.broadcasted_iota(jnp.int32, (96, 256), 0), 0), axis=0, keepdims=True
    )
    index_copy = pltpu.make_async_copy(index_row, src_index, local_sem.at[12])
    index_copy.start()
    lanes = lax.broadcasted_iota(jnp.int32, (64, 128), 1)
    found_patch = jnp.zeros((64, 128), jnp.int32)
    for r in range(3):
        mine = slot_across == lax.broadcasted_iota(jnp.int32, (64, 96), 0) * 3 + r
        value = jnp.sum(jnp.where(mine, patch_across, 0), axis=1, keepdims=True) - 1
        found_patch = jnp.where(lanes == r, value, found_patch)
    slot_patch[...] = found_patch.astype(F32).reshape(64, 1, 128)

    loads[2].wait()
    for n in range(16):
        pairs_wide[pl.ds(n, 96, stride=16), :] = pairs[:, n * 128 : (n + 1) * 128].astype(F32)
    pairs_tiles[...] = pairs_wide[...].reshape(96, 16, 128).astype(BF)
    index_copy.wait()

    def place(s, carry):
        obs_send[s] = pairs_tiles[src_index[0, s]]
        return carry

    lax.fori_loop(0, 192, place, 0, unroll=8)
    pl.semaphore_wait(barrier, 88)
    start_piece(0)

    def send_obs(k, carry):
        to = (sp + k) % 64
        push(
            obs_send.at[pl.ds(to * 3, 3)],
            obs_recv.at[pl.ds(sp * 3, 3)],
            bulk_send.at[0],
            bulk_recv.at[0],
            to,
            y,
        )
        push(slot_patch.at[to], patch_recv.at[sp], bulk_send.at[1], bulk_recv.at[1], to, y)
        return carry

    lax.fori_loop(1, 64, send_obs, 0)
    for i in range(1, 5):
        start_piece(i)
    obs_recv[pl.ds(sp * 3, 3)] = obs_send[pl.ds(sp * 3, 3)]
    patch_recv[sp] = slot_patch[sp]

    def share_start(j, source, full):
        rows = full.at[pl.ds(mult(part * 128, 128), 128), :]
        push(source, rows, gather_send.at[j], gather_recv.at[j, 0], sib, y)
        for k in range(1, 4):
            push(
                source,
                rows,
                gather_send.at[j],
                gather_recv.at[j, k],
                z * 8 + ((x + k) % 4) * 2 + core,
                y,
            )

    def share_forward(j, full):
        for k in range(1, 4):
            rows = full.at[pl.ds(mult((((x - k + 4) % 4) * 2 + core) * 128, 128), 128), :]
            await_bytes(rows, gather_recv.at[j, k])
            push(rows, rows, share_send.at[j], share_recv.at[j], sib, y)

    def share_finish(j, full):
        await_bytes(full.at[pl.ds(0, 128), :], gather_recv.at[j, 0])
        await_bytes(full.at[pl.ds(0, 384), :], share_recv.at[j])

    def share_drain(j, full):
        await_bytes(full.at[pl.ds(0, 512), :], gather_send.at[j])
        await_bytes(full.at[pl.ds(0, 384), :], share_send.at[j])

    loads[3].wait()
    loads[4].wait()
    cot_all[pl.ds(mult(part * 128, 128), 128), :] = cot[...]

    normed = normalize(tokens[...]).astype(BF)
    advance(0, 1)
    advance(0, 2)
    advance(1, 1)
    advance(0, 3)
    advance(1, 2)
    advance(2, 1)
    finish_piece(0)

    def columns(count, width, source, weight, target, offset):
        def step(n, carry):
            cols = pl.ds(mult(offset + n * width, width), width)
            target[:, cols] = dot(source, weight[:, cols]).astype(BF)
            return carry

        lax.fori_loop(0, count, step, 0)

    columns(4, 256, normed, wq, queries, 0)
    advance(1, 3)
    advance(2, 2)
    advance(3, 1)

    await_bytes(obs_recv.at[pl.ds(0, 189)], bulk_recv.at[0])
    await_bytes(patch_recv.at[pl.ds(0, 63)], bulk_recv.at[1])
    advance(2, 3)
    advance(3, 2)
    advance(4, 1)
    share_start(0, cot, cot_all)
    obs_wide[...] = obs_recv[...].astype(F32).reshape(3072, 128)
    patches = patch_recv[...].reshape(64, 128)
    slot_lane = lax.broadcasted_iota(jnp.int32, (64, 192), 1)
    slot_from = lax.broadcasted_iota(jnp.int32, (64, 192), 0) * 3
    slot_row = jnp.zeros((1, 192), F32)
    for r in range(3):
        slot_row += jnp.sum(
            jnp.where(slot_lane == slot_from + r, patches[:, r : r + 1], 0.0),
            axis=0,
            keepdims=True,
        )
    cell_patch = (lax.broadcasted_iota(jnp.int32, (128, 192), 0) // 32).astype(F32)
    same_patch = cell_patch == slot_row
    low = lax.broadcasted_iota(jnp.int32, (128, 128), 1) < 64
    zero = jnp.zeros((128, 128), BF)

    def cross_pair(g, carry):
        cols = pl.ds(mult(g * 128, 128), 128)
        keys = obs_wide[pl.ds(g, 192, stride=16), :].astype(BF)
        values = obs_wide[pl.ds(g + 8, 192, stride=16), :].astype(BF)
        both = queries[:, cols]
        found = []
        for half in (jnp.where(low, both, zero), jnp.where(low, zero, both)):
            masked = jnp.where(same_patch, dot_t(half, keys) * SCALE, -1e30)
            top = jnp.maximum(jnp.max(masked, axis=-1, keepdims=True), 0.0)
            terms = jnp.where(same_patch, jnp.exp(masked - top), 0.0)
            total = jnp.exp(-top) + jnp.sum(terms, axis=-1, keepdims=True)
            found.append(dot((terms / total).astype(BF), values))
        context[:, cols] = jnp.where(low, found[0], found[1]).astype(BF)
        return carry

    lax.fori_loop(0, 8, cross_pair, 0)

    advance(3, 3)
    advance(4, 2)
    finish_piece(1)

    def cross_out(n, carry):
        cols = pl.ds(mult(n * 256, 256), 256)
        after_cross[:, cols] = (
            tokens[:, cols].astype(F32) + dot(context[...], wc[:, cols])
        ).astype(BF)
        return carry

    lax.fori_loop(0, 4, cross_out, 0)
    normed_axial = normalize(after_cross[...]).astype(BF)
    finish_piece(2)
    columns(6, 256, normed_axial, wkv, axial, 0)

    cell_at, group_at = z, x

    def send_lat(k, carry):
        to = (chip + k) % 32
        push(
            axial.at[pl.ds(mult((to // 4) * 16, 16), 16), pl.ds(mult((to % 4) * 384, 128), 384)],
            lat_own.at[chip],
            bulk_send.at[2],
            bulk_recv.at[2],
            to * 2 + core,
            y,
        )
        return carry

    lax.fori_loop(1, 32, send_lat, 0)
    lat_own[chip] = axial[pl.ds(mult(cell_at * 16, 16), 16), pl.ds(mult(group_at * 384, 128), 384)]

    share_forward(0, cot_all)

    advance(4, 3)
    finish_piece(3)
    columns(6, 256, normed_axial, wkv, axial, 1536)

    def lon_pair(p, carry):
        both = axial[:, pl.ds(mult(1536 + p * 128, 128), 128)]
        keys = axial[:, pl.ds(mult(2048 + p * 128, 128), 128)]
        values = axial[:, pl.ds(mult(2560 + p * 128, 128), 128)]
        found = []
        for half in (jnp.where(low, both, zero), jnp.where(low, zero, both)):
            scores = dot_t(half, keys) * SCALE
            terms = jnp.exp(scores - jnp.max(scores, axis=-1, keepdims=True))
            weights = (terms / jnp.sum(terms, axis=-1, keepdims=True)).astype(BF)
            found.append(dot(weights, values))
        lon_context[:, pl.ds(mult(p * 128, 128), 128)] = jnp.where(low, found[0], found[1]).astype(
            BF
        )
        return carry

    lat_kv = lat_own.at[:, :, pl.ds(128, 256)]
    await_bytes(lat_own.at[pl.ds(0, 31)], bulk_recv.at[2])
    push(lat_kv, lat_sib, bulk_send.at[3], bulk_recv.at[3], sib, y)
    lax.fori_loop(0, 4, lon_pair, 0)
    q_wide[...] = lat_own[:, :, 0:128].astype(F32).reshape(512, 128)
    k_wide[...] = lat_own[:, :, 128:256].astype(F32).reshape(512, 128)
    v_wide[...] = lat_own[:, :, 256:384].astype(F32).reshape(512, 128)
    await_bytes(lat_sib, bulk_recv.at[3])
    ks_wide[...] = lat_sib[:, :, 0:128].astype(F32).reshape(512, 128)
    vs_wide[...] = lat_sib[:, :, 128:256].astype(F32).reshape(512, 128)
    low_rows = lax.broadcasted_iota(jnp.int32, (32, 128), 1) < 64

    def lat_cell(l, carry):
        rows = pl.ds(l, 32, stride=16)
        q = q_wide[rows, :]
        both = jnp.concatenate(
            [jnp.where(low_rows, q, 0.0), jnp.where(low_rows, 0.0, q)], axis=0
        ).astype(BF)
        keys = jnp.concatenate([k_wide[rows, :], ks_wide[rows, :]], axis=0).astype(BF)
        values = jnp.concatenate([v_wide[rows, :], vs_wide[rows, :]], axis=0).astype(BF)
        scores = dot_t(both, keys) * SCALE
        terms = jnp.exp(scores - jnp.max(scores, axis=-1, keepdims=True))
        weights = (terms / jnp.sum(terms, axis=-1, keepdims=True)).astype(BF)
        found = dot(weights, values)
        o_wide[rows, :] = jnp.where(low_rows, found[:32], found[32:])
        return carry

    lax.fori_loop(0, 16, lat_cell, 0, unroll=4)
    lat_out[...] = o_wide[...].reshape(32, 16, 128).astype(BF)
    home = (pl.ds(mult(cell_at * 16, 16), 16), pl.ds(mult(group_at * 128, 128), 128))

    def send_back(k, carry):
        to = (chip + k) % 32
        push(
            lat_out.at[to],
            lat_context.at[home],
            bulk_send.at[4],
            bulk_recv.at[4],
            to * 2 + core,
            y,
        )
        return carry

    lax.fori_loop(1, 32, send_back, 0)
    lat_context[home] = lat_out[chip]
    finish_piece(4)
    await_bytes(lat_out.at[pl.ds(0, 31)], bulk_recv.at[4])

    mine = pl.ds(mult(part * 128, 128), 128)

    def axial_out(n, carry):
        cols = pl.ds(mult(n * 256, 256), 256)
        context[:, cols] = (
            after_cross[:, cols].astype(F32)
            + dot(lat_context[...], wa[pl.ds(0, 512), cols])
            + dot(lon_context[...], wa[pl.ds(512, 512), cols])
        ).astype(BF)
        return carry

    lax.fori_loop(0, 4, axial_out, 0)
    normed_all[mine, :] = normalize(context[...]).astype(BF)
    share_start(1, normed_all.at[mine, :], normed_all)
    share_finish(0, cot_all)
    wi_copy.wait()
    wo_copy.wait()
    share_forward(1, normed_all)
    share_finish(1, normed_all)

    def ff_rows(n, carry):
        rows = pl.ds(mult(n * 256, 256), 256)
        pre_act = dot(normed_all[rows, :], wi[...])
        hidden_grad = dot_t(cot_all[rows, :], wo[...])
        cdf = 0.5 * (1.0 + lax.erf(pre_act * ROOT_HALF))
        slope = cdf + pre_act * jnp.exp(-0.5 * pre_act * pre_act) * INV_ROOT_TWO_PI
        hidden_t[:, rows] = (pre_act * cdf).astype(BF).T
        pre_grad_t[:, rows] = (hidden_grad * slope).astype(BF).T
        return carry

    lax.fori_loop(0, 4, ff_rows, 0)

    down = lax.broadcasted_iota(jnp.int32, (128, 128), 0)
    across = lax.broadcasted_iota(jnp.int32, (128, 128), 1)
    turn = (across == ((down % 32) // 4) * 16 + (down // 32) * 4 + down % 4).astype(F32).astype(BF)

    def grad_cols(n, carry):
        cols = pl.ds(mult(n * 256, 256), 256)
        gout_send[:, cols] = dot(hidden_t[...], cot_all[:, cols]).astype(BF)
        grad = dot(pre_grad_t[...], normed_all[:, cols]).astype(BF)
        for half in range(2):
            gin_send[pl.ds(mult(n * 256 + half * 128, 128), 128), :] = dot_t(
                turn, grad[:, half * 128 : half * 128 + 128]
            ).astype(BF)
        return carry

    lax.fori_loop(0, 4, grad_cols, 0)

    place_at = z * 4 + y

    def blocks(to):
        return (
            (pl.ds(mult(to * 32, 32), 32), slice(None)),
            (pl.ds(mult((to // 2) * 16, 16), 16), pl.ds(mult((to % 2) * 512, 512), 512)),
        )

    def send_grads(k, carry):
        to = (place_at + k) % 32
        at_in, at_out = blocks(to)
        to_sp, to_dp = (to // 4) * 8 + part, to % 4
        push(
            gin_send.at[at_in],
            gin_recv.at[place_at],
            bulk_send.at[5],
            bulk_recv.at[5],
            to_sp,
            to_dp,
        )
        push(
            gout_send.at[at_out],
            gout_recv.at[place_at],
            bulk_send.at[6],
            bulk_recv.at[6],
            to_sp,
            to_dp,
        )
        return carry

    lax.fori_loop(1, 32, send_grads, 0)
    at_in, at_out = blocks(place_at)
    gin_recv[place_at] = gin_send[at_in]
    gout_recv[place_at] = gout_send[at_out]
    await_bytes(gin_recv.at[pl.ds(0, 31)], bulk_recv.at[5])
    await_bytes(gout_recv.at[pl.ds(0, 31)], bulk_recv.at[6])

    def add_in(n, total):
        return total + gin_recv[n].astype(F32)

    def add_out(n, total):
        return total + gout_recv[n].astype(F32)

    sum_in = lax.fori_loop(0, 32, add_in, jnp.zeros((32, 256), F32), unroll=4)
    sum_out = lax.fori_loop(0, 32, add_out, jnp.zeros((16, 512), F32), unroll=4)
    for n in range(8):
        fin_in_send[n] = sum_in[n * 4 : n * 4 + 4]
    for n in range(2):
        fin_out_send[n] = sum_out[n * 8 : n * 8 + 8]

    fin_in_recv[part] = fin_in_send[part]
    for k in range(1, 8):
        n = (part + k) % 8
        push(
            fin_in_send.at[n], fin_in_recv.at[part], last_send.at[0], last_in.at[0], z * 8 + n, y
        )
    to_sp = part * 8 + z
    odd = y % 2
    push(
        fin_out_send.at[1 - odd],
        fin_out_recv.at[odd],
        last_send.at[1],
        last_out.at[0],
        to_sp,
        y + 1 - 2 * odd,
    )

    @pl.when(part == z)
    def _():
        fin_out_recv[odd] = fin_out_send[odd]

    @pl.when(part != z)
    def _():
        push(
            fin_out_send.at[odd],
            fin_out_recv.at[odd],
            last_send.at[2],
            last_out.at[1],
            to_sp,
            y,
        )
        await_bytes(fin_out_recv.at[0], last_out.at[1])
        await_bytes(fin_out_send.at[0], last_send.at[2])

    await_bytes(fin_out_recv.at[0], last_out.at[0])
    for n in range(2):
        out_out[:, n * 512 : (n + 1) * 512] = fin_out_recv[n]
    await_bytes(fin_in_recv.at[pl.ds(0, 7)], last_in.at[0])
    for n in range(8):
        out_in[:, n * 256 : (n + 1) * 256] = fin_in_recv[n]

    for i in range(5):
        drain_piece(i)
    share_drain(0, cot_all)
    share_drain(1, normed_all)
    await_bytes(obs_recv.at[pl.ds(0, 189)], bulk_send.at[0])
    await_bytes(patch_recv.at[pl.ds(0, 63)], bulk_send.at[1])
    await_bytes(lat_own.at[pl.ds(0, 31)], bulk_send.at[2])
    await_bytes(lat_sib, bulk_send.at[3])
    await_bytes(lat_out.at[pl.ds(0, 31)], bulk_send.at[4])
    await_bytes(gin_recv.at[pl.ds(0, 31)], bulk_send.at[5])
    await_bytes(gout_recv.at[pl.ds(0, 31)], bulk_send.at[6])
    await_bytes(fin_in_send.at[pl.ds(0, 7)], last_send.at[0])
    await_bytes(fin_out_send.at[0], last_send.at[1])


def scratch():
    vmem = pltpu.VMEM
    dma = pltpu.SemaphoreType.DMA
    return [
        vmem((128, 1024), BF),
        vmem((128, 1024), BF),
        vmem((96, 2048), BF),
        vmem((1, 96), jnp.int32),
        vmem((1, 96), jnp.int32),
        vmem((1536, 128), F32),
        vmem((96, 16, 128), BF),
        vmem((1, 256), jnp.int32),
        pltpu.SMEM((1, 256), jnp.int32),
        vmem((64, 1, 128), F32),
        vmem((1024, 1024), BF),
        vmem((1024, 1024), BF),
        vmem((1024, 3072), BF),
        vmem((1024, 1024), BF),
        vmem((1024, 256), BF),
        vmem((256, 1024), BF),
        vmem((192, 16, 128), BF),
        vmem((192, 16, 128), BF),
        vmem((3072, 128), F32),
        vmem((64, 1, 128), F32),
        vmem((128, 1024), BF),
        vmem((128, 1024), BF),
        vmem((128, 1024), BF),
        vmem((128, 3072), BF),
        vmem((32, 16, 384), BF),
        vmem((32, 16, 256), BF),
        vmem((512, 128), F32),
        vmem((512, 128), F32),
        vmem((512, 128), F32),
        vmem((512, 128), F32),
        vmem((512, 128), F32),
        vmem((512, 128), F32),
        vmem((32, 16, 128), BF),
        vmem((128, 512), BF),
        vmem((128, 512), BF),
        vmem((1024, 1024), BF),
        vmem((1024, 1024), BF),
        vmem((256, 1024), BF),
        vmem((256, 1024), BF),
        vmem((1024, 256), BF),
        vmem((256, 1024), BF),
        vmem((32, 32, 256), BF),
        vmem((32, 16, 512), BF),
        vmem((8, 4, 256), F32),
        vmem((8, 4, 256), F32),
        vmem((2, 8, 512), F32),
        vmem((2, 8, 512), F32),
        dma((13,)),
        dma((5, 4)),
        dma((5, 4)),
        dma((2,)),
        dma((2, 4)),
        dma((2,)),
        dma((2,)),
        dma((7,)),
        dma((7,)),
        dma((3,)),
        dma((1,)),
        dma((2,)),
    ]


def local(
    grid_tokens,
    cotangent,
    obs_pairs,
    obs_route,
    obs_patch,
    w_query,
    w_cross_out,
    w_qkv,
    w_axial_out,
    w_in,
    w_out,
):
    vmem = pl.BlockSpec(memory_space=pltpu.VMEM)
    hbm = pl.BlockSpec(memory_space=pltpu.HBM)
    return pl.pallas_call(
        kernel,
        out_shape=(
            jax.ShapeDtypeStruct((4, 2048), F32),
            jax.ShapeDtypeStruct((8, 1024), F32),
        ),
        in_specs=[hbm] * 11,
        out_specs=(vmem, vmem),
        scratch_shapes=scratch(),
        compiler_params=pltpu.CompilerParams(
            collective_id=0, has_side_effects=True, vmem_limit_bytes=62 * 1024 * 1024
        ),
    )(
        grid_tokens.reshape(128, 1024),
        cotangent.reshape(128, 1024),
        obs_pairs.reshape(96, 2048),
        obs_route.reshape(1, 96),
        obs_patch.reshape(1, 96),
        w_query,
        w_cross_out,
        w_qkv,
        w_axial_out,
        w_in,
        w_out,
    )


def solution(mesh):
    return jax.shard_map(
        local,
        mesh=mesh,
        in_specs=(
            P("dp", "sp", None, None),
            P("dp", "sp", None, None),
            P("dp", "sp", None, None),
            P("dp", "sp", None, None),
            P("dp", "sp", None),
            P("dp", None),
            P("dp", None),
            P("dp", None),
            P("dp", None),
            P(),
            P(),
        ),
        out_specs=(P(("sp", "dp"), None), P(("sp", "dp"), None)),
        check_vma=False,
    )
```

```python
import jax
import jax.numpy as jnp
from jax import lax
from jax.experimental import pallas as pl
from jax.experimental.pallas import tpu as pltpu
from jax.sharding import PartitionSpec as P

BF = jnp.bfloat16
F32 = jnp.float32
EPS = 1e-06
ROOT_HALF = 0.7071067811865476
INV_ROOT_TWO_PI = 0.3989422804014327
SCALE = 0.125


def normalize(values):
    values = values.astype(F32)
    return values * lax.rsqrt(jnp.mean(values * values, axis=-1, keepdims=True) + EPS)


def dot(a, b):
    return jnp.dot(a, b, preferred_element_type=F32)


def dot_t(a, b):
    return lax.dot_general(a, b, (((1,), (1,)), ((), ())), preferred_element_type=F32)


def mult(value, by):
    return pl.multiple_of(value, by)


def push(src, dst, send, recv, sp, dp):
    pltpu.make_async_remote_copy(
        src_ref=src,
        dst_ref=dst,
        send_sem=send,
        recv_sem=recv,
        device_id={"sp": sp, "dp": dp},
        device_id_type=pl.DeviceIdType.MESH,
    ).start()


def await_bytes(ref, sem):
    pltpu.make_async_copy(ref, ref, sem).wait()


def kernel(
    tokens_hbm,
    cot_hbm,
    pairs_hbm,
    route_hbm,
    patch_hbm,
    wq_hbm,
    wc_hbm,
    wkv_hbm,
    wa_hbm,
    wi_hbm,
    wo_hbm,
    out_in,
    out_out,
    tokens,
    cot,
    pairs,
    route,
    patch,
    pairs_wide,
    pairs_tiles,
    index_row,
    src_index,
    slot_patch,
    wq,
    wc,
    wkv,
    wa,
    wi,
    wo,
    obs_send,
    obs_recv,
    obs_wide,
    patch_recv,
    queries,
    context,
    after_cross,
    axial,
    lat_own,
    lat_sib,
    q_wide,
    k_wide,
    v_wide,
    ks_wide,
    vs_wide,
    o_wide,
    lat_out,
    lat_context,
    lon_context,
    axial_sum,
    normed_all,
    cot_all,
    hidden_t,
    pre_grad_t,
    gin_send,
    gout_send,
    gin_recv,
    gout_recv,
    fin_in_send,
    fin_in_recv,
    fin_out_send,
    fin_out_recv,
    local_sem,
    w_send,
    w_recv,
    gather_send,
    gather_recv,
    share_send,
    share_recv,
    bulk_send,
    bulk_recv,
    last_send,
    last_in,
    last_out,
):
    sp = lax.axis_index("sp")
    y = lax.axis_index("dp")
    core = sp % 2
    sib = sp + 1 - 2 * core
    chip = sp // 2
    x = chip % 4
    z = chip // 4
    part = sp % 8

    barrier = pltpu.get_barrier_semaphore()

    def greet(to_sp, to_dp):
        pl.semaphore_signal(
            barrier,
            inc=1,
            device_id={"sp": to_sp, "dp": to_dp},
            device_id_type=pl.DeviceIdType.MESH,
        )

    def greet_row(k, carry):
        greet((sp + k) % 64, y)
        return carry

    def greet_member(k, carry):
        for other in range(1, 4):
            greet(k * 8 + part, (y + other) % 4)
        return carry

    lax.fori_loop(1, 64, greet_row, 0)
    lax.fori_loop(0, 8, greet_member, 0)
    greet(part * 8 + z, y + 1 - 2 * (y % 2))

    loads = [
        pltpu.make_async_copy(source, target, local_sem.at[7 + i])
        for i, (source, target) in enumerate(
            (
                (route_hbm, route),
                (patch_hbm, patch),
                (pairs_hbm, pairs),
                (tokens_hbm, tokens),
                (cot_hbm, cot),
            )
        )
    ]
    for load in loads:
        load.start()

    pieces = (
        (wq_hbm, wq, 0, 1024, "x"),
        (wc_hbm, wc, 0, 1024, "x"),
        (wkv_hbm, wkv, 0, 1536, "xz"),
        (wkv_hbm, wkv, 1536, 1536, "zx"),
        (wa_hbm, wa, 0, 1024, "x"),
    )
    place_of = {"x": (x + core) % 2, "z": (z + core) % 2}
    mate_of = {
        "x": z * 8 + ((x + 5 - 2 * place_of["x"]) % 4) * 2 + core,
        "z": ((z + 9 - 2 * place_of["z"]) % 8) * 8 + x * 2 + core,
    }

    def spans(plan):
        rows = 128 >> len(plan)
        first = core * 128
        for n, axis in enumerate(plan):
            first += place_of[axis] * (rows << n)
        made = [(first, rows, None)]
        for n, axis in enumerate(plan):
            made.append((first, rows << n, mate_of[axis]))
            first -= place_of[axis] * (rows << n)
        made.append((core * 128, 128, sib))
        return made

    stages = [spans(piece[4]) for piece in pieces]

    def landing(i, stage):
        full, col, width = pieces[i][1:4]
        return full.at[pl.ds(0, 3 * stages[i][stage][1]), pl.ds(col, width)]

    def start_piece(i):
        hbm, full, col, width, _ = pieces[i]
        first, rows, _ = stages[i][0]
        for k in range(1, 4):
            push(
                hbm.at[pl.ds(mult(first, 32), rows), pl.ds(col, width)],
                full.at[pl.ds(mult(y * 256 + first, 32), rows), pl.ds(col, width)],
                w_send.at[i, 0],
                w_recv.at[i, 0],
                sp,
                (y + k) % 4,
            )

    def own_piece(i):
        hbm, full, col, width, _ = pieces[i]
        return pltpu.make_async_copy(
            hbm.at[:, pl.ds(col, width)],
            full.at[pl.ds(mult(y * 256, 256), 256), pl.ds(col, width)],
            local_sem.at[i],
        )

    def advance(i, stage):
        full, col, width = pieces[i][1:4]
        await_bytes(landing(i, stage - 1), w_recv.at[i, stage - 1])
        first, rows, mate = stages[i][stage]
        for k in range(1, 4):
            part_rows = full.at[
                pl.ds(mult(((y + k) % 4) * 256 + first, 32), rows), pl.ds(col, width)
            ]
            push(part_rows, part_rows, w_send.at[i, stage], w_recv.at[i, stage], mate, y)

    def finish_piece(i):
        last = len(stages[i]) - 1
        await_bytes(landing(i, last), w_recv.at[i, last])
        own_piece(i).wait()

    def drain_piece(i):
        for stage in range(len(stages[i])):
            await_bytes(landing(i, stage), w_send.at[i, stage])

    for i in range(5):
        own_piece(i).start()
    wi_copy = pltpu.make_async_copy(
        wi_hbm.at[:, pl.ds(mult(part * 256, 256), 256)], wi, local_sem.at[5]
    )
    wo_copy = pltpu.make_async_copy(
        wo_hbm.at[pl.ds(mult(part * 256, 256), 256), :], wo, local_sem.at[6]
    )
    wi_copy.start()
    wo_copy.start()

    loads[0].wait()
    loads[1].wait()
    line = lax.broadcasted_iota(jnp.int32, (96, 96), 0)
    lane = lax.broadcasted_iota(jnp.int32, (96, 96), 1)

    def upright(row):
        return jnp.sum(jnp.where(line == lane, row, 0), axis=1, keepdims=True)

    row_across = route[...]
    row_down = upright(row_across)
    patch_across = patch[...] + 1
    same = row_across == row_down
    rank_across = jnp.sum(jnp.where(same & (line < lane), 1, 0), axis=0, keepdims=True)
    rank_down = jnp.sum(jnp.where(same & (lane < line), 1, 0), axis=1, keepdims=True)
    slot_across = row_across * 3 + rank_across
    slot_down = row_down * 3 + rank_down
    hit = slot_down == lax.broadcasted_iota(jnp.int32, (96, 256), 1)
    index_row[...] = jnp.sum(
        jnp.where(hit, lax.broadcasted_iota(jnp.int32, (96, 256), 0), 0), axis=0, keepdims=True
    )
    index_copy = pltpu.make_async_copy(index_row, src_index, local_sem.at[12])
    index_copy.start()
    lanes = lax.broadcasted_iota(jnp.int32, (64, 128), 1)
    found_patch = jnp.zeros((64, 128), jnp.int32)
    for r in range(3):
        mine = slot_across == lax.broadcasted_iota(jnp.int32, (64, 96), 0) * 3 + r
        value = jnp.sum(jnp.where(mine, patch_across, 0), axis=1, keepdims=True) - 1
        found_patch = jnp.where(lanes == r, value, found_patch)
    slot_patch[...] = found_patch.astype(F32).reshape(64, 1, 128)

    loads[2].wait()
    for n in range(16):
        pairs_wide[pl.ds(n, 96, stride=16), :] = pairs[:, n * 128 : (n + 1) * 128].astype(F32)
    pairs_tiles[...] = pairs_wide[...].reshape(96, 16, 128).astype(BF)
    index_copy.wait()

    def place(s, carry):
        obs_send[s] = pairs_tiles[src_index[0, s]]
        return carry

    lax.fori_loop(0, 192, place, 0, unroll=8)
    pl.semaphore_wait(barrier, 88)
    start_piece(0)

    def send_obs(k, carry):
        to = (sp + k) % 64
        push(
            obs_send.at[pl.ds(to * 3, 3)],
            obs_recv.at[pl.ds(sp * 3, 3)],
            bulk_send.at[0],
            bulk_recv.at[0],
            to,
            y,
        )
        push(slot_patch.at[to], patch_recv.at[sp], bulk_send.at[1], bulk_recv.at[1], to, y)
        return carry

    lax.fori_loop(1, 64, send_obs, 0)
    start_piece(1)
    obs_recv[pl.ds(sp * 3, 3)] = obs_send[pl.ds(sp * 3, 3)]
    patch_recv[sp] = slot_patch[sp]

    def share_start(j, source, full):
        rows = full.at[pl.ds(mult(part * 128, 128), 128), :]
        push(source, rows, gather_send.at[j], gather_recv.at[j, 0], sib, y)
        for k in range(1, 4):
            push(
                source,
                rows,
                gather_send.at[j],
                gather_recv.at[j, k],
                z * 8 + ((x + k) % 4) * 2 + core,
                y,
            )

    def from_chip(full, k, cores):
        first = ((x - k + 4) % 4) * 256 + (core * 128 if cores == 1 else 0)
        return full.at[pl.ds(mult(first, 128), 128 * cores), :]

    def share_forward(j, full, k):
        rows = from_chip(full, k, 1)
        await_bytes(rows, gather_recv.at[j, k])
        push(rows, rows, share_send.at[j], share_recv.at[j, k], sib, y)

    def share_drain(j, full):
        await_bytes(full.at[pl.ds(0, 512), :], gather_send.at[j])
        await_bytes(full.at[pl.ds(0, 384), :], share_send.at[j])

    loads[3].wait()
    loads[4].wait()
    cot_all[pl.ds(mult(part * 128, 128), 128), :] = cot[...]

    normed = normalize(tokens[...]).astype(BF)
    advance(0, 1)
    start_piece(2)
    advance(1, 1)
    start_piece(3)
    advance(0, 2)
    finish_piece(0)

    def columns(count, width, source, weight, target, offset):
        def step(n, carry):
            cols = pl.ds(mult(offset + n * width, width), width)
            target[:, cols] = dot(source, weight[:, cols]).astype(BF)
            return carry

        lax.fori_loop(0, count, step, 0)

    columns(4, 256, normed, wq, queries, 0)
    advance(1, 2)
    advance(2, 1)
    start_piece(4)
    advance(3, 1)
    advance(2, 2)
    advance(4, 1)

    await_bytes(obs_recv.at[pl.ds(0, 189)], bulk_recv.at[0])
    await_bytes(patch_recv.at[pl.ds(0, 63)], bulk_recv.at[1])
    advance(2, 3)
    advance(3, 2)
    obs_wide[...] = obs_recv[...].astype(F32).reshape(3072, 128)
    patches = patch_recv[...].reshape(64, 128)
    slot_lane = lax.broadcasted_iota(jnp.int32, (64, 192), 1)
    slot_from = lax.broadcasted_iota(jnp.int32, (64, 192), 0) * 3
    slot_row = jnp.zeros((1, 192), F32)
    for r in range(3):
        slot_row += jnp.sum(
            jnp.where(slot_lane == slot_from + r, patches[:, r : r + 1], 0.0),
            axis=0,
            keepdims=True,
        )
    cell_patch = (lax.broadcasted_iota(jnp.int32, (128, 192), 0) // 32).astype(F32)
    same_patch = cell_patch == slot_row
    low = lax.broadcasted_iota(jnp.int32, (128, 128), 1) < 64
    zero = jnp.zeros((128, 128), BF)

    def cross_pair(g, carry):
        cols = pl.ds(mult(g * 128, 128), 128)
        keys = obs_wide[pl.ds(g, 192, stride=16), :].astype(BF)
        values = obs_wide[pl.ds(g + 8, 192, stride=16), :].astype(BF)
        both = queries[:, cols]
        found = []
        for half in (jnp.where(low, both, zero), jnp.where(low, zero, both)):
            masked = jnp.where(same_patch, dot_t(half, keys) * SCALE, -1e30)
            top = jnp.maximum(jnp.max(masked, axis=-1, keepdims=True), 0.0)
            terms = jnp.where(same_patch, jnp.exp(masked - top), 0.0)
            total = jnp.exp(-top) + jnp.sum(terms, axis=-1, keepdims=True)
            found.append(dot((terms / total).astype(BF), values))
        context[:, cols] = jnp.where(low, found[0], found[1]).astype(BF)
        return carry

    lax.fori_loop(0, 8, cross_pair, 0, unroll=4)

    advance(3, 3)
    advance(4, 2)
    finish_piece(1)

    def cross_out(n, carry):
        cols = pl.ds(mult(n * 256, 256), 256)
        after_cross[:, cols] = (
            tokens[:, cols].astype(F32) + dot(context[...], wc[:, cols])
        ).astype(BF)
        return carry

    lax.fori_loop(0, 4, cross_out, 0)
    normed_axial = normalize(after_cross[...]).astype(BF)
    finish_piece(2)
    columns(6, 256, normed_axial, wkv, axial, 0)

    cell_at, group_at = z, x

    def send_lat(k, carry):
        to = (chip + k) % 32
        push(
            axial.at[pl.ds(mult((to // 4) * 16, 16), 16), pl.ds(mult((to % 4) * 384, 128), 384)],
            lat_own.at[chip],
            bulk_send.at[2],
            bulk_recv.at[2],
            to * 2 + core,
            y,
        )
        return carry

    lax.fori_loop(1, 32, send_lat, 0)
    lat_own[chip] = axial[pl.ds(mult(cell_at * 16, 16), 16), pl.ds(mult(group_at * 384, 128), 384)]

    share_start(0, cot, cot_all)

    finish_piece(3)
    columns(6, 256, normed_axial, wkv, axial, 1536)

    def lon_pair(p, carry):
        both = axial[:, pl.ds(mult(1536 + p * 128, 128), 128)]
        keys = axial[:, pl.ds(mult(2048 + p * 128, 128), 128)]
        values = axial[:, pl.ds(mult(2560 + p * 128, 128), 128)]
        found = []
        for half in (jnp.where(low, both, zero), jnp.where(low, zero, both)):
            scores = dot_t(half, keys) * SCALE
            terms = jnp.exp(scores - jnp.max(scores, axis=-1, keepdims=True))
            weights = (terms / jnp.sum(terms, axis=-1, keepdims=True)).astype(BF)
            found.append(dot(weights, values))
        lon_context[:, pl.ds(mult(p * 128, 128), 128)] = jnp.where(low, found[0], found[1]).astype(
            BF
        )
        return carry

    lat_kv = lat_own.at[:, :, pl.ds(128, 256)]
    await_bytes(lat_own.at[pl.ds(0, 31)], bulk_recv.at[2])
    push(lat_kv, lat_sib, bulk_send.at[3], bulk_recv.at[3], sib, y)
    lax.fori_loop(0, 4, lon_pair, 0, unroll=4)
    q_wide[...] = lat_own[:, :, 0:128].astype(F32).reshape(512, 128)
    k_wide[...] = lat_own[:, :, 128:256].astype(F32).reshape(512, 128)
    v_wide[...] = lat_own[:, :, 256:384].astype(F32).reshape(512, 128)
    await_bytes(lat_sib, bulk_recv.at[3])
    ks_wide[...] = lat_sib[:, :, 0:128].astype(F32).reshape(512, 128)
    vs_wide[...] = lat_sib[:, :, 128:256].astype(F32).reshape(512, 128)
    low_rows = lax.broadcasted_iota(jnp.int32, (32, 128), 1) < 64

    def lat_cell(l, carry):
        rows = pl.ds(l, 32, stride=16)
        q = q_wide[rows, :]
        both = jnp.concatenate(
            [jnp.where(low_rows, q, 0.0), jnp.where(low_rows, 0.0, q)], axis=0
        ).astype(BF)
        keys = jnp.concatenate([k_wide[rows, :], ks_wide[rows, :]], axis=0).astype(BF)
        values = jnp.concatenate([v_wide[rows, :], vs_wide[rows, :]], axis=0).astype(BF)
        scores = dot_t(both, keys) * SCALE
        terms = jnp.exp(scores - jnp.max(scores, axis=-1, keepdims=True))
        weights = (terms / jnp.sum(terms, axis=-1, keepdims=True)).astype(BF)
        found = dot(weights, values)
        o_wide[rows, :] = jnp.where(low_rows, found[:32], found[32:])
        return carry

    lax.fori_loop(0, 16, lat_cell, 0, unroll=8)
    lat_out[...] = o_wide[...].reshape(32, 16, 128).astype(BF)
    home = (pl.ds(mult(cell_at * 16, 16), 16), pl.ds(mult(group_at * 128, 128), 128))

    def send_back(k, carry):
        to = (chip + k) % 32
        push(
            lat_out.at[to],
            lat_context.at[home],
            bulk_send.at[4],
            bulk_recv.at[4],
            to * 2 + core,
            y,
        )
        return carry

    lax.fori_loop(1, 32, send_back, 0)
    lat_context[home] = lat_out[chip]
    finish_piece(4)

    def axial_lon(n, carry):
        cols = pl.ds(mult(n * 256, 256), 256)
        axial_sum[:, cols] = after_cross[:, cols].astype(F32) + dot(
            lon_context[...], wa[pl.ds(512, 512), cols]
        )
        return carry

    def axial_lat(n, carry):
        cols = pl.ds(mult(n * 256, 256), 256)
        context[:, cols] = (
            axial_sum[:, cols] + dot(lat_context[...], wa[pl.ds(0, 512), cols])
        ).astype(BF)
        return carry

    lax.fori_loop(0, 4, axial_lon, 0)
    await_bytes(lat_out.at[pl.ds(0, 31)], bulk_recv.at[4])
    lax.fori_loop(0, 4, axial_lat, 0)
    mine = pl.ds(mult(part * 128, 128), 128)
    normed_all[mine, :] = normalize(context[...]).astype(BF)
    share_start(1, normed_all.at[mine, :], normed_all)
    for k in range(1, 4):
        share_forward(0, cot_all, k)
    await_bytes(cot_all.at[pl.ds(0, 128), :], gather_recv.at[0, 0])
    for k in range(1, 4):
        await_bytes(from_chip(cot_all, k, 1), share_recv.at[0, k])
    wi_copy.wait()
    wo_copy.wait()
    await_bytes(normed_all.at[pl.ds(0, 128), :], gather_recv.at[1, 0])

    def ff_chip(i, carry):
        k = jnp.where(i == 2, 3, jnp.where(i == 3, 2, i))

        @pl.when(i == 1)
        def _():
            share_forward(1, normed_all, 1)
            share_forward(1, normed_all, 3)

        @pl.when(i == 2)
        def _():
            share_forward(1, normed_all, 2)

        @pl.when(i > 0)
        def _():
            await_bytes(normed_all.at[pl.ds(0, 128), :], share_recv.at[1, k])

        rows = pl.ds(mult(((x - k + 4) % 4) * 256, 256), 256)
        pre_act = dot(normed_all[rows, :], wi[...])
        hidden_grad = dot_t(cot_all[rows, :], wo[...])
        cdf = 0.5 * (1.0 + lax.erf(pre_act * ROOT_HALF))
        slope = cdf + pre_act * jnp.exp(-0.5 * pre_act * pre_act) * INV_ROOT_TWO_PI
        hidden_t[:, rows] = (pre_act * cdf).astype(BF).T
        pre_grad_t[:, rows] = (hidden_grad * slope).astype(BF).T
        return carry

    lax.fori_loop(0, 4, ff_chip, 0)

    place_at = z * 4 + y

    def in_block(to):
        return (pl.ds(mult(to * 32, 32), 32), slice(None))

    def out_block(to):
        return (pl.ds(mult((to // 2) * 16, 16), 16), pl.ds(mult((to % 2) * 512, 512), 512))

    def send_grads(source, block, received, at):
        def one(k, carry):
            to = (place_at + k) % 32
            push(
                source.at[block(to)],
                received.at[place_at],
                bulk_send.at[at],
                bulk_recv.at[at],
                (to // 4) * 8 + part,
                to % 4,
            )
            return carry

        lax.fori_loop(1, 32, one, 0)
        received[place_at] = source[block(place_at)]

    def grad_out_cols(n, carry):
        cols = pl.ds(mult(n * 256, 256), 256)
        gout_send[:, cols] = dot(hidden_t[...], cot_all[:, cols]).astype(BF)
        return carry

    lax.fori_loop(0, 4, grad_out_cols, 0)
    send_grads(gout_send, out_block, gout_recv, 6)

    down = lax.broadcasted_iota(jnp.int32, (128, 128), 0)
    across = lax.broadcasted_iota(jnp.int32, (128, 128), 1)
    turn = (across == ((down % 32) // 4) * 16 + (down // 32) * 4 + down % 4).astype(F32).astype(BF)

    def grad_cols(n, carry):
        cols = pl.ds(mult(n * 256, 256), 256)
        grad = dot(pre_grad_t[...], normed_all[:, cols]).astype(BF)
        for half in range(2):
            gin_send[pl.ds(mult(n * 256 + half * 128, 128), 128), :] = dot_t(
                turn, grad[:, half * 128 : half * 128 + 128]
            ).astype(BF)
        return carry

    lax.fori_loop(0, 4, grad_cols, 0)

    send_grads(gin_send, in_block, gin_recv, 5)
    def add_in(n, total):
        return total + gin_recv[n].astype(F32)

    def add_out(n, total):
        return total + gout_recv[n].astype(F32)

    await_bytes(gout_recv.at[pl.ds(0, 31)], bulk_recv.at[6])
    sum_out = lax.fori_loop(0, 32, add_out, jnp.zeros((16, 512), F32), unroll=4)
    await_bytes(gin_recv.at[pl.ds(0, 31)], bulk_recv.at[5])
    sum_in = lax.fori_loop(0, 32, add_in, jnp.zeros((32, 256), F32), unroll=4)
    for n in range(8):
        fin_in_send[n] = sum_in[n * 4 : n * 4 + 4]
    for n in range(2):
        fin_out_send[n] = sum_out[n * 8 : n * 8 + 8]

    fin_in_recv[part] = fin_in_send[part]
    for k in range(1, 8):
        n = (part + k) % 8
        push(
            fin_in_send.at[n], fin_in_recv.at[part], last_send.at[0], last_in.at[0], z * 8 + n, y
        )
    to_sp = part * 8 + z
    odd = y % 2
    push(
        fin_out_send.at[1 - odd],
        fin_out_recv.at[odd],
        last_send.at[1],
        last_out.at[0],
        to_sp,
        y + 1 - 2 * odd,
    )

    @pl.when(part == z)
    def _():
        fin_out_recv[odd] = fin_out_send[odd]

    @pl.when(part != z)
    def _():
        push(
            fin_out_send.at[odd],
            fin_out_recv.at[odd],
            last_send.at[2],
            last_out.at[1],
            to_sp,
            y,
        )
        await_bytes(fin_out_recv.at[0], last_out.at[1])
        await_bytes(fin_out_send.at[0], last_send.at[2])

    await_bytes(fin_out_recv.at[0], last_out.at[0])
    for n in range(2):
        out_out[:, n * 512 : (n + 1) * 512] = fin_out_recv[n]
    await_bytes(fin_in_recv.at[pl.ds(0, 7)], last_in.at[0])
    for n in range(8):
        out_in[:, n * 256 : (n + 1) * 256] = fin_in_recv[n]

    for i in range(5):
        drain_piece(i)
    share_drain(0, cot_all)
    share_drain(1, normed_all)
    await_bytes(obs_recv.at[pl.ds(0, 189)], bulk_send.at[0])
    await_bytes(patch_recv.at[pl.ds(0, 63)], bulk_send.at[1])
    await_bytes(lat_own.at[pl.ds(0, 31)], bulk_send.at[2])
    await_bytes(lat_sib, bulk_send.at[3])
    await_bytes(lat_out.at[pl.ds(0, 31)], bulk_send.at[4])
    await_bytes(gin_recv.at[pl.ds(0, 31)], bulk_send.at[5])
    await_bytes(gout_recv.at[pl.ds(0, 31)], bulk_send.at[6])
    await_bytes(fin_in_send.at[pl.ds(0, 7)], last_send.at[0])
    await_bytes(fin_out_send.at[0], last_send.at[1])


def scratch():
    vmem = pltpu.VMEM
    dma = pltpu.SemaphoreType.DMA
    return [
        vmem((128, 1024), BF),
        vmem((128, 1024), BF),
        vmem((96, 2048), BF),
        vmem((1, 96), jnp.int32),
        vmem((1, 96), jnp.int32),
        vmem((1536, 128), F32),
        vmem((96, 16, 128), BF),
        vmem((1, 256), jnp.int32),
        pltpu.SMEM((1, 256), jnp.int32),
        vmem((64, 1, 128), F32),
        vmem((1024, 1024), BF),
        vmem((1024, 1024), BF),
        vmem((1024, 3072), BF),
        vmem((1024, 1024), BF),
        vmem((1024, 256), BF),
        vmem((256, 1024), BF),
        vmem((192, 16, 128), BF),
        vmem((192, 16, 128), BF),
        vmem((3072, 128), F32),
        vmem((64, 1, 128), F32),
        vmem((128, 1024), BF),
        vmem((128, 1024), BF),
        vmem((128, 1024), BF),
        vmem((128, 3072), BF),
        vmem((32, 16, 384), BF),
        vmem((32, 16, 256), BF),
        vmem((512, 128), F32),
        vmem((512, 128), F32),
        vmem((512, 128), F32),
        vmem((512, 128), F32),
        vmem((512, 128), F32),
        vmem((512, 128), F32),
        vmem((32, 16, 128), BF),
        vmem((128, 512), BF),
        vmem((128, 512), BF),
        vmem((128, 1024), F32),
        vmem((1024, 1024), BF),
        vmem((1024, 1024), BF),
        vmem((256, 1024), BF),
        vmem((256, 1024), BF),
        vmem((1024, 256), BF),
        vmem((256, 1024), BF),
        vmem((32, 32, 256), BF),
        vmem((32, 16, 512), BF),
        vmem((8, 4, 256), F32),
        vmem((8, 4, 256), F32),
        vmem((2, 8, 512), F32),
        vmem((2, 8, 512), F32),
        dma((13,)),
        dma((5, 4)),
        dma((5, 4)),
        dma((2,)),
        dma((2, 4)),
        dma((2,)),
        dma((2, 4)),
        dma((7,)),
        dma((7,)),
        dma((3,)),
        dma((1,)),
        dma((2,)),
    ]


def local(
    grid_tokens,
    cotangent,
    obs_pairs,
    obs_route,
    obs_patch,
    w_query,
    w_cross_out,
    w_qkv,
    w_axial_out,
    w_in,
    w_out,
):
    vmem = pl.BlockSpec(memory_space=pltpu.VMEM)
    hbm = pl.BlockSpec(memory_space=pltpu.HBM)
    return pl.pallas_call(
        kernel,
        out_shape=(
            jax.ShapeDtypeStruct((4, 2048), F32),
            jax.ShapeDtypeStruct((8, 1024), F32),
        ),
        in_specs=[hbm] * 11,
        out_specs=(vmem, vmem),
        scratch_shapes=scratch(),
        compiler_params=pltpu.CompilerParams(
            collective_id=0, has_side_effects=True, vmem_limit_bytes=62 * 1024 * 1024
        ),
    )(
        grid_tokens.reshape(128, 1024),
        cotangent.reshape(128, 1024),
        obs_pairs.reshape(96, 2048),
        obs_route.reshape(1, 96),
        obs_patch.reshape(1, 96),
        w_query,
        w_cross_out,
        w_qkv,
        w_axial_out,
        w_in,
        w_out,
    )


def solution(mesh):
    return jax.shard_map(
        local,
        mesh=mesh,
        in_specs=(
            P("dp", "sp", None, None),
            P("dp", "sp", None, None),
            P("dp", "sp", None, None),
            P("dp", "sp", None, None),
            P("dp", "sp", None),
            P("dp", None),
            P("dp", None),
            P("dp", None),
            P("dp", None),
            P(),
            P(),
        ),
        out_specs=(P(("sp", "dp"), None), P(("sp", "dp"), None)),
        check_vma=False,
    )
```

```python
import jax
import jax.numpy as jnp
from jax import lax
from jax.experimental import pallas as pl
from jax.experimental.pallas import tpu as pltpu
from jax.sharding import PartitionSpec as P

BF = jnp.bfloat16
F32 = jnp.float32
EPS = 1e-06
ROOT_HALF = 0.7071067811865476
INV_ROOT_TWO_PI = 0.3989422804014327
SCALE = 0.125


def normalize(values):
    values = values.astype(F32)
    return values * lax.rsqrt(jnp.mean(values * values, axis=-1, keepdims=True) + EPS)


def dot(a, b):
    return jnp.dot(a, b, preferred_element_type=F32)


def dot_t(a, b):
    return lax.dot_general(a, b, (((1,), (1,)), ((), ())), preferred_element_type=F32)


def mult(value, by):
    return pl.multiple_of(value, by)


def push(src, dst, send, recv, sp, dp):
    pltpu.make_async_remote_copy(
        src_ref=src,
        dst_ref=dst,
        send_sem=send,
        recv_sem=recv,
        device_id={"sp": sp, "dp": dp},
        device_id_type=pl.DeviceIdType.MESH,
    ).start()


def await_bytes(ref, sem):
    pltpu.make_async_copy(ref, ref, sem).wait()


def kernel(
    tokens_hbm,
    cot_hbm,
    pairs_hbm,
    route_hbm,
    patch_hbm,
    wq_hbm,
    wc_hbm,
    wkv_hbm,
    wa_hbm,
    wi_hbm,
    wo_hbm,
    out_in,
    out_out,
    tokens,
    cot,
    pairs,
    route,
    patch,
    pairs_wide,
    pairs_tiles,
    index_row,
    src_index,
    slot_patch,
    wq,
    wc,
    wkv,
    wa,
    wi,
    wo,
    obs_send,
    obs_recv,
    obs_wide,
    patch_recv,
    queries,
    context,
    after_cross,
    axial,
    lat_own,
    lat_sib,
    q_wide,
    k_wide,
    v_wide,
    ks_wide,
    vs_wide,
    o_wide,
    lat_out,
    lat_context,
    lon_context,
    axial_sum,
    normed_all,
    cot_all,
    hidden_t,
    pre_grad_t,
    gin_send,
    gout_send,
    gin_recv,
    gout_recv,
    gin_mid,
    gout_mid,
    gin_ends,
    gout_ends,
    fin_in_send,
    fin_in_recv,
    fin_out_send,
    fin_out_recv,
    local_sem,
    w_send,
    w_recv,
    gather_send,
    gather_recv,
    share_send,
    share_recv,
    bulk_send,
    bulk_recv,
    last_send,
    last_in,
    last_out,
    entered,
):
    sp = lax.axis_index("sp")
    y = lax.axis_index("dp")
    core = sp % 2
    sib = sp + 1 - 2 * core
    chip = sp // 2
    x = chip % 4
    z = chip // 4
    part = sp % 8

    barrier = pltpu.get_barrier_semaphore()

    def greet(to_sp, to_dp):
        pl.semaphore_signal(
            barrier,
            inc=1,
            device_id={"sp": to_sp, "dp": to_dp},
            device_id_type=pl.DeviceIdType.MESH,
        )

    def greet_line(k, carry):
        greet(((z + k) % 8) * 8 + part, y)
        greet(z * 8 + (part + k) % 8, y)
        return carry

    lax.fori_loop(1, 8, greet_line, 0)
    for k in range(1, 4):
        greet(sp, (y + k) % 4)
    greet(part * 8 + z, y + 1 - 2 * (y % 2))

    loads = [
        pltpu.make_async_copy(source, target, local_sem.at[7 + i])
        for i, (source, target) in enumerate(
            (
                (route_hbm, route),
                (patch_hbm, patch),
                (pairs_hbm, pairs),
                (tokens_hbm, tokens),
                (cot_hbm, cot),
            )
        )
    ]
    for load in loads:
        load.start()

    pieces = (
        (wq_hbm, wq, 0, 1024, "x"),
        (wc_hbm, wc, 0, 1024, "x"),
        (wkv_hbm, wkv, 0, 1536, "xz"),
        (wkv_hbm, wkv, 1536, 1536, "zx"),
        (wa_hbm, wa, 0, 1024, "x"),
    )
    place_of = {"x": (x + core) % 2, "z": (z + core) % 2}
    mate_of = {
        "x": z * 8 + ((x + 5 - 2 * place_of["x"]) % 4) * 2 + core,
        "z": ((z + 9 - 2 * place_of["z"]) % 8) * 8 + x * 2 + core,
    }

    def spans(plan):
        rows = 128 >> len(plan)
        first = core * 128
        for n, axis in enumerate(plan):
            first += place_of[axis] * (rows << n)
        made = [(first, rows, None)]
        for n, axis in enumerate(plan):
            made.append((first, rows << n, mate_of[axis]))
            first -= place_of[axis] * (rows << n)
        made.append((core * 128, 128, sib))
        return made

    stages = [spans(piece[4]) for piece in pieces]

    def landing(i, stage):
        full, col, width = pieces[i][1:4]
        return full.at[pl.ds(0, 3 * stages[i][stage][1]), pl.ds(col, width)]

    def start_piece(i):
        hbm, full, col, width, _ = pieces[i]
        first, rows, _ = stages[i][0]
        for k in range(1, 4):
            push(
                hbm.at[pl.ds(mult(first, 32), rows), pl.ds(col, width)],
                full.at[pl.ds(mult(y * 256 + first, 32), rows), pl.ds(col, width)],
                w_send.at[i, 0],
                w_recv.at[i, 0],
                sp,
                (y + k) % 4,
            )

    def own_piece(i):
        hbm, full, col, width, _ = pieces[i]
        return pltpu.make_async_copy(
            hbm.at[:, pl.ds(col, width)],
            full.at[pl.ds(mult(y * 256, 256), 256), pl.ds(col, width)],
            local_sem.at[i],
        )

    def advance(i, stage):
        full, col, width = pieces[i][1:4]
        await_bytes(landing(i, stage - 1), w_recv.at[i, stage - 1])
        first, rows, mate = stages[i][stage]
        for k in range(1, 4):
            part_rows = full.at[
                pl.ds(mult(((y + k) % 4) * 256 + first, 32), rows), pl.ds(col, width)
            ]
            push(part_rows, part_rows, w_send.at[i, stage], w_recv.at[i, stage], mate, y)

    def finish_piece(i):
        last = len(stages[i]) - 1
        await_bytes(landing(i, last), w_recv.at[i, last])
        own_piece(i).wait()

    def drain_piece(i):
        for stage in range(len(stages[i])):
            await_bytes(landing(i, stage), w_send.at[i, stage])

    for i in range(5):
        own_piece(i).start()
    wi_copy = pltpu.make_async_copy(
        wi_hbm.at[:, pl.ds(mult(part * 256, 256), 256)], wi, local_sem.at[5]
    )
    wo_copy = pltpu.make_async_copy(
        wo_hbm.at[pl.ds(mult(part * 256, 256), 256), :], wo, local_sem.at[6]
    )
    wi_copy.start()
    wo_copy.start()

    loads[0].wait()
    loads[1].wait()
    line = lax.broadcasted_iota(jnp.int32, (96, 96), 0)
    lane = lax.broadcasted_iota(jnp.int32, (96, 96), 1)

    def upright(row):
        return jnp.sum(jnp.where(line == lane, row, 0), axis=1, keepdims=True)

    row_across = route[...]
    row_down = upright(row_across)
    patch_across = patch[...] + 1
    same = row_across == row_down
    rank_across = jnp.sum(jnp.where(same & (line < lane), 1, 0), axis=0, keepdims=True)
    rank_down = jnp.sum(jnp.where(same & (lane < line), 1, 0), axis=1, keepdims=True)
    slot_across = row_across * 3 + rank_across
    slot_down = row_down * 3 + rank_down
    hit = slot_down == lax.broadcasted_iota(jnp.int32, (96, 256), 1)
    index_row[...] = jnp.sum(
        jnp.where(hit, lax.broadcasted_iota(jnp.int32, (96, 256), 0), 0), axis=0, keepdims=True
    )
    index_copy = pltpu.make_async_copy(index_row, src_index, local_sem.at[12])
    index_copy.start()
    lanes = lax.broadcasted_iota(jnp.int32, (64, 128), 1)
    found_patch = jnp.zeros((64, 128), jnp.int32)
    for r in range(3):
        mine = slot_across == lax.broadcasted_iota(jnp.int32, (64, 96), 0) * 3 + r
        value = jnp.sum(jnp.where(mine, patch_across, 0), axis=1, keepdims=True) - 1
        found_patch = jnp.where(lanes == r, value, found_patch)
    slot_patch[...] = found_patch.astype(F32).reshape(64, 1, 128)

    pl.semaphore_wait(barrier, 18)

    def greet_again(k, carry):
        pl.semaphore_signal(
            entered,
            inc=1,
            device_id={"sp": z * 8 + (part + k) % 8, "dp": y},
            device_id_type=pl.DeviceIdType.MESH,
        )
        return carry

    lax.fori_loop(1, 8, greet_again, 0)

    loads[2].wait()
    for n in range(16):
        pairs_wide[pl.ds(n, 96, stride=16), :] = pairs[:, n * 128 : (n + 1) * 128].astype(F32)
    pairs_tiles[...] = pairs_wide[...].reshape(96, 16, 128).astype(BF)
    index_copy.wait()

    def place(s, carry):
        obs_send[s] = pairs_tiles[src_index[0, s]]
        return carry

    lax.fori_loop(0, 192, place, 0, unroll=8)
    pl.semaphore_wait(entered, 7)
    start_piece(0)

    def send_obs(k, carry):
        to = (sp + k) % 64
        push(
            obs_send.at[pl.ds(to * 3, 3)],
            obs_recv.at[pl.ds(sp * 3, 3)],
            bulk_send.at[0],
            bulk_recv.at[0],
            to,
            y,
        )
        push(slot_patch.at[to], patch_recv.at[sp], bulk_send.at[1], bulk_recv.at[1], to, y)
        return carry

    lax.fori_loop(1, 64, send_obs, 0)
    start_piece(1)
    obs_recv[pl.ds(sp * 3, 3)] = obs_send[pl.ds(sp * 3, 3)]
    patch_recv[sp] = slot_patch[sp]

    def share_start(j, source, full):
        rows = full.at[pl.ds(mult(part * 128, 128), 128), :]
        push(source, rows, gather_send.at[j], gather_recv.at[j, 0], sib, y)
        for k in range(1, 4):
            push(
                source,
                rows,
                gather_send.at[j],
                gather_recv.at[j, k],
                z * 8 + ((x + k) % 4) * 2 + core,
                y,
            )

    def from_chip(full, k, cores):
        first = ((x - k + 4) % 4) * 256 + (core * 128 if cores == 1 else 0)
        return full.at[pl.ds(mult(first, 128), 128 * cores), :]

    def share_forward(j, full, k):
        rows = from_chip(full, k, 1)
        await_bytes(rows, gather_recv.at[j, k])
        push(rows, rows, share_send.at[j], share_recv.at[j, k], sib, y)

    def share_drain(j, full):
        await_bytes(full.at[pl.ds(0, 512), :], gather_send.at[j])
        await_bytes(full.at[pl.ds(0, 384), :], share_send.at[j])

    loads[3].wait()
    loads[4].wait()
    cot_all[pl.ds(mult(part * 128, 128), 128), :] = cot[...]

    normed = normalize(tokens[...]).astype(BF)
    advance(0, 1)
    start_piece(2)
    advance(1, 1)
    start_piece(3)
    advance(0, 2)
    finish_piece(0)

    def columns(count, width, source, weight, target, offset):
        def step(n, carry):
            cols = pl.ds(mult(offset + n * width, width), width)
            target[:, cols] = dot(source, weight[:, cols]).astype(BF)
            return carry

        lax.fori_loop(0, count, step, 0)

    columns(4, 256, normed, wq, queries, 0)
    advance(1, 2)
    advance(2, 1)
    start_piece(4)
    advance(3, 1)
    advance(2, 2)
    advance(4, 1)

    await_bytes(obs_recv.at[pl.ds(0, 189)], bulk_recv.at[0])
    await_bytes(patch_recv.at[pl.ds(0, 63)], bulk_recv.at[1])
    advance(2, 3)
    advance(3, 2)
    obs_wide[...] = obs_recv[...].astype(F32).reshape(3072, 128)
    patches = patch_recv[...].reshape(64, 128)
    slot_lane = lax.broadcasted_iota(jnp.int32, (64, 192), 1)
    slot_from = lax.broadcasted_iota(jnp.int32, (64, 192), 0) * 3
    slot_row = jnp.zeros((1, 192), F32)
    for r in range(3):
        slot_row += jnp.sum(
            jnp.where(slot_lane == slot_from + r, patches[:, r : r + 1], 0.0),
            axis=0,
            keepdims=True,
        )
    cell_patch = (lax.broadcasted_iota(jnp.int32, (128, 192), 0) // 32).astype(F32)
    same_patch = cell_patch == slot_row
    low = lax.broadcasted_iota(jnp.int32, (128, 128), 1) < 64
    zero = jnp.zeros((128, 128), BF)

    def cross_pair(g, carry):
        cols = pl.ds(mult(g * 128, 128), 128)
        keys = obs_wide[pl.ds(g, 192, stride=16), :].astype(BF)
        values = obs_wide[pl.ds(g + 8, 192, stride=16), :].astype(BF)
        both = queries[:, cols]
        found = []
        for half in (jnp.where(low, both, zero), jnp.where(low, zero, both)):
            masked = jnp.where(same_patch, dot_t(half, keys) * SCALE, -1e30)
            top = jnp.maximum(jnp.max(masked, axis=-1, keepdims=True), 0.0)
            terms = jnp.where(same_patch, jnp.exp(masked - top), 0.0)
            total = jnp.exp(-top) + jnp.sum(terms, axis=-1, keepdims=True)
            found.append(dot((terms / total).astype(BF), values))
        context[:, cols] = jnp.where(low, found[0], found[1]).astype(BF)
        return carry

    lax.fori_loop(0, 8, cross_pair, 0, unroll=4)

    advance(3, 3)
    advance(4, 2)
    finish_piece(1)

    def cross_out(n, carry):
        cols = pl.ds(mult(n * 256, 256), 256)
        after_cross[:, cols] = (
            tokens[:, cols].astype(F32) + dot(context[...], wc[:, cols])
        ).astype(BF)
        return carry

    lax.fori_loop(0, 4, cross_out, 0)
    normed_axial = normalize(after_cross[...]).astype(BF)
    finish_piece(2)
    columns(6, 256, normed_axial, wkv, axial, 0)

    cell_at, group_at = z, x

    def send_lat(k, carry):
        to = (chip + k) % 32
        push(
            axial.at[pl.ds(mult((to // 4) * 16, 16), 16), pl.ds(mult((to % 4) * 384, 128), 384)],
            lat_own.at[chip],
            bulk_send.at[2],
            bulk_recv.at[2],
            to * 2 + core,
            y,
        )
        return carry

    lax.fori_loop(1, 32, send_lat, 0)
    lat_own[chip] = axial[pl.ds(mult(cell_at * 16, 16), 16), pl.ds(mult(group_at * 384, 128), 384)]

    share_start(0, cot, cot_all)

    finish_piece(3)
    columns(6, 256, normed_axial, wkv, axial, 1536)

    def lon_pair(p, carry):
        both = axial[:, pl.ds(mult(1536 + p * 128, 128), 128)]
        keys = axial[:, pl.ds(mult(2048 + p * 128, 128), 128)]
        values = axial[:, pl.ds(mult(2560 + p * 128, 128), 128)]
        found = []
        for half in (jnp.where(low, both, zero), jnp.where(low, zero, both)):
            scores = dot_t(half, keys) * SCALE
            terms = jnp.exp(scores - jnp.max(scores, axis=-1, keepdims=True))
            weights = (terms / jnp.sum(terms, axis=-1, keepdims=True)).astype(BF)
            found.append(dot(weights, values))
        lon_context[:, pl.ds(mult(p * 128, 128), 128)] = jnp.where(low, found[0], found[1]).astype(
            BF
        )
        return carry

    lat_kv = lat_own.at[:, :, pl.ds(128, 256)]
    await_bytes(lat_own.at[pl.ds(0, 31)], bulk_recv.at[2])
    push(lat_kv, lat_sib, bulk_send.at[3], bulk_recv.at[3], sib, y)
    lax.fori_loop(0, 4, lon_pair, 0, unroll=4)
    q_wide[...] = lat_own[:, :, 0:128].astype(F32).reshape(512, 128)
    k_wide[...] = lat_own[:, :, 128:256].astype(F32).reshape(512, 128)
    v_wide[...] = lat_own[:, :, 256:384].astype(F32).reshape(512, 128)
    await_bytes(lat_sib, bulk_recv.at[3])
    ks_wide[...] = lat_sib[:, :, 0:128].astype(F32).reshape(512, 128)
    vs_wide[...] = lat_sib[:, :, 128:256].astype(F32).reshape(512, 128)
    low_rows = lax.broadcasted_iota(jnp.int32, (32, 128), 1) < 64

    def lat_cell(l, carry):
        rows = pl.ds(l, 32, stride=16)
        q = q_wide[rows, :]
        both = jnp.concatenate(
            [jnp.where(low_rows, q, 0.0), jnp.where(low_rows, 0.0, q)], axis=0
        ).astype(BF)
        keys = jnp.concatenate([k_wide[rows, :], ks_wide[rows, :]], axis=0).astype(BF)
        values = jnp.concatenate([v_wide[rows, :], vs_wide[rows, :]], axis=0).astype(BF)
        scores = dot_t(both, keys) * SCALE
        terms = jnp.exp(scores - jnp.max(scores, axis=-1, keepdims=True))
        weights = (terms / jnp.sum(terms, axis=-1, keepdims=True)).astype(BF)
        found = dot(weights, values)
        o_wide[rows, :] = jnp.where(low_rows, found[:32], found[32:])
        return carry

    lax.fori_loop(0, 16, lat_cell, 0, unroll=8)
    lat_out[...] = o_wide[...].reshape(32, 16, 128).astype(BF)
    home = (pl.ds(mult(cell_at * 16, 16), 16), pl.ds(mult(group_at * 128, 128), 128))

    def send_back(k, carry):
        to = (chip + k) % 32
        push(
            lat_out.at[to],
            lat_context.at[home],
            bulk_send.at[4],
            bulk_recv.at[4],
            to * 2 + core,
            y,
        )
        return carry

    lax.fori_loop(1, 32, send_back, 0)
    lat_context[home] = lat_out[chip]
    finish_piece(4)

    def axial_lon(n, carry):
        cols = pl.ds(mult(n * 256, 256), 256)
        axial_sum[:, cols] = after_cross[:, cols].astype(F32) + dot(
            lon_context[...], wa[pl.ds(512, 512), cols]
        )
        return carry

    def axial_lat(n, carry):
        cols = pl.ds(mult(n * 256, 256), 256)
        context[:, cols] = (
            axial_sum[:, cols] + dot(lat_context[...], wa[pl.ds(0, 512), cols])
        ).astype(BF)
        return carry

    lax.fori_loop(0, 4, axial_lon, 0)
    await_bytes(lat_out.at[pl.ds(0, 31)], bulk_recv.at[4])
    lax.fori_loop(0, 4, axial_lat, 0)
    mine = pl.ds(mult(part * 128, 128), 128)
    normed_all[mine, :] = normalize(context[...]).astype(BF)
    share_start(1, normed_all.at[mine, :], normed_all)
    for k in range(1, 4):
        share_forward(0, cot_all, k)
    await_bytes(cot_all.at[pl.ds(0, 128), :], gather_recv.at[0, 0])
    for k in range(1, 4):
        await_bytes(from_chip(cot_all, k, 1), share_recv.at[0, k])
    wi_copy.wait()
    wo_copy.wait()
    await_bytes(normed_all.at[pl.ds(0, 128), :], gather_recv.at[1, 0])

    def ff_chip(i, carry):
        k = jnp.where(i == 2, 3, jnp.where(i == 3, 2, i))

        @pl.when(i == 1)
        def _():
            share_forward(1, normed_all, 1)
            share_forward(1, normed_all, 3)

        @pl.when(i == 2)
        def _():
            share_forward(1, normed_all, 2)

        @pl.when(i > 0)
        def _():
            await_bytes(normed_all.at[pl.ds(0, 128), :], share_recv.at[1, k])

        rows = pl.ds(mult(((x - k + 4) % 4) * 256, 256), 256)
        pre_act = dot(normed_all[rows, :], wi[...])
        hidden_grad = dot_t(cot_all[rows, :], wo[...])
        cdf = 0.5 * (1.0 + lax.erf(pre_act * ROOT_HALF))
        slope = cdf + pre_act * jnp.exp(-0.5 * pre_act * pre_act) * INV_ROOT_TWO_PI
        hidden_t[:, rows] = (pre_act * cdf).astype(BF).T
        pre_grad_t[:, rows] = (hidden_grad * slope).astype(BF).T
        return carry

    lax.fori_loop(0, 4, ff_chip, 0)

    def fold(source, received, at):
        for k in range(1, 4):
            push(
                source.at[(y + k) % 4],
                received.at[y],
                bulk_send.at[at],
                bulk_recv.at[at],
                sp,
                (y + k) % 4,
            )
        received[y] = source[y]

    def pass_on(received, middle, ends, at, to):
        await_bytes(received.at[pl.ds(0, 3)], bulk_recv.at[at])

        def total(n, carry):
            found = received[0, n].astype(F32)
            for k in range(1, 4):
                found += received[k, n].astype(F32)
            middle[n] = found.astype(BF)
            return carry

        lax.fori_loop(0, 8, total, 0)

        def one(k, carry):
            push(
                middle.at[(z + k) % 8],
                ends.at[z],
                bulk_send.at[to],
                bulk_recv.at[to],
                ((z + k) % 8) * 8 + part,
                y,
            )
            return carry

        lax.fori_loop(1, 8, one, 0)
        ends[z] = middle[z]

    def end_sum(ends, at):
        await_bytes(ends.at[pl.ds(0, 7)], bulk_recv.at[at])
        found = ends[0].astype(F32)
        for n in range(1, 8):
            found += ends[n].astype(F32)
        return found

    def grad_out_cols(n, carry):
        cols = pl.ds(mult(n * 256, 256), 256)
        grad = dot(hidden_t[...], cot_all[:, cols]).astype(BF)
        inner = pl.ds(mult((n % 2) * 256, 256), 256)
        for at in range(16):
            gout_send[(at % 2) * 2 + n // 2, at // 2, :, inner] = grad[at * 16 : at * 16 + 16]
        return carry

    lax.fori_loop(0, 4, grad_out_cols, 0)
    fold(gout_send, gout_recv, 6)

    down = lax.broadcasted_iota(jnp.int32, (128, 128), 0)
    across = lax.broadcasted_iota(jnp.int32, (128, 128), 1)
    turn = (across == ((down % 32) // 4) * 16 + (down // 32) * 4 + down % 4).astype(F32).astype(BF)

    def grad_cols(n, carry):
        cols = pl.ds(mult(n * 256, 256), 256)
        grad = dot(pre_grad_t[...], normed_all[:, cols]).astype(BF)
        for half in range(2):
            turned = dot_t(turn, grad[:, half * 128 : half * 128 + 128]).astype(BF)
            for m in range(4):
                gin_send[m, n * 2 + half] = turned[m * 32 : m * 32 + 32]
        return carry

    lax.fori_loop(0, 4, grad_cols, 0)

    fold(gin_send, gin_recv, 5)
    pass_on(gout_recv, gout_mid, gout_ends, 6, 8)
    pass_on(gin_recv, gin_mid, gin_ends, 5, 7)
    sum_out = end_sum(gout_ends, 8)
    sum_in = end_sum(gin_ends, 7)
    for n in range(8):
        fin_in_send[n] = sum_in[n * 4 : n * 4 + 4]
    for n in range(2):
        fin_out_send[n] = sum_out[n * 8 : n * 8 + 8]

    fin_in_recv[part] = fin_in_send[part]
    for k in range(1, 8):
        n = (part + k) % 8
        push(
            fin_in_send.at[n], fin_in_recv.at[part], last_send.at[0], last_in.at[0], z * 8 + n, y
        )
    to_sp = part * 8 + z
    odd = y % 2
    push(
        fin_out_send.at[1 - odd],
        fin_out_recv.at[odd],
        last_send.at[1],
        last_out.at[0],
        to_sp,
        y + 1 - 2 * odd,
    )

    @pl.when(part == z)
    def _():
        fin_out_recv[odd] = fin_out_send[odd]

    @pl.when(part != z)
    def _():
        push(
            fin_out_send.at[odd],
            fin_out_recv.at[odd],
            last_send.at[2],
            last_out.at[1],
            to_sp,
            y,
        )
        await_bytes(fin_out_recv.at[0], last_out.at[1])
        await_bytes(fin_out_send.at[0], last_send.at[2])

    await_bytes(fin_out_recv.at[0], last_out.at[0])
    for n in range(2):
        out_out[:, n * 512 : (n + 1) * 512] = fin_out_recv[n]
    await_bytes(fin_in_recv.at[pl.ds(0, 7)], last_in.at[0])
    for n in range(8):
        out_in[:, n * 256 : (n + 1) * 256] = fin_in_recv[n]

    for i in range(5):
        drain_piece(i)
    share_drain(0, cot_all)
    share_drain(1, normed_all)
    await_bytes(obs_recv.at[pl.ds(0, 189)], bulk_send.at[0])
    await_bytes(patch_recv.at[pl.ds(0, 63)], bulk_send.at[1])
    await_bytes(lat_own.at[pl.ds(0, 31)], bulk_send.at[2])
    await_bytes(lat_sib, bulk_send.at[3])
    await_bytes(lat_out.at[pl.ds(0, 31)], bulk_send.at[4])
    await_bytes(gin_recv.at[pl.ds(0, 3)], bulk_send.at[5])
    await_bytes(gout_recv.at[pl.ds(0, 3)], bulk_send.at[6])
    await_bytes(gin_ends.at[pl.ds(0, 7)], bulk_send.at[7])
    await_bytes(gout_ends.at[pl.ds(0, 7)], bulk_send.at[8])
    await_bytes(fin_in_send.at[pl.ds(0, 7)], last_send.at[0])
    await_bytes(fin_out_send.at[0], last_send.at[1])


def scratch():
    vmem = pltpu.VMEM
    dma = pltpu.SemaphoreType.DMA
    return [
        vmem((128, 1024), BF),
        vmem((128, 1024), BF),
        vmem((96, 2048), BF),
        vmem((1, 96), jnp.int32),
        vmem((1, 96), jnp.int32),
        vmem((1536, 128), F32),
        vmem((96, 16, 128), BF),
        vmem((1, 256), jnp.int32),
        pltpu.SMEM((1, 256), jnp.int32),
        vmem((64, 1, 128), F32),
        vmem((1024, 1024), BF),
        vmem((1024, 1024), BF),
        vmem((1024, 3072), BF),
        vmem((1024, 1024), BF),
        vmem((1024, 256), BF),
        vmem((256, 1024), BF),
        vmem((192, 16, 128), BF),
        vmem((192, 16, 128), BF),
        vmem((3072, 128), F32),
        vmem((64, 1, 128), F32),
        vmem((128, 1024), BF),
        vmem((128, 1024), BF),
        vmem((128, 1024), BF),
        vmem((128, 3072), BF),
        vmem((32, 16, 384), BF),
        vmem((32, 16, 256), BF),
        vmem((512, 128), F32),
        vmem((512, 128), F32),
        vmem((512, 128), F32),
        vmem((512, 128), F32),
        vmem((512, 128), F32),
        vmem((512, 128), F32),
        vmem((32, 16, 128), BF),
        vmem((128, 512), BF),
        vmem((128, 512), BF),
        vmem((128, 1024), F32),
        vmem((1024, 1024), BF),
        vmem((1024, 1024), BF),
        vmem((256, 1024), BF),
        vmem((256, 1024), BF),
        vmem((4, 8, 32, 256), BF),
        vmem((4, 8, 16, 512), BF),
        vmem((4, 8, 32, 256), BF),
        vmem((4, 8, 16, 512), BF),
        vmem((8, 32, 256), BF),
        vmem((8, 16, 512), BF),
        vmem((8, 32, 256), BF),
        vmem((8, 16, 512), BF),
        vmem((8, 4, 256), F32),
        vmem((8, 4, 256), F32),
        vmem((2, 8, 512), F32),
        vmem((2, 8, 512), F32),
        dma((13,)),
        dma((5, 4)),
        dma((5, 4)),
        dma((2,)),
        dma((2, 4)),
        dma((2,)),
        dma((2, 4)),
        dma((9,)),
        dma((9,)),
        dma((3,)),
        dma((1,)),
        dma((2,)),
        pltpu.SemaphoreType.REGULAR,
    ]


def local(
    grid_tokens,
    cotangent,
    obs_pairs,
    obs_route,
    obs_patch,
    w_query,
    w_cross_out,
    w_qkv,
    w_axial_out,
    w_in,
    w_out,
):
    vmem = pl.BlockSpec(memory_space=pltpu.VMEM)
    hbm = pl.BlockSpec(memory_space=pltpu.HBM)
    return pl.pallas_call(
        kernel,
        out_shape=(
            jax.ShapeDtypeStruct((4, 2048), F32),
            jax.ShapeDtypeStruct((8, 1024), F32),
        ),
        in_specs=[hbm] * 11,
        out_specs=(vmem, vmem),
        scratch_shapes=scratch(),
        compiler_params=pltpu.CompilerParams(
            collective_id=0, has_side_effects=True, vmem_limit_bytes=62 * 1024 * 1024
        ),
    )(
        grid_tokens.reshape(128, 1024),
        cotangent.reshape(128, 1024),
        obs_pairs.reshape(96, 2048),
        obs_route.reshape(1, 96),
        obs_patch.reshape(1, 96),
        w_query,
        w_cross_out,
        w_qkv,
        w_axial_out,
        w_in,
        w_out,
    )


def solution(mesh):
    return jax.shard_map(
        local,
        mesh=mesh,
        in_specs=(
            P("dp", "sp", None, None),
            P("dp", "sp", None, None),
            P("dp", "sp", None, None),
            P("dp", "sp", None, None),
            P("dp", "sp", None),
            P("dp", None),
            P("dp", None),
            P("dp", None),
            P("dp", None),
            P(),
            P(),
        ),
        out_specs=(P(("sp", "dp"), None), P(("sp", "dp"), None)),
        check_vma=False,
    )
```

```python
import jax
import jax.numpy as jnp
from jax import lax
from jax.experimental import pallas as pl
from jax.experimental.pallas import tpu as pltpu
from jax.sharding import PartitionSpec as P

BF = jnp.bfloat16
F32 = jnp.float32
EPS = 1e-06
ROOT_HALF = 0.7071067811865476
INV_ROOT_TWO_PI = 0.3989422804014327
SCALE = 0.125


def normalize(values):
    values = values.astype(F32)
    return values * lax.rsqrt(jnp.mean(values * values, axis=-1, keepdims=True) + EPS)


def dot(a, b):
    return jnp.dot(a, b, preferred_element_type=F32)


def dot_t(a, b):
    return lax.dot_general(a, b, (((1,), (1,)), ((), ())), preferred_element_type=F32)


def mult(value, by):
    return pl.multiple_of(value, by)


def push(src, dst, send, recv, sp, dp):
    pltpu.make_async_remote_copy(
        src_ref=src,
        dst_ref=dst,
        send_sem=send,
        recv_sem=recv,
        device_id={"sp": sp, "dp": dp},
        device_id_type=pl.DeviceIdType.MESH,
    ).start()


def await_bytes(ref, sem):
    pltpu.make_async_copy(ref, ref, sem).wait()


def kernel(
    tokens_hbm,
    cot_hbm,
    pairs_hbm,
    route_hbm,
    patch_hbm,
    wq_hbm,
    wc_hbm,
    wkv_hbm,
    wa_hbm,
    wi_hbm,
    wo_hbm,
    out_in,
    out_out,
    tokens,
    cot,
    pairs,
    route,
    patch,
    pairs_wide,
    pairs_tiles,
    index_row,
    src_index,
    slot_patch,
    wq,
    wc,
    wkv,
    wa,
    wi,
    wo,
    obs_send,
    obs_recv,
    obs_wide,
    patch_recv,
    queries,
    context,
    after_cross,
    axial,
    lat_own,
    lat_sib,
    q_wide,
    k_wide,
    v_wide,
    ks_wide,
    vs_wide,
    o_wide,
    lat_out,
    lat_context,
    lon_context,
    axial_sum,
    normed_all,
    cot_all,
    hidden_t,
    pre_grad_t,
    gin_send,
    gout_send,
    gin_recv,
    gout_recv,
    gin_mid,
    gout_mid,
    gin_ends,
    gout_ends,
    fin_in_send,
    fin_in_recv,
    fin_out_send,
    fin_out_recv,
    local_sem,
    w_send,
    w_recv,
    gather_send,
    gather_recv,
    share_send,
    share_recv,
    bulk_send,
    bulk_recv,
    last_send,
    last_in,
    last_out,
    entered,
):
    sp = lax.axis_index("sp")
    y = lax.axis_index("dp")
    core = sp % 2
    sib = sp + 1 - 2 * core
    chip = sp // 2
    x = chip % 4
    z = chip // 4
    part = sp % 8

    barrier = pltpu.get_barrier_semaphore()

    def greet(to_sp, to_dp):
        pl.semaphore_signal(
            barrier,
            inc=1,
            device_id={"sp": to_sp, "dp": to_dp},
            device_id_type=pl.DeviceIdType.MESH,
        )

    def greet_line(k, carry):
        greet(((z + k) % 8) * 8 + part, y)
        greet(z * 8 + (part + k) % 8, y)
        return carry

    lax.fori_loop(1, 8, greet_line, 0)
    for k in range(1, 4):
        greet(sp, (y + k) % 4)
    greet(part * 8 + z, y + 1 - 2 * (y % 2))

    loads = [
        pltpu.make_async_copy(source, target, local_sem.at[7 + i])
        for i, (source, target) in enumerate(
            (
                (route_hbm, route),
                (patch_hbm, patch),
                (pairs_hbm, pairs),
                (tokens_hbm, tokens),
                (cot_hbm, cot),
            )
        )
    ]
    for load in loads:
        load.start()

    pieces = (
        (wq_hbm, wq, 0, 1024, "x"),
        (wc_hbm, wc, 0, 1024, "x"),
        (wkv_hbm, wkv, 0, 1536, "xz"),
        (wkv_hbm, wkv, 1536, 1536, "zx"),
        (wa_hbm, wa, 0, 1024, "x"),
    )
    place_of = {"x": (x + core) % 2, "z": (z + core) % 2}
    mate_of = {
        "x": z * 8 + ((x + 5 - 2 * place_of["x"]) % 4) * 2 + core,
        "z": ((z + 9 - 2 * place_of["z"]) % 8) * 8 + x * 2 + core,
    }

    def spans(plan):
        rows = 128 >> len(plan)
        first = core * 128
        for n, axis in enumerate(plan):
            first += place_of[axis] * (rows << n)
        made = [(first, rows, None)]
        for n, axis in enumerate(plan):
            made.append((first, rows << n, mate_of[axis]))
            first -= place_of[axis] * (rows << n)
        made.append((core * 128, 128, sib))
        return made

    stages = [spans(piece[4]) for piece in pieces]

    def landing(i, stage):
        full, col, width = pieces[i][1:4]
        return full.at[pl.ds(0, 3 * stages[i][stage][1]), pl.ds(col, width)]

    def start_piece(i):
        hbm, full, col, width, _ = pieces[i]
        first, rows, _ = stages[i][0]
        for k in range(1, 4):
            push(
                hbm.at[pl.ds(mult(first, 32), rows), pl.ds(col, width)],
                full.at[pl.ds(mult(y * 256 + first, 32), rows), pl.ds(col, width)],
                w_send.at[i, 0],
                w_recv.at[i, 0],
                sp,
                (y + k) % 4,
            )

    def own_piece(i):
        hbm, full, col, width, _ = pieces[i]
        return pltpu.make_async_copy(
            hbm.at[:, pl.ds(col, width)],
            full.at[pl.ds(mult(y * 256, 256), 256), pl.ds(col, width)],
            local_sem.at[i],
        )

    def advance(i, stage):
        full, col, width = pieces[i][1:4]
        await_bytes(landing(i, stage - 1), w_recv.at[i, stage - 1])
        first, rows, mate = stages[i][stage]
        for k in range(1, 4):
            part_rows = full.at[
                pl.ds(mult(((y + k) % 4) * 256 + first, 32), rows), pl.ds(col, width)
            ]
            push(part_rows, part_rows, w_send.at[i, stage], w_recv.at[i, stage], mate, y)

    def finish_piece(i):
        last = len(stages[i]) - 1
        await_bytes(landing(i, last), w_recv.at[i, last])
        own_piece(i).wait()

    def drain_piece(i):
        for stage in range(len(stages[i])):
            await_bytes(landing(i, stage), w_send.at[i, stage])

    for i in range(5):
        own_piece(i).start()
    wi_copy = pltpu.make_async_copy(
        wi_hbm.at[:, pl.ds(mult(part * 256, 256), 256)], wi, local_sem.at[5]
    )
    wo_copy = pltpu.make_async_copy(
        wo_hbm.at[pl.ds(mult(part * 256, 256), 256), :], wo, local_sem.at[6]
    )
    wi_copy.start()
    wo_copy.start()

    loads[0].wait()
    loads[1].wait()
    line = lax.broadcasted_iota(jnp.int32, (96, 96), 0)
    lane = lax.broadcasted_iota(jnp.int32, (96, 96), 1)

    def upright(row):
        return jnp.sum(jnp.where(line == lane, row, 0), axis=1, keepdims=True)

    row_across = route[...]
    row_down = upright(row_across)
    patch_across = patch[...] + 1
    same = row_across == row_down
    rank_across = jnp.sum(jnp.where(same & (line < lane), 1, 0), axis=0, keepdims=True)
    rank_down = jnp.sum(jnp.where(same & (lane < line), 1, 0), axis=1, keepdims=True)
    slot_across = row_across * 3 + rank_across
    slot_down = row_down * 3 + rank_down
    hit = slot_down == lax.broadcasted_iota(jnp.int32, (96, 256), 1)
    index_row[...] = jnp.sum(
        jnp.where(hit, lax.broadcasted_iota(jnp.int32, (96, 256), 0), 0), axis=0, keepdims=True
    )
    index_copy = pltpu.make_async_copy(index_row, src_index, local_sem.at[12])
    index_copy.start()
    lanes = lax.broadcasted_iota(jnp.int32, (64, 128), 1)
    found_patch = jnp.zeros((64, 128), jnp.int32)
    for r in range(3):
        mine = slot_across == lax.broadcasted_iota(jnp.int32, (64, 96), 0) * 3 + r
        value = jnp.sum(jnp.where(mine, patch_across, 0), axis=1, keepdims=True) - 1
        found_patch = jnp.where(lanes == r, value, found_patch)
    slot_patch[...] = found_patch.astype(F32).reshape(64, 1, 128)

    pl.semaphore_wait(barrier, 18)

    def greet_again(k, carry):
        pl.semaphore_signal(
            entered,
            inc=1,
            device_id={"sp": z * 8 + (part + k) % 8, "dp": y},
            device_id_type=pl.DeviceIdType.MESH,
        )
        return carry

    lax.fori_loop(1, 8, greet_again, 0)

    loads[2].wait()
    for n in range(16):
        pairs_wide[pl.ds(n, 96, stride=16), :] = pairs[:, n * 128 : (n + 1) * 128].astype(F32)
    pairs_tiles[...] = pairs_wide[...].reshape(96, 16, 128).astype(BF)
    index_copy.wait()

    def place(s, carry):
        obs_send[s] = pairs_tiles[src_index[0, s]]
        return carry

    lax.fori_loop(0, 192, place, 0, unroll=8)
    pl.semaphore_wait(entered, 7)
    start_piece(0)

    def send_obs(k, carry):
        to = (sp + k) % 64
        push(
            obs_send.at[pl.ds(to * 3, 3)],
            obs_recv.at[pl.ds(sp * 3, 3)],
            bulk_send.at[0],
            bulk_recv.at[0],
            to,
            y,
        )
        push(slot_patch.at[to], patch_recv.at[sp], bulk_send.at[1], bulk_recv.at[1], to, y)
        return carry

    lax.fori_loop(1, 64, send_obs, 0)
    start_piece(1)
    start_piece(2)
    obs_recv[pl.ds(sp * 3, 3)] = obs_send[pl.ds(sp * 3, 3)]
    patch_recv[sp] = slot_patch[sp]

    def share_start(j, source, full):
        rows = full.at[pl.ds(mult(part * 128, 128), 128), :]
        push(source, rows, gather_send.at[j], gather_recv.at[j, 0], sib, y)
        for k in range(1, 4):
            push(
                source,
                rows,
                gather_send.at[j],
                gather_recv.at[j, k],
                z * 8 + ((x + k) % 4) * 2 + core,
                y,
            )

    def from_chip(full, k, cores):
        first = ((x - k + 4) % 4) * 256 + (core * 128 if cores == 1 else 0)
        return full.at[pl.ds(mult(first, 128), 128 * cores), :]

    def share_forward(j, full, k):
        rows = from_chip(full, k, 1)
        await_bytes(rows, gather_recv.at[j, k])
        push(rows, rows, share_send.at[j], share_recv.at[j, k], sib, y)

    def share_drain(j, full):
        await_bytes(full.at[pl.ds(0, 512), :], gather_send.at[j])
        await_bytes(full.at[pl.ds(0, 384), :], share_send.at[j])

    loads[3].wait()
    loads[4].wait()
    cot_all[pl.ds(mult(part * 128, 128), 128), :] = cot[...]

    normed = normalize(tokens[...]).astype(BF)
    advance(0, 1)
    advance(1, 1)
    advance(0, 2)
    finish_piece(0)

    def columns(count, width, source, weight, target, offset):
        def step(n, carry):
            cols = pl.ds(mult(offset + n * width, width), width)
            target[:, cols] = dot(source, weight[:, cols]).astype(BF)
            return carry

        lax.fori_loop(0, count, step, 0)

    columns(4, 256, normed, wq, queries, 0)
    advance(2, 1)
    start_piece(3)
    advance(1, 2)
    advance(2, 2)

    await_bytes(obs_recv.at[pl.ds(0, 189)], bulk_recv.at[0])
    await_bytes(patch_recv.at[pl.ds(0, 63)], bulk_recv.at[1])
    obs_wide[...] = obs_recv[...].astype(F32).reshape(3072, 128)
    patches = patch_recv[...].reshape(64, 128)
    slot_lane = lax.broadcasted_iota(jnp.int32, (64, 192), 1)
    slot_from = lax.broadcasted_iota(jnp.int32, (64, 192), 0) * 3
    slot_row = jnp.zeros((1, 192), F32)
    for r in range(3):
        slot_row += jnp.sum(
            jnp.where(slot_lane == slot_from + r, patches[:, r : r + 1], 0.0),
            axis=0,
            keepdims=True,
        )
    cell_patch = (lax.broadcasted_iota(jnp.int32, (128, 192), 0) // 32).astype(F32)
    same_patch = cell_patch == slot_row
    low = lax.broadcasted_iota(jnp.int32, (128, 128), 1) < 64
    zero = jnp.zeros((128, 128), BF)

    def cross_pair(g, carry):
        cols = pl.ds(mult(g * 128, 128), 128)
        keys = obs_wide[pl.ds(g, 192, stride=16), :].astype(BF)
        values = obs_wide[pl.ds(g + 8, 192, stride=16), :].astype(BF)
        both = queries[:, cols]
        found = []
        for half in (jnp.where(low, both, zero), jnp.where(low, zero, both)):
            masked = jnp.where(same_patch, dot_t(half, keys) * SCALE, -1e30)
            top = jnp.maximum(jnp.max(masked, axis=-1, keepdims=True), 0.0)
            terms = jnp.where(same_patch, jnp.exp(masked - top), 0.0)
            total = jnp.exp(-top) + jnp.sum(terms, axis=-1, keepdims=True)
            found.append(dot((terms / total).astype(BF), values))
        context[:, cols] = jnp.where(low, found[0], found[1]).astype(BF)
        return carry

    def cross_four(i, carry):
        @pl.when(i == 1)
        def _():
            advance(2, 3)
            advance(3, 1)
            start_piece(4)

        for g in range(4):
            cross_pair(i * 4 + g, 0)
        return carry

    lax.fori_loop(0, 2, cross_four, 0)

    finish_piece(1)

    def cross_out(n, carry):
        cols = pl.ds(mult(n * 256, 256), 256)
        after_cross[:, cols] = (
            tokens[:, cols].astype(F32) + dot(context[...], wc[:, cols])
        ).astype(BF)
        return carry

    lax.fori_loop(0, 4, cross_out, 0)
    advance(3, 2)
    normed_axial = normalize(after_cross[...]).astype(BF)
    finish_piece(2)
    columns(6, 256, normed_axial, wkv, axial, 0)

    cell_at, group_at = z, x

    def send_lat(k, carry):
        to = (chip + k) % 32
        push(
            axial.at[pl.ds(mult((to // 4) * 16, 16), 16), pl.ds(mult((to % 4) * 384, 128), 384)],
            lat_own.at[chip],
            bulk_send.at[2],
            bulk_recv.at[2],
            to * 2 + core,
            y,
        )
        return carry

    lax.fori_loop(1, 32, send_lat, 0)
    lat_own[chip] = axial[pl.ds(mult(cell_at * 16, 16), 16), pl.ds(mult(group_at * 384, 128), 384)]

    share_start(0, cot, cot_all)

    advance(4, 1)
    advance(3, 3)
    finish_piece(3)
    columns(6, 256, normed_axial, wkv, axial, 1536)

    def lon_pair(p, carry):
        both = axial[:, pl.ds(mult(1536 + p * 128, 128), 128)]
        keys = axial[:, pl.ds(mult(2048 + p * 128, 128), 128)]
        values = axial[:, pl.ds(mult(2560 + p * 128, 128), 128)]
        found = []
        for half in (jnp.where(low, both, zero), jnp.where(low, zero, both)):
            scores = dot_t(half, keys) * SCALE
            terms = jnp.exp(scores - jnp.max(scores, axis=-1, keepdims=True))
            weights = (terms / jnp.sum(terms, axis=-1, keepdims=True)).astype(BF)
            found.append(dot(weights, values))
        lon_context[:, pl.ds(mult(p * 128, 128), 128)] = jnp.where(low, found[0], found[1]).astype(
            BF
        )
        return carry

    lat_kv = lat_own.at[:, :, pl.ds(128, 256)]
    await_bytes(lat_own.at[pl.ds(0, 31)], bulk_recv.at[2])
    push(lat_kv, lat_sib, bulk_send.at[3], bulk_recv.at[3], sib, y)
    lax.fori_loop(0, 4, lon_pair, 0, unroll=4)
    advance(4, 2)
    q_wide[...] = lat_own[:, :, 0:128].astype(F32).reshape(512, 128)
    k_wide[...] = lat_own[:, :, 128:256].astype(F32).reshape(512, 128)
    v_wide[...] = lat_own[:, :, 256:384].astype(F32).reshape(512, 128)
    await_bytes(lat_sib, bulk_recv.at[3])
    ks_wide[...] = lat_sib[:, :, 0:128].astype(F32).reshape(512, 128)
    vs_wide[...] = lat_sib[:, :, 128:256].astype(F32).reshape(512, 128)
    low_rows = lax.broadcasted_iota(jnp.int32, (32, 128), 1) < 64

    def lat_cell(l, carry):
        rows = pl.ds(l, 32, stride=16)
        q = q_wide[rows, :]
        both = jnp.concatenate(
            [jnp.where(low_rows, q, 0.0), jnp.where(low_rows, 0.0, q)], axis=0
        ).astype(BF)
        keys = jnp.concatenate([k_wide[rows, :], ks_wide[rows, :]], axis=0).astype(BF)
        values = jnp.concatenate([v_wide[rows, :], vs_wide[rows, :]], axis=0).astype(BF)
        scores = dot_t(both, keys) * SCALE
        terms = jnp.exp(scores - jnp.max(scores, axis=-1, keepdims=True))
        weights = (terms / jnp.sum(terms, axis=-1, keepdims=True)).astype(BF)
        found = dot(weights, values)
        o_wide[rows, :] = jnp.where(low_rows, found[:32], found[32:])
        return carry

    lax.fori_loop(0, 16, lat_cell, 0, unroll=8)
    lat_out[...] = o_wide[...].reshape(32, 16, 128).astype(BF)
    home = (pl.ds(mult(cell_at * 16, 16), 16), pl.ds(mult(group_at * 128, 128), 128))

    def send_back(k, carry):
        to = (chip + k) % 32
        push(
            lat_out.at[to],
            lat_context.at[home],
            bulk_send.at[4],
            bulk_recv.at[4],
            to * 2 + core,
            y,
        )
        return carry

    lax.fori_loop(1, 32, send_back, 0)
    lat_context[home] = lat_out[chip]
    finish_piece(4)

    def axial_lon(n, carry):
        cols = pl.ds(mult(n * 256, 256), 256)
        axial_sum[:, cols] = after_cross[:, cols].astype(F32) + dot(
            lon_context[...], wa[pl.ds(512, 512), cols]
        )
        return carry

    def axial_lat(n, carry):
        cols = pl.ds(mult(n * 256, 256), 256)
        context[:, cols] = (
            axial_sum[:, cols] + dot(lat_context[...], wa[pl.ds(0, 512), cols])
        ).astype(BF)
        return carry

    lax.fori_loop(0, 4, axial_lon, 0)
    await_bytes(lat_out.at[pl.ds(0, 31)], bulk_recv.at[4])
    lax.fori_loop(0, 4, axial_lat, 0)
    mine = pl.ds(mult(part * 128, 128), 128)
    normed_all[mine, :] = normalize(context[...]).astype(BF)
    share_start(1, normed_all.at[mine, :], normed_all)
    for k in range(1, 4):
        share_forward(0, cot_all, k)
    await_bytes(cot_all.at[pl.ds(0, 128), :], gather_recv.at[0, 0])
    for k in range(1, 4):
        await_bytes(from_chip(cot_all, k, 1), share_recv.at[0, k])
    wi_copy.wait()
    wo_copy.wait()
    await_bytes(normed_all.at[pl.ds(0, 128), :], gather_recv.at[1, 0])

    def ff_chip(i, carry):
        k = jnp.where(i == 2, 3, jnp.where(i == 3, 2, i))

        @pl.when(i == 1)
        def _():
            share_forward(1, normed_all, 1)
            share_forward(1, normed_all, 3)

        @pl.when(i == 2)
        def _():
            share_forward(1, normed_all, 2)

        @pl.when(i > 0)
        def _():
            await_bytes(normed_all.at[pl.ds(0, 128), :], share_recv.at[1, k])

        rows = pl.ds(mult(((x - k + 4) % 4) * 256, 256), 256)
        pre_act = dot(normed_all[rows, :], wi[...])
        hidden_grad = dot_t(cot_all[rows, :], wo[...])
        cdf = 0.5 * (1.0 + lax.erf(pre_act * ROOT_HALF))
        slope = cdf + pre_act * jnp.exp(-0.5 * pre_act * pre_act) * INV_ROOT_TWO_PI
        hidden_t[:, rows] = (pre_act * cdf).astype(BF).T
        pre_grad_t[:, rows] = (hidden_grad * slope).astype(BF).T
        return carry

    lax.fori_loop(0, 4, ff_chip, 0)

    def fold(source, received, at):
        for k in range(1, 4):
            push(
                source.at[(y + k) % 4],
                received.at[y],
                bulk_send.at[at],
                bulk_recv.at[at],
                sp,
                (y + k) % 4,
            )
        received[y] = source[y]

    def pass_on(received, middle, ends, at, to):
        await_bytes(received.at[pl.ds(0, 3)], bulk_recv.at[at])

        def total(n, carry):
            found = received[0, n].astype(F32)
            for k in range(1, 4):
                found += received[k, n].astype(F32)
            middle[n] = found.astype(BF)
            return carry

        lax.fori_loop(0, 8, total, 0)

        def one(k, carry):
            push(
                middle.at[(z + k) % 8],
                ends.at[z],
                bulk_send.at[to],
                bulk_recv.at[to],
                ((z + k) % 8) * 8 + part,
                y,
            )
            return carry

        lax.fori_loop(1, 8, one, 0)
        ends[z] = middle[z]

    def end_sum(ends, at):
        await_bytes(ends.at[pl.ds(0, 7)], bulk_recv.at[at])
        found = ends[0].astype(F32)
        for n in range(1, 8):
            found += ends[n].astype(F32)
        return found

    def grad_out_cols(n, carry):
        cols = pl.ds(mult(n * 256, 256), 256)
        grad = dot(hidden_t[...], cot_all[:, cols]).astype(BF)
        inner = pl.ds(mult((n % 2) * 256, 256), 256)
        for at in range(16):
            gout_send[(at % 2) * 2 + n // 2, at // 2, :, inner] = grad[at * 16 : at * 16 + 16]
        return carry

    lax.fori_loop(0, 4, grad_out_cols, 0)
    fold(gout_send, gout_recv, 6)

    down = lax.broadcasted_iota(jnp.int32, (128, 128), 0)
    across = lax.broadcasted_iota(jnp.int32, (128, 128), 1)
    turn = (across == ((down % 32) // 4) * 16 + (down // 32) * 4 + down % 4).astype(F32).astype(BF)

    def grad_cols(n, carry):
        cols = pl.ds(mult(n * 256, 256), 256)
        grad = dot(pre_grad_t[...], normed_all[:, cols]).astype(BF)
        for half in range(2):
            turned = dot_t(turn, grad[:, half * 128 : half * 128 + 128]).astype(BF)
            for m in range(4):
                gin_send[m, n * 2 + half] = turned[m * 32 : m * 32 + 32]
        return carry

    lax.fori_loop(0, 4, grad_cols, 0)

    fold(gin_send, gin_recv, 5)
    pass_on(gout_recv, gout_mid, gout_ends, 6, 8)
    pass_on(gin_recv, gin_mid, gin_ends, 5, 7)
    sum_out = end_sum(gout_ends, 8)
    sum_in = end_sum(gin_ends, 7)
    for n in range(8):
        fin_in_send[n] = sum_in[n * 4 : n * 4 + 4]
    for n in range(2):
        fin_out_send[n] = sum_out[n * 8 : n * 8 + 8]

    fin_in_recv[part] = fin_in_send[part]
    for k in range(1, 8):
        n = (part + k) % 8
        push(
            fin_in_send.at[n], fin_in_recv.at[part], last_send.at[0], last_in.at[0], z * 8 + n, y
        )
    to_sp = part * 8 + z
    odd = y % 2
    push(
        fin_out_send.at[1 - odd],
        fin_out_recv.at[odd],
        last_send.at[1],
        last_out.at[0],
        to_sp,
        y + 1 - 2 * odd,
    )

    @pl.when(part == z)
    def _():
        fin_out_recv[odd] = fin_out_send[odd]

    @pl.when(part != z)
    def _():
        push(
            fin_out_send.at[odd],
            fin_out_recv.at[odd],
            last_send.at[2],
            last_out.at[1],
            to_sp,
            y,
        )
        await_bytes(fin_out_recv.at[0], last_out.at[1])
        await_bytes(fin_out_send.at[0], last_send.at[2])

    await_bytes(fin_out_recv.at[0], last_out.at[0])
    for n in range(2):
        out_out[:, n * 512 : (n + 1) * 512] = fin_out_recv[n]
    await_bytes(fin_in_recv.at[pl.ds(0, 7)], last_in.at[0])
    for n in range(8):
        out_in[:, n * 256 : (n + 1) * 256] = fin_in_recv[n]

    for i in range(5):
        drain_piece(i)
    share_drain(0, cot_all)
    share_drain(1, normed_all)
    await_bytes(obs_recv.at[pl.ds(0, 189)], bulk_send.at[0])
    await_bytes(patch_recv.at[pl.ds(0, 63)], bulk_send.at[1])
    await_bytes(lat_own.at[pl.ds(0, 31)], bulk_send.at[2])
    await_bytes(lat_sib, bulk_send.at[3])
    await_bytes(lat_out.at[pl.ds(0, 31)], bulk_send.at[4])
    await_bytes(gin_recv.at[pl.ds(0, 3)], bulk_send.at[5])
    await_bytes(gout_recv.at[pl.ds(0, 3)], bulk_send.at[6])
    await_bytes(gin_ends.at[pl.ds(0, 7)], bulk_send.at[7])
    await_bytes(gout_ends.at[pl.ds(0, 7)], bulk_send.at[8])
    await_bytes(fin_in_send.at[pl.ds(0, 7)], last_send.at[0])
    await_bytes(fin_out_send.at[0], last_send.at[1])


def scratch():
    vmem = pltpu.VMEM
    dma = pltpu.SemaphoreType.DMA
    return [
        vmem((128, 1024), BF),
        vmem((128, 1024), BF),
        vmem((96, 2048), BF),
        vmem((1, 96), jnp.int32),
        vmem((1, 96), jnp.int32),
        vmem((1536, 128), F32),
        vmem((96, 16, 128), BF),
        vmem((1, 256), jnp.int32),
        pltpu.SMEM((1, 256), jnp.int32),
        vmem((64, 1, 128), F32),
        vmem((1024, 1024), BF),
        vmem((1024, 1024), BF),
        vmem((1024, 3072), BF),
        vmem((1024, 1024), BF),
        vmem((1024, 256), BF),
        vmem((256, 1024), BF),
        vmem((192, 16, 128), BF),
        vmem((192, 16, 128), BF),
        vmem((3072, 128), F32),
        vmem((64, 1, 128), F32),
        vmem((128, 1024), BF),
        vmem((128, 1024), BF),
        vmem((128, 1024), BF),
        vmem((128, 3072), BF),
        vmem((32, 16, 384), BF),
        vmem((32, 16, 256), BF),
        vmem((512, 128), F32),
        vmem((512, 128), F32),
        vmem((512, 128), F32),
        vmem((512, 128), F32),
        vmem((512, 128), F32),
        vmem((512, 128), F32),
        vmem((32, 16, 128), BF),
        vmem((128, 512), BF),
        vmem((128, 512), BF),
        vmem((128, 1024), F32),
        vmem((1024, 1024), BF),
        vmem((1024, 1024), BF),
        vmem((256, 1024), BF),
        vmem((256, 1024), BF),
        vmem((4, 8, 32, 256), BF),
        vmem((4, 8, 16, 512), BF),
        vmem((4, 8, 32, 256), BF),
        vmem((4, 8, 16, 512), BF),
        vmem((8, 32, 256), BF),
        vmem((8, 16, 512), BF),
        vmem((8, 32, 256), BF),
        vmem((8, 16, 512), BF),
        vmem((8, 4, 256), F32),
        vmem((8, 4, 256), F32),
        vmem((2, 8, 512), F32),
        vmem((2, 8, 512), F32),
        dma((13,)),
        dma((5, 4)),
        dma((5, 4)),
        dma((2,)),
        dma((2, 4)),
        dma((2,)),
        dma((2, 4)),
        dma((9,)),
        dma((9,)),
        dma((3,)),
        dma((1,)),
        dma((2,)),
        pltpu.SemaphoreType.REGULAR,
    ]


def local(
    grid_tokens,
    cotangent,
    obs_pairs,
    obs_route,
    obs_patch,
    w_query,
    w_cross_out,
    w_qkv,
    w_axial_out,
    w_in,
    w_out,
):
    vmem = pl.BlockSpec(memory_space=pltpu.VMEM)
    hbm = pl.BlockSpec(memory_space=pltpu.HBM)
    return pl.pallas_call(
        kernel,
        out_shape=(
            jax.ShapeDtypeStruct((4, 2048), F32),
            jax.ShapeDtypeStruct((8, 1024), F32),
        ),
        in_specs=[hbm] * 11,
        out_specs=(vmem, vmem),
        scratch_shapes=scratch(),
        compiler_params=pltpu.CompilerParams(
            collective_id=0, has_side_effects=True, vmem_limit_bytes=62 * 1024 * 1024
        ),
    )(
        grid_tokens.reshape(128, 1024),
        cotangent.reshape(128, 1024),
        obs_pairs.reshape(96, 2048),
        obs_route.reshape(1, 96),
        obs_patch.reshape(1, 96),
        w_query,
        w_cross_out,
        w_qkv,
        w_axial_out,
        w_in,
        w_out,
    )


def solution(mesh):
    return jax.shard_map(
        local,
        mesh=mesh,
        in_specs=(
            P("dp", "sp", None, None),
            P("dp", "sp", None, None),
            P("dp", "sp", None, None),
            P("dp", "sp", None, None),
            P("dp", "sp", None),
            P("dp", None),
            P("dp", None),
            P("dp", None),
            P("dp", None),
            P(),
            P(),
        ),
        out_specs=(P(("sp", "dp"), None), P(("sp", "dp"), None)),
        check_vma=False,
    )
```

```python
import jax
import jax.numpy as jnp
from jax import lax
from jax.experimental import pallas as pl
from jax.experimental.pallas import tpu as pltpu
from jax.sharding import PartitionSpec as P

BF = jnp.bfloat16
F32 = jnp.float32
EPS = 1e-06
ROOT_HALF = 0.7071067811865476
INV_ROOT_TWO_PI = 0.3989422804014327
SCALE = 0.125


def normalize(values):
    values = values.astype(F32)
    return values * lax.rsqrt(jnp.mean(values * values, axis=-1, keepdims=True) + EPS)


def dot(a, b):
    return jnp.dot(a, b, preferred_element_type=F32)


def dot_t(a, b):
    return lax.dot_general(a, b, (((1,), (1,)), ((), ())), preferred_element_type=F32)


def mult(value, by):
    return pl.multiple_of(value, by)


def push(src, dst, send, recv, sp, dp):
    pltpu.make_async_remote_copy(
        src_ref=src,
        dst_ref=dst,
        send_sem=send,
        recv_sem=recv,
        device_id={"sp": sp, "dp": dp},
        device_id_type=pl.DeviceIdType.MESH,
    ).start()


def await_bytes(ref, sem):
    pltpu.make_async_copy(ref, ref, sem).wait()


def kernel(
    tokens_hbm,
    cot_hbm,
    pairs_hbm,
    route_hbm,
    patch_hbm,
    wq_hbm,
    wc_hbm,
    wkv_hbm,
    wa_hbm,
    wi_hbm,
    wo_hbm,
    out_in,
    out_out,
    tokens,
    cot,
    pairs,
    route,
    patch,
    pairs_wide,
    pairs_tiles,
    index_row,
    src_index,
    slot_patch,
    wq,
    wc,
    wkv,
    wa,
    wi,
    wo,
    obs_send,
    obs_recv,
    obs_wide,
    patch_recv,
    queries,
    context,
    after_cross,
    axial,
    lat_own,
    lat_sib,
    q_wide,
    k_wide,
    v_wide,
    ks_wide,
    vs_wide,
    o_wide,
    lat_out,
    lat_context,
    lon_context,
    axial_sum,
    normed_all,
    cot_all,
    hidden_t,
    pre_grad_t,
    gin_send,
    gout_send,
    gin_recv,
    gout_recv,
    gin_mid,
    gout_mid,
    gin_ends,
    gout_ends,
    fin_in_send,
    fin_in_recv,
    fin_out_send,
    fin_out_recv,
    local_sem,
    w_send,
    w_recv,
    gather_send,
    gather_recv,
    share_send,
    share_recv,
    bulk_send,
    bulk_recv,
    last_send,
    last_in,
    last_out,
    entered,
):
    sp = lax.axis_index("sp")
    y = lax.axis_index("dp")
    core = sp % 2
    sib = sp + 1 - 2 * core
    chip = sp // 2
    x = chip % 4
    z = chip // 4
    part = sp % 8

    barrier = pltpu.get_barrier_semaphore()

    def greet(to_sp, to_dp):
        pl.semaphore_signal(
            barrier,
            inc=1,
            device_id={"sp": to_sp, "dp": to_dp},
            device_id_type=pl.DeviceIdType.MESH,
        )

    def greet_line(k, carry):
        greet(((z + k) % 8) * 8 + part, y)
        greet(z * 8 + (part + k) % 8, y)
        return carry

    lax.fori_loop(1, 8, greet_line, 0)
    for k in range(1, 4):
        greet(sp, (y + k) % 4)
    greet(part * 8 + z, y + 1 - 2 * (y % 2))

    loads = [
        pltpu.make_async_copy(source, target, local_sem.at[7 + i])
        for i, (source, target) in enumerate(
            (
                (route_hbm, route),
                (patch_hbm, patch),
                (pairs_hbm, pairs),
                (tokens_hbm, tokens),
                (cot_hbm, cot),
            )
        )
    ]
    for load in loads:
        load.start()

    pieces = (
        (wq_hbm, wq, 0, 1024, "x"),
        (wc_hbm, wc, 0, 1024, "x"),
        (wkv_hbm, wkv, 0, 1536, "xz"),
        (wkv_hbm, wkv, 1536, 1536, "zx"),
        (wa_hbm, wa, 0, 1024, "x"),
    )
    place_of = {"x": (x + core) % 2, "z": (z + core) % 2}
    mate_of = {
        "x": z * 8 + ((x + 5 - 2 * place_of["x"]) % 4) * 2 + core,
        "z": ((z + 9 - 2 * place_of["z"]) % 8) * 8 + x * 2 + core,
    }

    def spans(plan):
        rows = 128 >> len(plan)
        first = core * 128
        for n, axis in enumerate(plan):
            first += place_of[axis] * (rows << n)
        made = [(first, rows, None)]
        for n, axis in enumerate(plan):
            made.append((first, rows << n, mate_of[axis]))
            first -= place_of[axis] * (rows << n)
        made.append((core * 128, 128, sib))
        return made

    stages = [spans(piece[4]) for piece in pieces]

    def landing(i, stage):
        full, col, width = pieces[i][1:4]
        return full.at[pl.ds(0, 3 * stages[i][stage][1]), pl.ds(col, width)]

    def start_piece(i):
        hbm, full, col, width, _ = pieces[i]
        first, rows, _ = stages[i][0]
        for k in range(1, 4):
            push(
                hbm.at[pl.ds(mult(first, 32), rows), pl.ds(col, width)],
                full.at[pl.ds(mult(y * 256 + first, 32), rows), pl.ds(col, width)],
                w_send.at[i, 0],
                w_recv.at[i, 0],
                sp,
                (y + k) % 4,
            )

    def own_piece(i):
        hbm, full, col, width, _ = pieces[i]
        return pltpu.make_async_copy(
            hbm.at[:, pl.ds(col, width)],
            full.at[pl.ds(mult(y * 256, 256), 256), pl.ds(col, width)],
            local_sem.at[i],
        )

    def advance(i, stage):
        full, col, width = pieces[i][1:4]
        await_bytes(landing(i, stage - 1), w_recv.at[i, stage - 1])
        first, rows, mate = stages[i][stage]
        for k in range(1, 4):
            part_rows = full.at[
                pl.ds(mult(((y + k) % 4) * 256 + first, 32), rows), pl.ds(col, width)
            ]
            push(part_rows, part_rows, w_send.at[i, stage], w_recv.at[i, stage], mate, y)

    def finish_piece(i):
        last = len(stages[i]) - 1
        await_bytes(landing(i, last), w_recv.at[i, last])
        own_piece(i).wait()

    def drain_piece(i):
        for stage in range(len(stages[i])):
            await_bytes(landing(i, stage), w_send.at[i, stage])

    for i in range(5):
        own_piece(i).start()
    wi_copy = pltpu.make_async_copy(
        wi_hbm.at[:, pl.ds(mult(part * 256, 256), 256)], wi, local_sem.at[5]
    )
    wo_copy = pltpu.make_async_copy(
        wo_hbm.at[pl.ds(mult(part * 256, 256), 256), :], wo, local_sem.at[6]
    )
    wi_copy.start()
    wo_copy.start()

    loads[0].wait()
    loads[1].wait()
    line = lax.broadcasted_iota(jnp.int32, (96, 96), 0)
    lane = lax.broadcasted_iota(jnp.int32, (96, 96), 1)

    def upright(row):
        return jnp.sum(jnp.where(line == lane, row, 0), axis=1, keepdims=True)

    row_across = route[...]
    row_down = upright(row_across)
    patch_across = patch[...] + 1
    same = row_across == row_down
    rank_across = jnp.sum(jnp.where(same & (line < lane), 1, 0), axis=0, keepdims=True)
    rank_down = jnp.sum(jnp.where(same & (lane < line), 1, 0), axis=1, keepdims=True)
    slot_across = row_across * 3 + rank_across
    slot_down = row_down * 3 + rank_down
    hit = slot_down == lax.broadcasted_iota(jnp.int32, (96, 256), 1)
    index_row[...] = jnp.sum(
        jnp.where(hit, lax.broadcasted_iota(jnp.int32, (96, 256), 0), 0), axis=0, keepdims=True
    )
    index_copy = pltpu.make_async_copy(index_row, src_index, local_sem.at[12])
    index_copy.start()
    lanes = lax.broadcasted_iota(jnp.int32, (64, 128), 1)
    found_patch = jnp.zeros((64, 128), jnp.int32)
    for r in range(3):
        mine = slot_across == lax.broadcasted_iota(jnp.int32, (64, 96), 0) * 3 + r
        value = jnp.sum(jnp.where(mine, patch_across, 0), axis=1, keepdims=True) - 1
        found_patch = jnp.where(lanes == r, value, found_patch)
    slot_patch[...] = found_patch.astype(F32).reshape(64, 1, 128)

    pl.semaphore_wait(barrier, 18)

    def greet_again(k, carry):
        pl.semaphore_signal(
            entered,
            inc=1,
            device_id={"sp": z * 8 + (part + k) % 8, "dp": y},
            device_id_type=pl.DeviceIdType.MESH,
        )
        return carry

    lax.fori_loop(1, 8, greet_again, 0)

    loads[2].wait()
    for n in range(16):
        pairs_wide[pl.ds(n, 96, stride=16), :] = pairs[:, n * 128 : (n + 1) * 128].astype(F32)
    pairs_tiles[...] = pairs_wide[...].reshape(96, 16, 128).astype(BF)
    index_copy.wait()

    def place(s, carry):
        obs_send[s] = pairs_tiles[src_index[0, s]]
        return carry

    lax.fori_loop(0, 192, place, 0, unroll=8)
    pl.semaphore_wait(entered, 7)
    start_piece(0)

    def send_obs(k, carry):
        to = (sp + k) % 64
        push(
            obs_send.at[pl.ds(to * 3, 3)],
            obs_recv.at[pl.ds(sp * 3, 3)],
            bulk_send.at[0],
            bulk_recv.at[0],
            to,
            y,
        )
        push(slot_patch.at[to], patch_recv.at[sp], bulk_send.at[1], bulk_recv.at[1], to, y)
        return carry

    lax.fori_loop(1, 64, send_obs, 0)
    start_piece(1)
    start_piece(2)
    obs_recv[pl.ds(sp * 3, 3)] = obs_send[pl.ds(sp * 3, 3)]
    patch_recv[sp] = slot_patch[sp]

    def share_start(j, source, full):
        rows = full.at[pl.ds(mult(part * 128, 128), 128), :]
        push(source, rows, gather_send.at[j], gather_recv.at[j, 0], sib, y)
        for k in range(1, 4):
            push(
                source,
                rows,
                gather_send.at[j],
                gather_recv.at[j, k],
                z * 8 + ((x + k) % 4) * 2 + core,
                y,
            )

    def from_chip(full, k, cores):
        first = ((x - k + 4) % 4) * 256 + (core * 128 if cores == 1 else 0)
        return full.at[pl.ds(mult(first, 128), 128 * cores), :]

    def share_forward(j, full, k):
        rows = from_chip(full, k, 1)
        await_bytes(rows, gather_recv.at[j, k])
        push(rows, rows, share_send.at[j], share_recv.at[j, k], sib, y)

    def share_drain(j, full):
        await_bytes(full.at[pl.ds(0, 512), :], gather_send.at[j])
        await_bytes(full.at[pl.ds(0, 384), :], share_send.at[j])

    loads[3].wait()
    loads[4].wait()
    cot_all[pl.ds(mult(part * 128, 128), 128), :] = cot[...]

    normed = normalize(tokens[...]).astype(BF)
    advance(0, 1)
    advance(1, 1)
    advance(0, 2)
    start_piece(3)
    finish_piece(0)

    def columns(count, width, source, weight, target, offset):
        def step(n, carry):
            cols = pl.ds(mult(offset + n * width, width), width)
            target[:, cols] = dot(source, weight[:, cols]).astype(BF)
            return carry

        lax.fori_loop(0, count, step, 0)

    columns(4, 256, normed, wq, queries, 0)
    advance(2, 1)
    start_piece(4)
    advance(1, 2)
    advance(2, 2)

    await_bytes(obs_recv.at[pl.ds(0, 189)], bulk_recv.at[0])
    await_bytes(patch_recv.at[pl.ds(0, 63)], bulk_recv.at[1])
    obs_wide[...] = obs_recv[...].astype(F32).reshape(3072, 128)
    patches = patch_recv[...].reshape(64, 128)
    slot_lane = lax.broadcasted_iota(jnp.int32, (64, 192), 1)
    slot_from = lax.broadcasted_iota(jnp.int32, (64, 192), 0) * 3
    slot_row = jnp.zeros((1, 192), F32)
    for r in range(3):
        slot_row += jnp.sum(
            jnp.where(slot_lane == slot_from + r, patches[:, r : r + 1], 0.0),
            axis=0,
            keepdims=True,
        )
    cell_patch = (lax.broadcasted_iota(jnp.int32, (128, 192), 0) // 32).astype(F32)
    same_patch = cell_patch == slot_row
    low = lax.broadcasted_iota(jnp.int32, (128, 128), 1) < 64
    zero = jnp.zeros((128, 128), BF)

    def cross_pair(g, carry):
        cols = pl.ds(mult(g * 128, 128), 128)
        keys = obs_wide[pl.ds(g, 192, stride=16), :].astype(BF)
        values = obs_wide[pl.ds(g + 8, 192, stride=16), :].astype(BF)
        both = queries[:, cols]
        found = []
        for half in (jnp.where(low, both, zero), jnp.where(low, zero, both)):
            masked = jnp.where(same_patch, dot_t(half, keys) * SCALE, -1e30)
            top = jnp.maximum(jnp.max(masked, axis=-1, keepdims=True), 0.0)
            terms = jnp.where(same_patch, jnp.exp(masked - top), 0.0)
            total = jnp.exp(-top) + jnp.sum(terms, axis=-1, keepdims=True)
            found.append(dot((terms / total).astype(BF), values))
        context[:, cols] = jnp.where(low, found[0], found[1]).astype(BF)
        return carry

    def cross_four(i, carry):
        @pl.when(i == 1)
        def _():
            advance(2, 3)
            advance(3, 1)
            advance(4, 1)

        for g in range(4):
            cross_pair(i * 4 + g, 0)
        return carry

    lax.fori_loop(0, 2, cross_four, 0)

    finish_piece(1)

    def cross_out(n, carry):
        cols = pl.ds(mult(n * 256, 256), 256)
        after_cross[:, cols] = (
            tokens[:, cols].astype(F32) + dot(context[...], wc[:, cols])
        ).astype(BF)
        return carry

    lax.fori_loop(0, 4, cross_out, 0)
    advance(3, 2)
    advance(4, 2)
    share_start(0, cot, cot_all)
    normed_axial = normalize(after_cross[...]).astype(BF)
    finish_piece(2)
    columns(6, 256, normed_axial, wkv, axial, 0)

    cell_at, group_at = z, x

    def send_lat(k, carry):
        to = (chip + k) % 32
        push(
            axial.at[pl.ds(mult((to // 4) * 16, 16), 16), pl.ds(mult((to % 4) * 384, 128), 384)],
            lat_own.at[chip],
            bulk_send.at[2],
            bulk_recv.at[2],
            to * 2 + core,
            y,
        )
        return carry

    lax.fori_loop(1, 32, send_lat, 0)
    lat_own[chip] = axial[pl.ds(mult(cell_at * 16, 16), 16), pl.ds(mult(group_at * 384, 128), 384)]

    advance(3, 3)
    finish_piece(3)
    columns(6, 256, normed_axial, wkv, axial, 1536)

    def lon_pair(p, carry):
        both = axial[:, pl.ds(mult(1536 + p * 128, 128), 128)]
        keys = axial[:, pl.ds(mult(2048 + p * 128, 128), 128)]
        values = axial[:, pl.ds(mult(2560 + p * 128, 128), 128)]
        found = []
        for half in (jnp.where(low, both, zero), jnp.where(low, zero, both)):
            scores = dot_t(half, keys) * SCALE
            terms = jnp.exp(scores - jnp.max(scores, axis=-1, keepdims=True))
            weights = (terms / jnp.sum(terms, axis=-1, keepdims=True)).astype(BF)
            found.append(dot(weights, values))
        lon_context[:, pl.ds(mult(p * 128, 128), 128)] = jnp.where(low, found[0], found[1]).astype(
            BF
        )
        return carry

    lat_kv = lat_own.at[:, :, pl.ds(128, 256)]
    await_bytes(lat_own.at[pl.ds(0, 31)], bulk_recv.at[2])
    push(lat_kv, lat_sib, bulk_send.at[3], bulk_recv.at[3], sib, y)
    lax.fori_loop(0, 4, lon_pair, 0, unroll=4)
    q_wide[...] = lat_own[:, :, 0:128].astype(F32).reshape(512, 128)
    k_wide[...] = lat_own[:, :, 128:256].astype(F32).reshape(512, 128)
    v_wide[...] = lat_own[:, :, 256:384].astype(F32).reshape(512, 128)
    await_bytes(lat_sib, bulk_recv.at[3])
    ks_wide[...] = lat_sib[:, :, 0:128].astype(F32).reshape(512, 128)
    vs_wide[...] = lat_sib[:, :, 128:256].astype(F32).reshape(512, 128)
    low_rows = lax.broadcasted_iota(jnp.int32, (32, 128), 1) < 64

    def lat_cell(l, carry):
        rows = pl.ds(l, 32, stride=16)
        q = q_wide[rows, :]
        both = jnp.concatenate(
            [jnp.where(low_rows, q, 0.0), jnp.where(low_rows, 0.0, q)], axis=0
        ).astype(BF)
        keys = jnp.concatenate([k_wide[rows, :], ks_wide[rows, :]], axis=0).astype(BF)
        values = jnp.concatenate([v_wide[rows, :], vs_wide[rows, :]], axis=0).astype(BF)
        scores = dot_t(both, keys) * SCALE
        terms = jnp.exp(scores - jnp.max(scores, axis=-1, keepdims=True))
        weights = (terms / jnp.sum(terms, axis=-1, keepdims=True)).astype(BF)
        found = dot(weights, values)
        o_wide[rows, :] = jnp.where(low_rows, found[:32], found[32:])
        return carry

    lax.fori_loop(0, 16, lat_cell, 0, unroll=8)
    lat_out[...] = o_wide[...].reshape(32, 16, 128).astype(BF)
    home = (pl.ds(mult(cell_at * 16, 16), 16), pl.ds(mult(group_at * 128, 128), 128))

    def send_back(k, carry):
        to = (chip + k) % 32
        push(
            lat_out.at[to],
            lat_context.at[home],
            bulk_send.at[4],
            bulk_recv.at[4],
            to * 2 + core,
            y,
        )
        return carry

    lax.fori_loop(1, 32, send_back, 0)
    lat_context[home] = lat_out[chip]
    finish_piece(4)

    def axial_lon(n, carry):
        cols = pl.ds(mult(n * 256, 256), 256)
        axial_sum[:, cols] = after_cross[:, cols].astype(F32) + dot(
            lon_context[...], wa[pl.ds(512, 512), cols]
        )
        return carry

    def axial_lat(n, carry):
        cols = pl.ds(mult(n * 256, 256), 256)
        context[:, cols] = (
            axial_sum[:, cols] + dot(lat_context[...], wa[pl.ds(0, 512), cols])
        ).astype(BF)
        return carry

    for k in range(1, 4):
        share_forward(0, cot_all, k)
    lax.fori_loop(0, 4, axial_lon, 0)
    await_bytes(lat_out.at[pl.ds(0, 31)], bulk_recv.at[4])
    lax.fori_loop(0, 4, axial_lat, 0)
    mine = pl.ds(mult(part * 128, 128), 128)
    normed_all[mine, :] = normalize(context[...]).astype(BF)
    share_start(1, normed_all.at[mine, :], normed_all)
    await_bytes(cot_all.at[pl.ds(0, 128), :], gather_recv.at[0, 0])
    for k in range(1, 4):
        await_bytes(from_chip(cot_all, k, 1), share_recv.at[0, k])
    wi_copy.wait()
    wo_copy.wait()
    await_bytes(normed_all.at[pl.ds(0, 128), :], gather_recv.at[1, 0])

    def ff_chip(i, carry):
        k = jnp.where(i == 2, 3, jnp.where(i == 3, 2, i))

        @pl.when(i == 1)
        def _():
            share_forward(1, normed_all, 1)
            share_forward(1, normed_all, 3)

        @pl.when(i == 2)
        def _():
            share_forward(1, normed_all, 2)

        @pl.when(i > 0)
        def _():
            await_bytes(normed_all.at[pl.ds(0, 128), :], share_recv.at[1, k])

        rows = pl.ds(mult(((x - k + 4) % 4) * 256, 256), 256)
        pre_act = dot(normed_all[rows, :], wi[...])
        hidden_grad = dot_t(cot_all[rows, :], wo[...])
        cdf = 0.5 * (1.0 + lax.erf(pre_act * ROOT_HALF))
        slope = cdf + pre_act * jnp.exp(-0.5 * pre_act * pre_act) * INV_ROOT_TWO_PI
        hidden_t[:, rows] = (pre_act * cdf).astype(BF).T
        pre_grad_t[:, rows] = (hidden_grad * slope).astype(BF).T
        return carry

    lax.fori_loop(0, 4, ff_chip, 0)

    def fold(source, received, at):
        for k in range(1, 4):
            push(
                source.at[(y + k) % 4],
                received.at[y],
                bulk_send.at[at],
                bulk_recv.at[at],
                sp,
                (y + k) % 4,
            )
        received[y] = source[y]

    def pass_on(received, middle, ends, at, to):
        await_bytes(received.at[pl.ds(0, 3)], bulk_recv.at[at])

        def total(n, carry):
            found = received[0, n].astype(F32)
            for k in range(1, 4):
                found += received[k, n].astype(F32)
            middle[n] = found.astype(BF)
            return carry

        lax.fori_loop(0, 8, total, 0)

        def one(k, carry):
            push(
                middle.at[(z + k) % 8],
                ends.at[z],
                bulk_send.at[to],
                bulk_recv.at[to],
                ((z + k) % 8) * 8 + part,
                y,
            )
            return carry

        lax.fori_loop(1, 8, one, 0)
        ends[z] = middle[z]

    def end_sum(ends, at):
        await_bytes(ends.at[pl.ds(0, 7)], bulk_recv.at[at])
        found = ends[0].astype(F32)
        for n in range(1, 8):
            found += ends[n].astype(F32)
        return found

    def grad_out_cols(n, carry):
        cols = pl.ds(mult(n * 256, 256), 256)
        grad = dot(hidden_t[...], cot_all[:, cols]).astype(BF)
        inner = pl.ds(mult((n % 2) * 256, 256), 256)
        for at in range(16):
            gout_send[(at % 2) * 2 + n // 2, at // 2, :, inner] = grad[at * 16 : at * 16 + 16]
        return carry

    lax.fori_loop(0, 4, grad_out_cols, 0)
    fold(gout_send, gout_recv, 6)

    down = lax.broadcasted_iota(jnp.int32, (128, 128), 0)
    across = lax.broadcasted_iota(jnp.int32, (128, 128), 1)
    turn = (across == ((down % 32) // 4) * 16 + (down // 32) * 4 + down % 4).astype(F32).astype(BF)

    def grad_cols(n, carry):
        cols = pl.ds(mult(n * 256, 256), 256)
        grad = dot(pre_grad_t[...], normed_all[:, cols]).astype(BF)
        for half in range(2):
            turned = dot_t(turn, grad[:, half * 128 : half * 128 + 128]).astype(BF)
            for m in range(4):
                gin_send[m, n * 2 + half] = turned[m * 32 : m * 32 + 32]
        return carry

    lax.fori_loop(0, 4, grad_cols, 0)

    fold(gin_send, gin_recv, 5)
    pass_on(gout_recv, gout_mid, gout_ends, 6, 8)
    pass_on(gin_recv, gin_mid, gin_ends, 5, 7)
    sum_out = end_sum(gout_ends, 8)
    sum_in = end_sum(gin_ends, 7)
    for n in range(8):
        fin_in_send[n] = sum_in[n * 4 : n * 4 + 4]
    for n in range(2):
        fin_out_send[n] = sum_out[n * 8 : n * 8 + 8]

    fin_in_recv[part] = fin_in_send[part]
    for k in range(1, 8):
        n = (part + k) % 8
        push(
            fin_in_send.at[n], fin_in_recv.at[part], last_send.at[0], last_in.at[0], z * 8 + n, y
        )
    to_sp = part * 8 + z
    odd = y % 2
    push(
        fin_out_send.at[1 - odd],
        fin_out_recv.at[odd],
        last_send.at[1],
        last_out.at[0],
        to_sp,
        y + 1 - 2 * odd,
    )

    @pl.when(part == z)
    def _():
        fin_out_recv[odd] = fin_out_send[odd]

    @pl.when(part != z)
    def _():
        push(
            fin_out_send.at[odd],
            fin_out_recv.at[odd],
            last_send.at[2],
            last_out.at[1],
            to_sp,
            y,
        )
        await_bytes(fin_out_recv.at[0], last_out.at[1])
        await_bytes(fin_out_send.at[0], last_send.at[2])

    await_bytes(fin_out_recv.at[0], last_out.at[0])
    for n in range(2):
        out_out[:, n * 512 : (n + 1) * 512] = fin_out_recv[n]
    await_bytes(fin_in_recv.at[pl.ds(0, 7)], last_in.at[0])
    for n in range(8):
        out_in[:, n * 256 : (n + 1) * 256] = fin_in_recv[n]

    for i in range(5):
        drain_piece(i)
    share_drain(0, cot_all)
    share_drain(1, normed_all)
    await_bytes(obs_recv.at[pl.ds(0, 189)], bulk_send.at[0])
    await_bytes(patch_recv.at[pl.ds(0, 63)], bulk_send.at[1])
    await_bytes(lat_own.at[pl.ds(0, 31)], bulk_send.at[2])
    await_bytes(lat_sib, bulk_send.at[3])
    await_bytes(lat_out.at[pl.ds(0, 31)], bulk_send.at[4])
    await_bytes(gin_recv.at[pl.ds(0, 3)], bulk_send.at[5])
    await_bytes(gout_recv.at[pl.ds(0, 3)], bulk_send.at[6])
    await_bytes(gin_ends.at[pl.ds(0, 7)], bulk_send.at[7])
    await_bytes(gout_ends.at[pl.ds(0, 7)], bulk_send.at[8])
    await_bytes(fin_in_send.at[pl.ds(0, 7)], last_send.at[0])
    await_bytes(fin_out_send.at[0], last_send.at[1])


def scratch():
    vmem = pltpu.VMEM
    dma = pltpu.SemaphoreType.DMA
    return [
        vmem((128, 1024), BF),
        vmem((128, 1024), BF),
        vmem((96, 2048), BF),
        vmem((1, 96), jnp.int32),
        vmem((1, 96), jnp.int32),
        vmem((1536, 128), F32),
        vmem((96, 16, 128), BF),
        vmem((1, 256), jnp.int32),
        pltpu.SMEM((1, 256), jnp.int32),
        vmem((64, 1, 128), F32),
        vmem((1024, 1024), BF),
        vmem((1024, 1024), BF),
        vmem((1024, 3072), BF),
        vmem((1024, 1024), BF),
        vmem((1024, 256), BF),
        vmem((256, 1024), BF),
        vmem((192, 16, 128), BF),
        vmem((192, 16, 128), BF),
        vmem((3072, 128), F32),
        vmem((64, 1, 128), F32),
        vmem((128, 1024), BF),
        vmem((128, 1024), BF),
        vmem((128, 1024), BF),
        vmem((128, 3072), BF),
        vmem((32, 16, 384), BF),
        vmem((32, 16, 256), BF),
        vmem((512, 128), F32),
        vmem((512, 128), F32),
        vmem((512, 128), F32),
        vmem((512, 128), F32),
        vmem((512, 128), F32),
        vmem((512, 128), F32),
        vmem((32, 16, 128), BF),
        vmem((128, 512), BF),
        vmem((128, 512), BF),
        vmem((128, 1024), F32),
        vmem((1024, 1024), BF),
        vmem((1024, 1024), BF),
        vmem((256, 1024), BF),
        vmem((256, 1024), BF),
        vmem((4, 8, 32, 256), BF),
        vmem((4, 8, 16, 512), BF),
        vmem((4, 8, 32, 256), BF),
        vmem((4, 8, 16, 512), BF),
        vmem((8, 32, 256), BF),
        vmem((8, 16, 512), BF),
        vmem((8, 32, 256), BF),
        vmem((8, 16, 512), BF),
        vmem((8, 4, 256), F32),
        vmem((8, 4, 256), F32),
        vmem((2, 8, 512), F32),
        vmem((2, 8, 512), F32),
        dma((13,)),
        dma((5, 4)),
        dma((5, 4)),
        dma((2,)),
        dma((2, 4)),
        dma((2,)),
        dma((2, 4)),
        dma((9,)),
        dma((9,)),
        dma((3,)),
        dma((1,)),
        dma((2,)),
        pltpu.SemaphoreType.REGULAR,
    ]


def local(
    grid_tokens,
    cotangent,
    obs_pairs,
    obs_route,
    obs_patch,
    w_query,
    w_cross_out,
    w_qkv,
    w_axial_out,
    w_in,
    w_out,
):
    vmem = pl.BlockSpec(memory_space=pltpu.VMEM)
    hbm = pl.BlockSpec(memory_space=pltpu.HBM)
    return pl.pallas_call(
        kernel,
        out_shape=(
            jax.ShapeDtypeStruct((4, 2048), F32),
            jax.ShapeDtypeStruct((8, 1024), F32),
        ),
        in_specs=[hbm] * 11,
        out_specs=(vmem, vmem),
        scratch_shapes=scratch(),
        compiler_params=pltpu.CompilerParams(
            collective_id=0, has_side_effects=True, vmem_limit_bytes=62 * 1024 * 1024
        ),
    )(
        grid_tokens.reshape(128, 1024),
        cotangent.reshape(128, 1024),
        obs_pairs.reshape(96, 2048),
        obs_route.reshape(1, 96),
        obs_patch.reshape(1, 96),
        w_query,
        w_cross_out,
        w_qkv,
        w_axial_out,
        w_in,
        w_out,
    )


def solution(mesh):
    return jax.shard_map(
        local,
        mesh=mesh,
        in_specs=(
            P("dp", "sp", None, None),
            P("dp", "sp", None, None),
            P("dp", "sp", None, None),
            P("dp", "sp", None, None),
            P("dp", "sp", None),
            P("dp", None),
            P("dp", None),
            P("dp", None),
            P("dp", None),
            P(),
            P(),
        ),
        out_specs=(P(("sp", "dp"), None), P(("sp", "dp"), None)),
        check_vma=False,
    )
```

```python
import jax
import jax.numpy as jnp
from jax import lax
from jax.experimental import pallas as pl
from jax.experimental.pallas import tpu as pltpu
from jax.sharding import PartitionSpec as P

BF = jnp.bfloat16
F32 = jnp.float32
EPS = 1e-06
ROOT_HALF = 0.7071067811865476
INV_ROOT_TWO_PI = 0.3989422804014327
SCALE = 0.125


def normalize(values):
    values = values.astype(F32)
    return values * lax.rsqrt(jnp.mean(values * values, axis=-1, keepdims=True) + EPS)


def dot(a, b):
    return jnp.dot(a, b, preferred_element_type=F32)


def dot_t(a, b):
    return lax.dot_general(a, b, (((1,), (1,)), ((), ())), preferred_element_type=F32)


def mult(value, by):
    return pl.multiple_of(value, by)


def push(src, dst, send, recv, sp, dp):
    pltpu.make_async_remote_copy(
        src_ref=src,
        dst_ref=dst,
        send_sem=send,
        recv_sem=recv,
        device_id={"sp": sp, "dp": dp},
        device_id_type=pl.DeviceIdType.MESH,
    ).start()


def await_bytes(ref, sem):
    pltpu.make_async_copy(ref, ref, sem).wait()


def kernel(
    tokens_hbm,
    cot_hbm,
    pairs_hbm,
    route_hbm,
    patch_hbm,
    wq_hbm,
    wc_hbm,
    wkv_hbm,
    wa_hbm,
    wi_hbm,
    wo_hbm,
    out_in,
    out_out,
    tokens,
    cot,
    pairs,
    route,
    patch,
    pairs_wide,
    pairs_tiles,
    index_row,
    src_index,
    slot_patch,
    wq,
    wc,
    wkv,
    wa,
    wi,
    wo,
    obs_send,
    obs_recv,
    obs_wide,
    patch_recv,
    queries,
    context,
    after_cross,
    axial,
    lat_own,
    lat_sib,
    q_wide,
    k_wide,
    v_wide,
    ks_wide,
    vs_wide,
    o_wide,
    lat_out,
    lat_context,
    lon_context,
    axial_sum,
    normed_all,
    cot_all,
    hidden_t,
    pre_grad_t,
    gin_send,
    gout_send,
    gin_recv,
    gout_recv,
    gin_mid,
    gout_mid,
    gin_ends,
    gout_ends,
    gin_right,
    right_recv,
    right_mid,
    right_ends,
    fin_in_send,
    fin_in_recv,
    fin_out_send,
    fin_out_recv,
    local_sem,
    w_send,
    w_recv,
    gather_send,
    gather_recv,
    share_send,
    share_recv,
    bulk_send,
    bulk_recv,
    last_send,
    last_in,
    last_out,
    entered,
):
    sp = lax.axis_index("sp")
    y = lax.axis_index("dp")
    core = sp % 2
    sib = sp + 1 - 2 * core
    chip = sp // 2
    x = chip % 4
    z = chip // 4
    part = sp % 8

    barrier = pltpu.get_barrier_semaphore()

    def greet(to_sp, to_dp):
        pl.semaphore_signal(
            barrier,
            inc=1,
            device_id={"sp": to_sp, "dp": to_dp},
            device_id_type=pl.DeviceIdType.MESH,
        )

    def greet_line(k, carry):
        greet(((z + k) % 8) * 8 + part, y)
        greet(z * 8 + (part + k) % 8, y)
        return carry

    lax.fori_loop(1, 8, greet_line, 0)
    for k in range(1, 4):
        greet(sp, (y + k) % 4)
    greet(part * 8 + z, y + 1 - 2 * (y % 2))

    loads = [
        pltpu.make_async_copy(source, target, local_sem.at[7 + i])
        for i, (source, target) in enumerate(
            (
                (route_hbm, route),
                (patch_hbm, patch),
                (pairs_hbm, pairs),
                (tokens_hbm, tokens),
                (cot_hbm, cot),
            )
        )
    ]
    for load in loads:
        load.start()

    pieces = (
        (wq_hbm, wq, 0, 1024, "x"),
        (wc_hbm, wc, 0, 1024, "x"),
        (wkv_hbm, wkv, 0, 1536, "xz"),
        (wkv_hbm, wkv, 1536, 1536, "zx"),
        (wa_hbm, wa, 0, 1024, "x"),
    )
    place_of = {"x": (x + core) % 2, "z": (z + core) % 2}
    mate_of = {
        "x": z * 8 + ((x + 5 - 2 * place_of["x"]) % 4) * 2 + core,
        "z": ((z + 9 - 2 * place_of["z"]) % 8) * 8 + x * 2 + core,
    }

    def spans(plan):
        rows = 128 >> len(plan)
        first = core * 128
        for n, axis in enumerate(plan):
            first += place_of[axis] * (rows << n)
        made = [(first, rows, None)]
        for n, axis in enumerate(plan):
            made.append((first, rows << n, mate_of[axis]))
            first -= place_of[axis] * (rows << n)
        made.append((core * 128, 128, sib))
        return made

    stages = [spans(piece[4]) for piece in pieces]

    def landing(i, stage):
        full, col, width = pieces[i][1:4]
        return full.at[pl.ds(0, 3 * stages[i][stage][1]), pl.ds(col, width)]

    def start_piece(i):
        hbm, full, col, width, _ = pieces[i]
        first, rows, _ = stages[i][0]
        for k in range(1, 4):
            push(
                hbm.at[pl.ds(mult(first, 32), rows), pl.ds(col, width)],
                full.at[pl.ds(mult(y * 256 + first, 32), rows), pl.ds(col, width)],
                w_send.at[i, 0],
                w_recv.at[i, 0],
                sp,
                (y + k) % 4,
            )

    def own_piece(i):
        hbm, full, col, width, _ = pieces[i]
        return pltpu.make_async_copy(
            hbm.at[:, pl.ds(col, width)],
            full.at[pl.ds(mult(y * 256, 256), 256), pl.ds(col, width)],
            local_sem.at[i],
        )

    def advance(i, stage):
        full, col, width = pieces[i][1:4]
        await_bytes(landing(i, stage - 1), w_recv.at[i, stage - 1])
        first, rows, mate = stages[i][stage]
        for k in range(1, 4):
            part_rows = full.at[
                pl.ds(mult(((y + k) % 4) * 256 + first, 32), rows), pl.ds(col, width)
            ]
            push(part_rows, part_rows, w_send.at[i, stage], w_recv.at[i, stage], mate, y)

    def finish_piece(i):
        last = len(stages[i]) - 1
        await_bytes(landing(i, last), w_recv.at[i, last])
        own_piece(i).wait()

    def drain_piece(i):
        for stage in range(len(stages[i])):
            await_bytes(landing(i, stage), w_send.at[i, stage])

    for i in range(5):
        own_piece(i).start()
    wi_copy = pltpu.make_async_copy(
        wi_hbm.at[:, pl.ds(mult(part * 256, 256), 256)], wi, local_sem.at[5]
    )
    wo_copy = pltpu.make_async_copy(
        wo_hbm.at[pl.ds(mult(part * 256, 256), 256), :], wo, local_sem.at[6]
    )
    wi_copy.start()
    wo_copy.start()

    loads[0].wait()
    loads[1].wait()
    line = lax.broadcasted_iota(jnp.int32, (96, 96), 0)
    lane = lax.broadcasted_iota(jnp.int32, (96, 96), 1)

    def upright(row):
        return jnp.sum(jnp.where(line == lane, row, 0), axis=1, keepdims=True)

    row_across = route[...]
    row_down = upright(row_across)
    patch_across = patch[...] + 1
    same = row_across == row_down
    rank_across = jnp.sum(jnp.where(same & (line < lane), 1, 0), axis=0, keepdims=True)
    rank_down = jnp.sum(jnp.where(same & (lane < line), 1, 0), axis=1, keepdims=True)
    slot_across = row_across * 3 + rank_across
    slot_down = row_down * 3 + rank_down
    hit = slot_down == lax.broadcasted_iota(jnp.int32, (96, 256), 1)
    index_row[...] = jnp.sum(
        jnp.where(hit, lax.broadcasted_iota(jnp.int32, (96, 256), 0), 0), axis=0, keepdims=True
    )
    index_copy = pltpu.make_async_copy(index_row, src_index, local_sem.at[12])
    index_copy.start()
    lanes = lax.broadcasted_iota(jnp.int32, (64, 128), 1)
    found_patch = jnp.zeros((64, 128), jnp.int32)
    for r in range(3):
        mine = slot_across == lax.broadcasted_iota(jnp.int32, (64, 96), 0) * 3 + r
        value = jnp.sum(jnp.where(mine, patch_across, 0), axis=1, keepdims=True) - 1
        found_patch = jnp.where(lanes == r, value, found_patch)
    slot_patch[...] = found_patch.astype(F32).reshape(64, 1, 128)

    pl.semaphore_wait(barrier, 18)

    def greet_again(k, carry):
        pl.semaphore_signal(
            entered,
            inc=1,
            device_id={"sp": z * 8 + (part + k) % 8, "dp": y},
            device_id_type=pl.DeviceIdType.MESH,
        )
        return carry

    lax.fori_loop(1, 8, greet_again, 0)

    loads[2].wait()
    for n in range(16):
        pairs_wide[pl.ds(n, 96, stride=16), :] = pairs[:, n * 128 : (n + 1) * 128].astype(F32)
    pairs_tiles[...] = pairs_wide[...].reshape(96, 16, 128).astype(BF)
    index_copy.wait()

    def place(s, carry):
        obs_send[s] = pairs_tiles[src_index[0, s]]
        return carry

    lax.fori_loop(0, 192, place, 0, unroll=8)
    pl.semaphore_wait(entered, 7)
    start_piece(0)

    def send_obs(k, carry):
        to = (sp + k) % 64
        push(
            obs_send.at[pl.ds(to * 3, 3)],
            obs_recv.at[pl.ds(sp * 3, 3)],
            bulk_send.at[0],
            bulk_recv.at[0],
            to,
            y,
        )
        push(slot_patch.at[to], patch_recv.at[sp], bulk_send.at[1], bulk_recv.at[1], to, y)
        return carry

    lax.fori_loop(1, 64, send_obs, 0)
    start_piece(1)
    start_piece(2)
    obs_recv[pl.ds(sp * 3, 3)] = obs_send[pl.ds(sp * 3, 3)]
    patch_recv[sp] = slot_patch[sp]

    def share_start(j, source, full):
        rows = full.at[pl.ds(mult(part * 128, 128), 128), :]
        push(source, rows, gather_send.at[j], gather_recv.at[j, 0], sib, y)
        for k in range(1, 4):
            push(
                source,
                rows,
                gather_send.at[j],
                gather_recv.at[j, k],
                z * 8 + ((x + k) % 4) * 2 + core,
                y,
            )

    def from_chip(full, k, cores):
        first = ((x - k + 4) % 4) * 256 + (core * 128 if cores == 1 else 0)
        return full.at[pl.ds(mult(first, 128), 128 * cores), :]

    def share_forward(j, full, k):
        rows = from_chip(full, k, 1)
        await_bytes(rows, gather_recv.at[j, k])
        push(rows, rows, share_send.at[j], share_recv.at[j, k], sib, y)

    def share_drain(j, full):
        await_bytes(full.at[pl.ds(0, 512), :], gather_send.at[j])
        await_bytes(full.at[pl.ds(0, 384), :], share_send.at[j])

    loads[3].wait()
    loads[4].wait()
    cot_all[pl.ds(mult(part * 128, 128), 128), :] = cot[...]

    normed = normalize(tokens[...]).astype(BF)
    advance(0, 1)
    advance(1, 1)
    advance(0, 2)
    start_piece(3)
    finish_piece(0)

    def columns(count, width, source, weight, target, offset):
        def step(n, carry):
            cols = pl.ds(mult(offset + n * width, width), width)
            target[:, cols] = dot(source, weight[:, cols]).astype(BF)
            return carry

        lax.fori_loop(0, count, step, 0)

    columns(4, 256, normed, wq, queries, 0)
    advance(2, 1)
    start_piece(4)
    advance(1, 2)
    advance(2, 2)

    await_bytes(obs_recv.at[pl.ds(0, 189)], bulk_recv.at[0])
    await_bytes(patch_recv.at[pl.ds(0, 63)], bulk_recv.at[1])
    obs_wide[...] = obs_recv[...].astype(F32).reshape(3072, 128)
    patches = patch_recv[...].reshape(64, 128)
    slot_lane = lax.broadcasted_iota(jnp.int32, (64, 192), 1)
    slot_from = lax.broadcasted_iota(jnp.int32, (64, 192), 0) * 3
    slot_row = jnp.zeros((1, 192), F32)
    for r in range(3):
        slot_row += jnp.sum(
            jnp.where(slot_lane == slot_from + r, patches[:, r : r + 1], 0.0),
            axis=0,
            keepdims=True,
        )
    cell_patch = (lax.broadcasted_iota(jnp.int32, (128, 192), 0) // 32).astype(F32)
    same_patch = cell_patch == slot_row
    low = lax.broadcasted_iota(jnp.int32, (128, 128), 1) < 64
    zero = jnp.zeros((128, 128), BF)

    def cross_pair(g, carry):
        cols = pl.ds(mult(g * 128, 128), 128)
        keys = obs_wide[pl.ds(g, 192, stride=16), :].astype(BF)
        values = obs_wide[pl.ds(g + 8, 192, stride=16), :].astype(BF)
        both = queries[:, cols]
        found = []
        for half in (jnp.where(low, both, zero), jnp.where(low, zero, both)):
            masked = jnp.where(same_patch, dot_t(half, keys) * SCALE, -1e30)
            top = jnp.maximum(jnp.max(masked, axis=-1, keepdims=True), 0.0)
            terms = jnp.where(same_patch, jnp.exp(masked - top), 0.0)
            total = jnp.exp(-top) + jnp.sum(terms, axis=-1, keepdims=True)
            found.append(dot((terms / total).astype(BF), values))
        context[:, cols] = jnp.where(low, found[0], found[1]).astype(BF)
        return carry

    def cross_four(i, carry):
        @pl.when(i == 1)
        def _():
            advance(2, 3)
            advance(3, 1)
            advance(4, 1)

        for g in range(4):
            cross_pair(i * 4 + g, 0)
        return carry

    lax.fori_loop(0, 2, cross_four, 0)

    finish_piece(1)

    def cross_out(n, carry):
        cols = pl.ds(mult(n * 256, 256), 256)
        after_cross[:, cols] = (
            tokens[:, cols].astype(F32) + dot(context[...], wc[:, cols])
        ).astype(BF)
        return carry

    lax.fori_loop(0, 4, cross_out, 0)
    advance(3, 2)
    advance(4, 2)
    normed_axial = normalize(after_cross[...]).astype(BF)
    finish_piece(2)
    columns(6, 256, normed_axial, wkv, axial, 0)

    cell_at, group_at = z, x

    def send_lat(k, carry):
        to = (chip + k) % 32
        push(
            axial.at[pl.ds(mult((to // 4) * 16, 16), 16), pl.ds(mult((to % 4) * 384, 128), 384)],
            lat_own.at[chip],
            bulk_send.at[2],
            bulk_recv.at[2],
            to * 2 + core,
            y,
        )
        return carry

    lax.fori_loop(1, 32, send_lat, 0)
    lat_own[chip] = axial[pl.ds(mult(cell_at * 16, 16), 16), pl.ds(mult(group_at * 384, 128), 384)]

    advance(3, 3)
    finish_piece(3)
    columns(6, 256, normed_axial, wkv, axial, 1536)

    def lon_pair(p, carry):
        both = axial[:, pl.ds(mult(1536 + p * 128, 128), 128)]
        keys = axial[:, pl.ds(mult(2048 + p * 128, 128), 128)]
        values = axial[:, pl.ds(mult(2560 + p * 128, 128), 128)]
        found = []
        for half in (jnp.where(low, both, zero), jnp.where(low, zero, both)):
            scores = dot_t(half, keys) * SCALE
            terms = jnp.exp(scores - jnp.max(scores, axis=-1, keepdims=True))
            weights = (terms / jnp.sum(terms, axis=-1, keepdims=True)).astype(BF)
            found.append(dot(weights, values))
        lon_context[:, pl.ds(mult(p * 128, 128), 128)] = jnp.where(low, found[0], found[1]).astype(
            BF
        )
        return carry

    lat_kv = lat_own.at[:, :, pl.ds(128, 256)]
    await_bytes(lat_own.at[pl.ds(0, 31)], bulk_recv.at[2])
    share_start(0, cot, cot_all)
    push(lat_kv, lat_sib, bulk_send.at[3], bulk_recv.at[3], sib, y)
    lax.fori_loop(0, 4, lon_pair, 0, unroll=4)
    q_wide[...] = lat_own[:, :, 0:128].astype(F32).reshape(512, 128)
    k_wide[...] = lat_own[:, :, 128:256].astype(F32).reshape(512, 128)
    v_wide[...] = lat_own[:, :, 256:384].astype(F32).reshape(512, 128)
    await_bytes(lat_sib, bulk_recv.at[3])
    ks_wide[...] = lat_sib[:, :, 0:128].astype(F32).reshape(512, 128)
    vs_wide[...] = lat_sib[:, :, 128:256].astype(F32).reshape(512, 128)
    low_rows = lax.broadcasted_iota(jnp.int32, (32, 128), 1) < 64

    def lat_cell(l, carry):
        rows = pl.ds(l, 32, stride=16)
        q = q_wide[rows, :]
        both = jnp.concatenate(
            [jnp.where(low_rows, q, 0.0), jnp.where(low_rows, 0.0, q)], axis=0
        ).astype(BF)
        keys = jnp.concatenate([k_wide[rows, :], ks_wide[rows, :]], axis=0).astype(BF)
        values = jnp.concatenate([v_wide[rows, :], vs_wide[rows, :]], axis=0).astype(BF)
        scores = dot_t(both, keys) * SCALE
        terms = jnp.exp(scores - jnp.max(scores, axis=-1, keepdims=True))
        weights = (terms / jnp.sum(terms, axis=-1, keepdims=True)).astype(BF)
        found = dot(weights, values)
        o_wide[rows, :] = jnp.where(low_rows, found[:32], found[32:])
        return carry

    lax.fori_loop(0, 16, lat_cell, 0, unroll=8)
    lat_out[...] = o_wide[...].reshape(32, 16, 128).astype(BF)
    home = (pl.ds(mult(cell_at * 16, 16), 16), pl.ds(mult(group_at * 128, 128), 128))

    def send_back(k, carry):
        to = (chip + k) % 32
        push(
            lat_out.at[to],
            lat_context.at[home],
            bulk_send.at[4],
            bulk_recv.at[4],
            to * 2 + core,
            y,
        )
        return carry

    lax.fori_loop(1, 32, send_back, 0)
    lat_context[home] = lat_out[chip]
    finish_piece(4)

    def axial_lon(n, carry):
        cols = pl.ds(mult(n * 256, 256), 256)
        axial_sum[:, cols] = after_cross[:, cols].astype(F32) + dot(
            lon_context[...], wa[pl.ds(512, 512), cols]
        )
        return carry

    def axial_lat(n, carry):
        cols = pl.ds(mult(n * 256, 256), 256)
        context[:, cols] = (
            axial_sum[:, cols] + dot(lat_context[...], wa[pl.ds(0, 512), cols])
        ).astype(BF)
        return carry

    lax.fori_loop(0, 4, axial_lon, 0)
    await_bytes(lat_out.at[pl.ds(0, 31)], bulk_recv.at[4])
    lax.fori_loop(0, 4, axial_lat, 0)
    mine = pl.ds(mult(part * 128, 128), 128)
    normed_all[mine, :] = normalize(context[...]).astype(BF)
    share_start(1, normed_all.at[mine, :], normed_all)
    for k in range(1, 4):
        share_forward(0, cot_all, k)
    await_bytes(cot_all.at[pl.ds(0, 128), :], gather_recv.at[0, 0])
    for k in range(1, 4):
        await_bytes(from_chip(cot_all, k, 1), share_recv.at[0, k])
    wi_copy.wait()
    wo_copy.wait()
    await_bytes(normed_all.at[pl.ds(0, 128), :], gather_recv.at[1, 0])

    def ff_chip(i, carry):
        k = jnp.where(i == 2, 3, jnp.where(i == 3, 2, i))

        @pl.when(i == 1)
        def _():
            share_forward(1, normed_all, 1)
            share_forward(1, normed_all, 3)

        @pl.when(i == 2)
        def _():
            share_forward(1, normed_all, 2)

        @pl.when(i > 0)
        def _():
            await_bytes(normed_all.at[pl.ds(0, 128), :], share_recv.at[1, k])

        rows = pl.ds(mult(((x - k + 4) % 4) * 256, 256), 256)
        pre_act = dot(normed_all[rows, :], wi[...])
        hidden_grad = dot_t(cot_all[rows, :], wo[...])
        cdf = 0.5 * (1.0 + lax.erf(pre_act * ROOT_HALF))
        slope = cdf + pre_act * jnp.exp(-0.5 * pre_act * pre_act) * INV_ROOT_TWO_PI
        hidden_t[:, rows] = (pre_act * cdf).astype(BF).T
        pre_grad_t[:, rows] = (hidden_grad * slope).astype(BF).T
        return carry

    lax.fori_loop(0, 4, ff_chip, 0)

    def fold_line(source, received, at):
        for k in range(1, 8):
            push(
                source.at[(z + k) % 8],
                received.at[z],
                bulk_send.at[at],
                bulk_recv.at[at],
                ((z + k) % 8) * 8 + part,
                y,
            )
        received[z] = source[z]

    def pass_across(received, middle, ends, at, to):
        await_bytes(received.at[pl.ds(0, 7)], bulk_recv.at[at])
        for m in range(4):
            found = received[0, m].astype(F32)
            for k in range(1, 8):
                found += received[k, m].astype(F32)
            middle[m] = found.astype(BF)
        for k in range(1, 4):
            push(
                middle.at[(y + k) % 4],
                ends.at[y],
                bulk_send.at[to],
                bulk_recv.at[to],
                sp,
                (y + k) % 4,
            )
        ends[y] = middle[y]

    def fold(source, received, at):
        for k in range(1, 4):
            push(
                source.at[(y + k) % 4],
                received.at[y],
                bulk_send.at[at],
                bulk_recv.at[at],
                sp,
                (y + k) % 4,
            )
        received[y] = source[y]

    def pass_on(received, middle, ends, at, to):
        await_bytes(received.at[pl.ds(0, 3)], bulk_recv.at[at])

        def total(n, carry):
            found = received[0, n].astype(F32)
            for k in range(1, 4):
                found += received[k, n].astype(F32)
            middle[n] = found.astype(BF)
            return carry

        lax.fori_loop(0, 8, total, 0)

        def one(k, carry):
            push(
                middle.at[(z + k) % 8],
                ends.at[z],
                bulk_send.at[to],
                bulk_recv.at[to],
                ((z + k) % 8) * 8 + part,
                y,
            )
            return carry

        lax.fori_loop(1, 8, one, 0)
        ends[z] = middle[z]

    def end_sum(ends, at, count):
        await_bytes(ends.at[pl.ds(0, count - 1)], bulk_recv.at[at])
        found = ends[0].astype(F32)
        for n in range(1, count):
            found += ends[n].astype(F32)
        return found

    def grad_out_cols(n, carry):
        cols = pl.ds(mult(n * 256, 256), 256)
        grad = dot(hidden_t[...], cot_all[:, cols]).astype(BF)
        inner = pl.ds(mult((n % 2) * 256, 256), 256)
        for at in range(16):
            gout_send[(at % 2) * 2 + n // 2, at // 2, :, inner] = grad[at * 16 : at * 16 + 16]
        return carry

    lax.fori_loop(0, 4, grad_out_cols, 0)
    fold(gout_send, gout_recv, 6)

    down = lax.broadcasted_iota(jnp.int32, (128, 128), 0)
    across = lax.broadcasted_iota(jnp.int32, (128, 128), 1)
    turn = (across == ((down % 32) // 4) * 16 + (down // 32) * 4 + down % 4).astype(F32).astype(BF)

    def grad_cols(n, carry):
        cols = pl.ds(mult(n * 256, 256), 256)
        grad = dot(pre_grad_t[...], normed_all[:, cols]).astype(BF)
        for half in range(2):
            turned = dot_t(turn, grad[:, half * 128 : half * 128 + 128]).astype(BF)
            for m in range(4):
                gin_send[m, n * 2 + half] = turned[m * 32 : m * 32 + 32, :128]
                gin_right[n * 2 + half, m] = turned[m * 32 : m * 32 + 32, 128:]
        return carry

    lax.fori_loop(0, 4, grad_cols, 0)

    fold_line(gin_right, right_recv, 9)
    fold(gin_send, gin_recv, 5)
    pass_on(gout_recv, gout_mid, gout_ends, 6, 8)
    pass_on(gin_recv, gin_mid, gin_ends, 5, 7)
    pass_across(right_recv, right_mid, right_ends, 9, 10)
    sum_out = end_sum(gout_ends, 8, 8)
    sum_in = end_sum(gin_ends, 7, 8)
    sum_right = end_sum(right_ends, 10, 4)
    for n in range(8):
        fin_in_send[n, :, 0:128] = sum_in[n * 4 : n * 4 + 4]
        fin_in_send[n, :, 128:256] = sum_right[n * 4 : n * 4 + 4]
    for n in range(2):
        fin_out_send[n] = sum_out[n * 8 : n * 8 + 8]

    fin_in_recv[part] = fin_in_send[part]
    for k in range(1, 8):
        n = (part + k) % 8
        push(
            fin_in_send.at[n], fin_in_recv.at[part], last_send.at[0], last_in.at[0], z * 8 + n, y
        )
    to_sp = part * 8 + z
    odd = y % 2
    push(
        fin_out_send.at[1 - odd],
        fin_out_recv.at[odd],
        last_send.at[1],
        last_out.at[0],
        to_sp,
        y + 1 - 2 * odd,
    )

    @pl.when(part == z)
    def _():
        fin_out_recv[odd] = fin_out_send[odd]

    @pl.when(part != z)
    def _():
        push(
            fin_out_send.at[odd],
            fin_out_recv.at[odd],
            last_send.at[2],
            last_out.at[1],
            to_sp,
            y,
        )
        await_bytes(fin_out_recv.at[0], last_out.at[1])
        await_bytes(fin_out_send.at[0], last_send.at[2])

    await_bytes(fin_out_recv.at[0], last_out.at[0])
    for n in range(2):
        out_out[:, n * 512 : (n + 1) * 512] = fin_out_recv[n]
    await_bytes(fin_in_recv.at[pl.ds(0, 7)], last_in.at[0])
    for n in range(8):
        out_in[:, n * 256 : (n + 1) * 256] = fin_in_recv[n]

    for i in range(5):
        drain_piece(i)
    share_drain(0, cot_all)
    share_drain(1, normed_all)
    await_bytes(obs_recv.at[pl.ds(0, 189)], bulk_send.at[0])
    await_bytes(patch_recv.at[pl.ds(0, 63)], bulk_send.at[1])
    await_bytes(lat_own.at[pl.ds(0, 31)], bulk_send.at[2])
    await_bytes(lat_sib, bulk_send.at[3])
    await_bytes(lat_out.at[pl.ds(0, 31)], bulk_send.at[4])
    await_bytes(gin_recv.at[pl.ds(0, 3)], bulk_send.at[5])
    await_bytes(gout_recv.at[pl.ds(0, 3)], bulk_send.at[6])
    await_bytes(gin_ends.at[pl.ds(0, 7)], bulk_send.at[7])
    await_bytes(gout_ends.at[pl.ds(0, 7)], bulk_send.at[8])
    await_bytes(right_recv.at[pl.ds(0, 7)], bulk_send.at[9])
    await_bytes(right_ends.at[pl.ds(0, 3)], bulk_send.at[10])
    await_bytes(fin_in_send.at[pl.ds(0, 7)], last_send.at[0])
    await_bytes(fin_out_send.at[0], last_send.at[1])


def scratch():
    vmem = pltpu.VMEM
    dma = pltpu.SemaphoreType.DMA
    return [
        vmem((128, 1024), BF),
        vmem((128, 1024), BF),
        vmem((96, 2048), BF),
        vmem((1, 96), jnp.int32),
        vmem((1, 96), jnp.int32),
        vmem((1536, 128), F32),
        vmem((96, 16, 128), BF),
        vmem((1, 256), jnp.int32),
        pltpu.SMEM((1, 256), jnp.int32),
        vmem((64, 1, 128), F32),
        vmem((1024, 1024), BF),
        vmem((1024, 1024), BF),
        vmem((1024, 3072), BF),
        vmem((1024, 1024), BF),
        vmem((1024, 256), BF),
        vmem((256, 1024), BF),
        vmem((192, 16, 128), BF),
        vmem((192, 16, 128), BF),
        vmem((3072, 128), F32),
        vmem((64, 1, 128), F32),
        vmem((128, 1024), BF),
        vmem((128, 1024), BF),
        vmem((128, 1024), BF),
        vmem((128, 3072), BF),
        vmem((32, 16, 384), BF),
        vmem((32, 16, 256), BF),
        vmem((512, 128), F32),
        vmem((512, 128), F32),
        vmem((512, 128), F32),
        vmem((512, 128), F32),
        vmem((512, 128), F32),
        vmem((512, 128), F32),
        vmem((32, 16, 128), BF),
        vmem((128, 512), BF),
        vmem((128, 512), BF),
        vmem((128, 1024), F32),
        vmem((1024, 1024), BF),
        vmem((1024, 1024), BF),
        vmem((256, 1024), BF),
        vmem((256, 1024), BF),
        vmem((4, 8, 32, 128), BF),
        vmem((4, 8, 16, 512), BF),
        vmem((4, 8, 32, 128), BF),
        vmem((4, 8, 16, 512), BF),
        vmem((8, 32, 128), BF),
        vmem((8, 16, 512), BF),
        vmem((8, 32, 128), BF),
        vmem((8, 16, 512), BF),
        vmem((8, 4, 32, 128), BF),
        vmem((8, 4, 32, 128), BF),
        vmem((4, 32, 128), BF),
        vmem((4, 32, 128), BF),
        vmem((8, 4, 256), F32),
        vmem((8, 4, 256), F32),
        vmem((2, 8, 512), F32),
        vmem((2, 8, 512), F32),
        dma((13,)),
        dma((5, 4)),
        dma((5, 4)),
        dma((2,)),
        dma((2, 4)),
        dma((2,)),
        dma((2, 4)),
        dma((11,)),
        dma((11,)),
        dma((3,)),
        dma((1,)),
        dma((2,)),
        pltpu.SemaphoreType.REGULAR,
    ]


def local(
    grid_tokens,
    cotangent,
    obs_pairs,
    obs_route,
    obs_patch,
    w_query,
    w_cross_out,
    w_qkv,
    w_axial_out,
    w_in,
    w_out,
):
    vmem = pl.BlockSpec(memory_space=pltpu.VMEM)
    hbm = pl.BlockSpec(memory_space=pltpu.HBM)
    return pl.pallas_call(
        kernel,
        out_shape=(
            jax.ShapeDtypeStruct((4, 2048), F32),
            jax.ShapeDtypeStruct((8, 1024), F32),
        ),
        in_specs=[hbm] * 11,
        out_specs=(vmem, vmem),
        scratch_shapes=scratch(),
        compiler_params=pltpu.CompilerParams(
            collective_id=0, has_side_effects=True, vmem_limit_bytes=62 * 1024 * 1024
        ),
    )(
        grid_tokens.reshape(128, 1024),
        cotangent.reshape(128, 1024),
        obs_pairs.reshape(96, 2048),
        obs_route.reshape(1, 96),
        obs_patch.reshape(1, 96),
        w_query,
        w_cross_out,
        w_qkv,
        w_axial_out,
        w_in,
        w_out,
    )


def solution(mesh):
    return jax.shard_map(
        local,
        mesh=mesh,
        in_specs=(
            P("dp", "sp", None, None),
            P("dp", "sp", None, None),
            P("dp", "sp", None, None),
            P("dp", "sp", None, None),
            P("dp", "sp", None),
            P("dp", None),
            P("dp", None),
            P("dp", None),
            P("dp", None),
            P(),
            P(),
        ),
        out_specs=(P(("sp", "dp"), None), P(("sp", "dp"), None)),
        check_vma=False,
    )
```

```python
import jax
import jax.numpy as jnp
from jax import lax
from jax.experimental import pallas as pl
from jax.experimental.pallas import tpu as pltpu
from jax.sharding import PartitionSpec as P

BF = jnp.bfloat16
F32 = jnp.float32
EPS = 1e-06
ROOT_HALF = 0.7071067811865476
INV_ROOT_TWO_PI = 0.3989422804014327
SCALE = 0.125


def normalize(values):
    values = values.astype(F32)
    return values * lax.rsqrt(jnp.mean(values * values, axis=-1, keepdims=True) + EPS)


def dot(a, b):
    return jnp.dot(a, b, preferred_element_type=F32)


def dot_t(a, b):
    return lax.dot_general(a, b, (((1,), (1,)), ((), ())), preferred_element_type=F32)


def mult(value, by):
    return pl.multiple_of(value, by)


def push(src, dst, send, recv, sp, dp):
    pltpu.make_async_remote_copy(
        src_ref=src,
        dst_ref=dst,
        send_sem=send,
        recv_sem=recv,
        device_id={"sp": sp, "dp": dp},
        device_id_type=pl.DeviceIdType.MESH,
    ).start()


def await_bytes(ref, sem):
    pltpu.make_async_copy(ref, ref, sem).wait()


def kernel(
    tokens_hbm,
    cot_hbm,
    pairs_hbm,
    route_hbm,
    patch_hbm,
    wq_hbm,
    wc_hbm,
    wkv_hbm,
    wa_hbm,
    wi_hbm,
    wo_hbm,
    out_in,
    out_out,
    tokens,
    cot,
    pairs,
    route,
    patch,
    pairs_wide,
    pairs_tiles,
    index_row,
    src_index,
    slot_patch,
    wq,
    wc,
    wkv,
    wa,
    wi,
    wo,
    obs_send,
    obs_recv,
    obs_wide,
    patch_recv,
    queries,
    context,
    after_cross,
    axial,
    lat_own,
    lat_sib,
    q_wide,
    k_wide,
    v_wide,
    ks_wide,
    vs_wide,
    o_wide,
    lat_out,
    lat_context,
    lon_context,
    axial_sum,
    normed_all,
    cot_all,
    hidden_t,
    pre_grad_t,
    gin_send,
    gout_send,
    gin_recv,
    gout_recv,
    gin_mid,
    gout_mid,
    gin_ends,
    gout_ends,
    gin_right,
    right_recv,
    right_mid,
    right_ends,
    fin_in_send,
    fin_in_recv,
    fin_out_send,
    fin_out_recv,
    local_sem,
    w_send,
    w_recv,
    gather_send,
    gather_recv,
    share_send,
    share_recv,
    bulk_send,
    bulk_recv,
    last_send,
    last_in,
    last_out,
    entered,
):
    sp = lax.axis_index("sp")
    y = lax.axis_index("dp")
    core = sp % 2
    sib = sp + 1 - 2 * core
    chip = sp // 2
    x = chip % 4
    z = chip // 4
    part = sp % 8

    barrier = pltpu.get_barrier_semaphore()

    def greet(to_sp, to_dp):
        pl.semaphore_signal(
            barrier,
            inc=1,
            device_id={"sp": to_sp, "dp": to_dp},
            device_id_type=pl.DeviceIdType.MESH,
        )

    def greet_line(k, carry):
        greet(((z + k) % 8) * 8 + part, y)
        greet(z * 8 + (part + k) % 8, y)
        return carry

    lax.fori_loop(1, 8, greet_line, 0)
    for k in range(1, 4):
        greet(sp, (y + k) % 4)
    greet(part * 8 + z, y + 1 - 2 * (y % 2))

    loads = [
        pltpu.make_async_copy(source, target, local_sem.at[7 + i])
        for i, (source, target) in enumerate(
            (
                (route_hbm, route),
                (patch_hbm, patch),
                (pairs_hbm, pairs),
                (tokens_hbm, tokens),
                (cot_hbm, cot),
            )
        )
    ]
    for load in loads:
        load.start()

    pieces = (
        (wq_hbm, wq, 0, 1024, "x"),
        (wc_hbm, wc, 0, 1024, "x"),
        (wkv_hbm, wkv, 0, 1536, "x"),
        (wkv_hbm, wkv, 1536, 1536, "xz"),
        (wa_hbm, wa, 0, 1024, "zx"),
    )
    place_of = {"x": (x + core) % 2, "z": (z + core) % 2}
    mate_of = {
        "x": z * 8 + ((x + 5 - 2 * place_of["x"]) % 4) * 2 + core,
        "z": ((z + 9 - 2 * place_of["z"]) % 8) * 8 + x * 2 + core,
    }

    def spans(plan):
        rows = 128 >> len(plan)
        first = core * 128
        for n, axis in enumerate(plan):
            first += place_of[axis] * (rows << n)
        made = [(first, rows, None)]
        for n, axis in enumerate(plan):
            made.append((first, rows << n, mate_of[axis]))
            first -= place_of[axis] * (rows << n)
        made.append((core * 128, 128, sib))
        return made

    stages = [spans(piece[4]) for piece in pieces]

    def landing(i, stage):
        full, col, width = pieces[i][1:4]
        return full.at[pl.ds(0, 3 * stages[i][stage][1]), pl.ds(col, width)]

    def start_piece(i):
        hbm, full, col, width, _ = pieces[i]
        first, rows, _ = stages[i][0]
        for k in range(1, 4):
            push(
                hbm.at[pl.ds(mult(first, 32), rows), pl.ds(col, width)],
                full.at[pl.ds(mult(y * 256 + first, 32), rows), pl.ds(col, width)],
                w_send.at[i, 0],
                w_recv.at[i, 0],
                sp,
                (y + k) % 4,
            )

    def own_piece(i):
        hbm, full, col, width, _ = pieces[i]
        return pltpu.make_async_copy(
            hbm.at[:, pl.ds(col, width)],
            full.at[pl.ds(mult(y * 256, 256), 256), pl.ds(col, width)],
            local_sem.at[i],
        )

    def advance(i, stage):
        full, col, width = pieces[i][1:4]
        await_bytes(landing(i, stage - 1), w_recv.at[i, stage - 1])
        first, rows, mate = stages[i][stage]
        for k in range(1, 4):
            part_rows = full.at[
                pl.ds(mult(((y + k) % 4) * 256 + first, 32), rows), pl.ds(col, width)
            ]
            push(part_rows, part_rows, w_send.at[i, stage], w_recv.at[i, stage], mate, y)

    def finish_piece(i):
        last = len(stages[i]) - 1
        await_bytes(landing(i, last), w_recv.at[i, last])
        own_piece(i).wait()

    def drain_piece(i):
        for stage in range(len(stages[i])):
            await_bytes(landing(i, stage), w_send.at[i, stage])

    for i in range(5):
        own_piece(i).start()
    wi_copy = pltpu.make_async_copy(
        wi_hbm.at[:, pl.ds(mult(part * 256, 256), 256)], wi, local_sem.at[5]
    )
    wo_copy = pltpu.make_async_copy(
        wo_hbm.at[pl.ds(mult(part * 256, 256), 256), :], wo, local_sem.at[6]
    )
    wi_copy.start()
    wo_copy.start()

    loads[0].wait()
    loads[1].wait()
    line = lax.broadcasted_iota(jnp.int32, (96, 96), 0)
    lane = lax.broadcasted_iota(jnp.int32, (96, 96), 1)

    def upright(row):
        return jnp.sum(jnp.where(line == lane, row, 0), axis=1, keepdims=True)

    row_across = route[...]
    row_down = upright(row_across)
    patch_across = patch[...] + 1
    same = row_across == row_down
    rank_across = jnp.sum(jnp.where(same & (line < lane), 1, 0), axis=0, keepdims=True)
    rank_down = jnp.sum(jnp.where(same & (lane < line), 1, 0), axis=1, keepdims=True)
    slot_across = row_across * 3 + rank_across
    slot_down = row_down * 3 + rank_down
    hit = slot_down == lax.broadcasted_iota(jnp.int32, (96, 256), 1)
    index_row[...] = jnp.sum(
        jnp.where(hit, lax.broadcasted_iota(jnp.int32, (96, 256), 0), 0), axis=0, keepdims=True
    )
    index_copy = pltpu.make_async_copy(index_row, src_index, local_sem.at[12])
    index_copy.start()
    lanes = lax.broadcasted_iota(jnp.int32, (64, 128), 1)
    found_patch = jnp.zeros((64, 128), jnp.int32)
    for r in range(3):
        mine = slot_across == lax.broadcasted_iota(jnp.int32, (64, 96), 0) * 3 + r
        value = jnp.sum(jnp.where(mine, patch_across, 0), axis=1, keepdims=True) - 1
        found_patch = jnp.where(lanes == r, value, found_patch)
    slot_patch[...] = found_patch.astype(F32).reshape(64, 1, 128)

    pl.semaphore_wait(barrier, 18)

    def greet_again(k, carry):
        pl.semaphore_signal(
            entered,
            inc=1,
            device_id={"sp": z * 8 + (part + k) % 8, "dp": y},
            device_id_type=pl.DeviceIdType.MESH,
        )
        return carry

    lax.fori_loop(1, 8, greet_again, 0)

    loads[2].wait()
    for n in range(16):
        pairs_wide[pl.ds(n, 96, stride=16), :] = pairs[:, n * 128 : (n + 1) * 128].astype(F32)
    pairs_tiles[...] = pairs_wide[...].reshape(96, 16, 128).astype(BF)
    index_copy.wait()

    def place(s, carry):
        obs_send[s] = pairs_tiles[src_index[0, s]]
        return carry

    lax.fori_loop(0, 192, place, 0, unroll=8)
    pl.semaphore_wait(entered, 7)
    start_piece(0)
    start_piece(1)
    start_piece(2)
    start_piece(3)
    start_piece(4)

    def send_obs(k, carry):
        to = (sp + k) % 64
        push(
            obs_send.at[pl.ds(to * 3, 3)],
            obs_recv.at[pl.ds(sp * 3, 3)],
            bulk_send.at[0],
            bulk_recv.at[0],
            to,
            y,
        )
        push(slot_patch.at[to], patch_recv.at[sp], bulk_send.at[1], bulk_recv.at[1], to, y)
        return carry

    lax.fori_loop(1, 64, send_obs, 0)
    obs_recv[pl.ds(sp * 3, 3)] = obs_send[pl.ds(sp * 3, 3)]
    patch_recv[sp] = slot_patch[sp]

    def share_start(j, source, full):
        rows = full.at[pl.ds(mult(part * 128, 128), 128), :]
        push(source, rows, gather_send.at[j], gather_recv.at[j, 0], sib, y)
        for k in range(1, 4):
            push(
                source,
                rows,
                gather_send.at[j],
                gather_recv.at[j, k],
                z * 8 + ((x + k) % 4) * 2 + core,
                y,
            )

    def from_chip(full, k, cores):
        first = ((x - k + 4) % 4) * 256 + (core * 128 if cores == 1 else 0)
        return full.at[pl.ds(mult(first, 128), 128 * cores), :]

    def share_forward(j, full, k):
        rows = from_chip(full, k, 1)
        await_bytes(rows, gather_recv.at[j, k])
        push(rows, rows, share_send.at[j], share_recv.at[j, k], sib, y)

    def share_drain(j, full):
        await_bytes(full.at[pl.ds(0, 512), :], gather_send.at[j])
        await_bytes(full.at[pl.ds(0, 384), :], share_send.at[j])

    loads[3].wait()
    loads[4].wait()
    cot_all[pl.ds(mult(part * 128, 128), 128), :] = cot[...]

    normed = normalize(tokens[...]).astype(BF)
    advance(0, 1)
    advance(1, 1)
    advance(0, 2)
    finish_piece(0)

    def columns(count, width, source, weight, target, offset):
        def step(n, carry):
            cols = pl.ds(mult(offset + n * width, width), width)
            target[:, cols] = dot(source, weight[:, cols]).astype(BF)
            return carry

        lax.fori_loop(0, count, step, 0)

    columns(4, 256, normed, wq, queries, 0)
    advance(2, 1)
    advance(1, 2)
    advance(2, 2)
    advance(3, 1)
    advance(4, 1)

    await_bytes(obs_recv.at[pl.ds(0, 189)], bulk_recv.at[0])
    await_bytes(patch_recv.at[pl.ds(0, 63)], bulk_recv.at[1])
    obs_wide[...] = obs_recv[...].astype(F32).reshape(3072, 128)
    patches = patch_recv[...].reshape(64, 128)
    slot_lane = lax.broadcasted_iota(jnp.int32, (64, 192), 1)
    slot_from = lax.broadcasted_iota(jnp.int32, (64, 192), 0) * 3
    slot_row = jnp.zeros((1, 192), F32)
    for r in range(3):
        slot_row += jnp.sum(
            jnp.where(slot_lane == slot_from + r, patches[:, r : r + 1], 0.0),
            axis=0,
            keepdims=True,
        )
    cell_patch = (lax.broadcasted_iota(jnp.int32, (128, 192), 0) // 32).astype(F32)
    same_patch = cell_patch == slot_row
    low = lax.broadcasted_iota(jnp.int32, (128, 128), 1) < 64
    zero = jnp.zeros((128, 128), BF)

    def cross_pair(g, carry):
        cols = pl.ds(mult(g * 128, 128), 128)
        keys = obs_wide[pl.ds(g, 192, stride=16), :].astype(BF)
        values = obs_wide[pl.ds(g + 8, 192, stride=16), :].astype(BF)
        both = queries[:, cols]
        found = []
        for half in (jnp.where(low, both, zero), jnp.where(low, zero, both)):
            masked = jnp.where(same_patch, dot_t(half, keys) * SCALE, -1e30)
            top = jnp.maximum(jnp.max(masked, axis=-1, keepdims=True), 0.0)
            terms = jnp.where(same_patch, jnp.exp(masked - top), 0.0)
            total = jnp.exp(-top) + jnp.sum(terms, axis=-1, keepdims=True)
            found.append(dot((terms / total).astype(BF), values))
        context[:, cols] = jnp.where(low, found[0], found[1]).astype(BF)
        return carry

    def cross_four(i, carry):
        @pl.when(i == 1)
        def _():
            advance(3, 2)
            advance(4, 2)

        for g in range(4):
            cross_pair(i * 4 + g, 0)
        return carry

    lax.fori_loop(0, 2, cross_four, 0)

    finish_piece(1)

    def cross_out(n, carry):
        cols = pl.ds(mult(n * 256, 256), 256)
        after_cross[:, cols] = (
            tokens[:, cols].astype(F32) + dot(context[...], wc[:, cols])
        ).astype(BF)
        return carry

    lax.fori_loop(0, 4, cross_out, 0)
    advance(3, 3)
    advance(4, 3)
    normed_axial = normalize(after_cross[...]).astype(BF)
    finish_piece(2)
    columns(6, 256, normed_axial, wkv, axial, 0)

    cell_at, group_at = z, x

    def send_lat(k, carry):
        to = (chip + k) % 32
        push(
            axial.at[pl.ds(mult((to // 4) * 16, 16), 16), pl.ds(mult((to % 4) * 384, 128), 384)],
            lat_own.at[chip],
            bulk_send.at[2],
            bulk_recv.at[2],
            to * 2 + core,
            y,
        )
        return carry

    lax.fori_loop(1, 32, send_lat, 0)
    lat_own[chip] = axial[pl.ds(mult(cell_at * 16, 16), 16), pl.ds(mult(group_at * 384, 128), 384)]

    finish_piece(3)
    columns(6, 256, normed_axial, wkv, axial, 1536)

    def lon_pair(p, carry):
        both = axial[:, pl.ds(mult(1536 + p * 128, 128), 128)]
        keys = axial[:, pl.ds(mult(2048 + p * 128, 128), 128)]
        values = axial[:, pl.ds(mult(2560 + p * 128, 128), 128)]
        found = []
        for half in (jnp.where(low, both, zero), jnp.where(low, zero, both)):
            scores = dot_t(half, keys) * SCALE
            terms = jnp.exp(scores - jnp.max(scores, axis=-1, keepdims=True))
            weights = (terms / jnp.sum(terms, axis=-1, keepdims=True)).astype(BF)
            found.append(dot(weights, values))
        lon_context[:, pl.ds(mult(p * 128, 128), 128)] = jnp.where(low, found[0], found[1]).astype(
            BF
        )
        return carry

    lat_kv = lat_own.at[:, :, pl.ds(128, 256)]
    await_bytes(lat_own.at[pl.ds(0, 31)], bulk_recv.at[2])
    share_start(0, cot, cot_all)
    push(lat_kv, lat_sib, bulk_send.at[3], bulk_recv.at[3], sib, y)
    lax.fori_loop(0, 4, lon_pair, 0, unroll=4)
    q_wide[...] = lat_own[:, :, 0:128].astype(F32).reshape(512, 128)
    k_wide[...] = lat_own[:, :, 128:256].astype(F32).reshape(512, 128)
    v_wide[...] = lat_own[:, :, 256:384].astype(F32).reshape(512, 128)
    await_bytes(lat_sib, bulk_recv.at[3])
    ks_wide[...] = lat_sib[:, :, 0:128].astype(F32).reshape(512, 128)
    vs_wide[...] = lat_sib[:, :, 128:256].astype(F32).reshape(512, 128)
    low_rows = lax.broadcasted_iota(jnp.int32, (32, 128), 1) < 64

    def lat_cell(l, carry):
        rows = pl.ds(l, 32, stride=16)
        q = q_wide[rows, :]
        both = jnp.concatenate(
            [jnp.where(low_rows, q, 0.0), jnp.where(low_rows, 0.0, q)], axis=0
        ).astype(BF)
        keys = jnp.concatenate([k_wide[rows, :], ks_wide[rows, :]], axis=0).astype(BF)
        values = jnp.concatenate([v_wide[rows, :], vs_wide[rows, :]], axis=0).astype(BF)
        scores = dot_t(both, keys) * SCALE
        terms = jnp.exp(scores - jnp.max(scores, axis=-1, keepdims=True))
        weights = (terms / jnp.sum(terms, axis=-1, keepdims=True)).astype(BF)
        found = dot(weights, values)
        o_wide[rows, :] = jnp.where(low_rows, found[:32], found[32:])
        return carry

    lax.fori_loop(0, 16, lat_cell, 0, unroll=8)
    lat_out[...] = o_wide[...].reshape(32, 16, 128).astype(BF)
    home = (pl.ds(mult(cell_at * 16, 16), 16), pl.ds(mult(group_at * 128, 128), 128))

    def send_back(k, carry):
        to = (chip + k) % 32
        push(
            lat_out.at[to],
            lat_context.at[home],
            bulk_send.at[4],
            bulk_recv.at[4],
            to * 2 + core,
            y,
        )
        return carry

    lax.fori_loop(1, 32, send_back, 0)
    lat_context[home] = lat_out[chip]
    finish_piece(4)

    def axial_lon(n, carry):
        cols = pl.ds(mult(n * 256, 256), 256)
        axial_sum[:, cols] = after_cross[:, cols].astype(F32) + dot(
            lon_context[...], wa[pl.ds(512, 512), cols]
        )
        return carry

    def axial_lat(n, carry):
        cols = pl.ds(mult(n * 256, 256), 256)
        context[:, cols] = (
            axial_sum[:, cols] + dot(lat_context[...], wa[pl.ds(0, 512), cols])
        ).astype(BF)
        return carry

    lax.fori_loop(0, 4, axial_lon, 0)
    await_bytes(lat_out.at[pl.ds(0, 31)], bulk_recv.at[4])
    lax.fori_loop(0, 4, axial_lat, 0)
    mine = pl.ds(mult(part * 128, 128), 128)
    normed_all[mine, :] = normalize(context[...]).astype(BF)
    share_start(1, normed_all.at[mine, :], normed_all)
    for k in range(1, 4):
        share_forward(0, cot_all, k)
    await_bytes(cot_all.at[pl.ds(0, 128), :], gather_recv.at[0, 0])
    for k in range(1, 4):
        await_bytes(from_chip(cot_all, k, 1), share_recv.at[0, k])
    wi_copy.wait()
    wo_copy.wait()
    await_bytes(normed_all.at[pl.ds(0, 128), :], gather_recv.at[1, 0])

    def ff_chip(i, carry):
        k = jnp.where(i == 2, 3, jnp.where(i == 3, 2, i))

        @pl.when(i == 1)
        def _():
            share_forward(1, normed_all, 1)
            share_forward(1, normed_all, 3)

        @pl.when(i == 2)
        def _():
            share_forward(1, normed_all, 2)

        @pl.when(i > 0)
        def _():
            await_bytes(normed_all.at[pl.ds(0, 128), :], share_recv.at[1, k])

        rows = pl.ds(mult(((x - k + 4) % 4) * 256, 256), 256)
        pre_act = dot(normed_all[rows, :], wi[...])
        hidden_grad = dot_t(cot_all[rows, :], wo[...])
        cdf = 0.5 * (1.0 + lax.erf(pre_act * ROOT_HALF))
        slope = cdf + pre_act * jnp.exp(-0.5 * pre_act * pre_act) * INV_ROOT_TWO_PI
        hidden_t[:, rows] = (pre_act * cdf).astype(BF).T
        pre_grad_t[:, rows] = (hidden_grad * slope).astype(BF).T
        return carry

    lax.fori_loop(0, 4, ff_chip, 0)

    def fold_line(source, received, at):
        for k in range(1, 8):
            push(
                source.at[(z + k) % 8],
                received.at[z],
                bulk_send.at[at],
                bulk_recv.at[at],
                ((z + k) % 8) * 8 + part,
                y,
            )
        received[z] = source[z]

    def pass_across(received, middle, ends, at, to):
        await_bytes(received.at[pl.ds(0, 7)], bulk_recv.at[at])
        for m in range(4):
            found = received[0, m].astype(F32)
            for k in range(1, 8):
                found += received[k, m].astype(F32)
            middle[m] = found.astype(BF)
        for k in range(1, 4):
            push(
                middle.at[(y + k) % 4],
                ends.at[y],
                bulk_send.at[to],
                bulk_recv.at[to],
                sp,
                (y + k) % 4,
            )
        ends[y] = middle[y]

    def fold(source, received, at):
        for k in range(1, 4):
            push(
                source.at[(y + k) % 4],
                received.at[y],
                bulk_send.at[at],
                bulk_recv.at[at],
                sp,
                (y + k) % 4,
            )
        received[y] = source[y]

    def pass_on(received, middle, ends, at, to):
        await_bytes(received.at[pl.ds(0, 3)], bulk_recv.at[at])

        def total(n, carry):
            found = received[0, n].astype(F32)
            for k in range(1, 4):
                found += received[k, n].astype(F32)
            middle[n] = found.astype(BF)
            return carry

        lax.fori_loop(0, 8, total, 0)

        def one(k, carry):
            push(
                middle.at[(z + k) % 8],
                ends.at[z],
                bulk_send.at[to],
                bulk_recv.at[to],
                ((z + k) % 8) * 8 + part,
                y,
            )
            return carry

        lax.fori_loop(1, 8, one, 0)
        ends[z] = middle[z]

    def end_sum(ends, at, count):
        await_bytes(ends.at[pl.ds(0, count - 1)], bulk_recv.at[at])
        found = ends[0].astype(F32)
        for n in range(1, count):
            found += ends[n].astype(F32)
        return found

    def grad_out_cols(n, carry):
        cols = pl.ds(mult(n * 256, 256), 256)
        grad = dot(hidden_t[...], cot_all[:, cols]).astype(BF)
        inner = pl.ds(mult((n % 2) * 256, 256), 256)
        for at in range(16):
            gout_send[(at % 2) * 2 + n // 2, at // 2, :, inner] = grad[at * 16 : at * 16 + 16]
        return carry

    lax.fori_loop(0, 4, grad_out_cols, 0)
    fold(gout_send, gout_recv, 6)

    down = lax.broadcasted_iota(jnp.int32, (128, 128), 0)
    across = lax.broadcasted_iota(jnp.int32, (128, 128), 1)
    turn = (across == ((down % 32) // 4) * 16 + (down // 32) * 4 + down % 4).astype(F32).astype(BF)

    def grad_cols(n, carry):
        cols = pl.ds(mult(n * 256, 256), 256)
        grad = dot(pre_grad_t[...], normed_all[:, cols]).astype(BF)
        for half in range(2):
            turned = dot_t(turn, grad[:, half * 128 : half * 128 + 128]).astype(BF)
            for m in range(4):
                gin_send[m, n * 2 + half] = turned[m * 32 : m * 32 + 32, :128]
                gin_right[n * 2 + half, m] = turned[m * 32 : m * 32 + 32, 128:]
        return carry

    lax.fori_loop(0, 4, grad_cols, 0)

    fold_line(gin_right, right_recv, 9)
    fold(gin_send, gin_recv, 5)
    pass_on(gout_recv, gout_mid, gout_ends, 6, 8)
    pass_on(gin_recv, gin_mid, gin_ends, 5, 7)
    pass_across(right_recv, right_mid, right_ends, 9, 10)
    sum_out = end_sum(gout_ends, 8, 8)
    sum_in = end_sum(gin_ends, 7, 8)
    sum_right = end_sum(right_ends, 10, 4)
    for n in range(8):
        fin_in_send[n, :, 0:128] = sum_in[n * 4 : n * 4 + 4]
        fin_in_send[n, :, 128:256] = sum_right[n * 4 : n * 4 + 4]
    for n in range(2):
        fin_out_send[n] = sum_out[n * 8 : n * 8 + 8]

    fin_in_recv[part] = fin_in_send[part]
    for k in range(1, 8):
        n = (part + k) % 8
        push(
            fin_in_send.at[n], fin_in_recv.at[part], last_send.at[0], last_in.at[0], z * 8 + n, y
        )
    to_sp = part * 8 + z
    odd = y % 2
    push(
        fin_out_send.at[1 - odd],
        fin_out_recv.at[odd],
        last_send.at[1],
        last_out.at[0],
        to_sp,
        y + 1 - 2 * odd,
    )

    @pl.when(part == z)
    def _():
        fin_out_recv[odd] = fin_out_send[odd]

    @pl.when(part != z)
    def _():
        push(
            fin_out_send.at[odd],
            fin_out_recv.at[odd],
            last_send.at[2],
            last_out.at[1],
            to_sp,
            y,
        )
        await_bytes(fin_out_recv.at[0], last_out.at[1])
        await_bytes(fin_out_send.at[0], last_send.at[2])

    await_bytes(fin_out_recv.at[0], last_out.at[0])
    for n in range(2):
        out_out[:, n * 512 : (n + 1) * 512] = fin_out_recv[n]
    await_bytes(fin_in_recv.at[pl.ds(0, 7)], last_in.at[0])
    for n in range(8):
        out_in[:, n * 256 : (n + 1) * 256] = fin_in_recv[n]

    for i in range(5):
        drain_piece(i)
    share_drain(0, cot_all)
    share_drain(1, normed_all)
    await_bytes(obs_recv.at[pl.ds(0, 189)], bulk_send.at[0])
    await_bytes(patch_recv.at[pl.ds(0, 63)], bulk_send.at[1])
    await_bytes(lat_own.at[pl.ds(0, 31)], bulk_send.at[2])
    await_bytes(lat_sib, bulk_send.at[3])
    await_bytes(lat_out.at[pl.ds(0, 31)], bulk_send.at[4])
    await_bytes(gin_recv.at[pl.ds(0, 3)], bulk_send.at[5])
    await_bytes(gout_recv.at[pl.ds(0, 3)], bulk_send.at[6])
    await_bytes(gin_ends.at[pl.ds(0, 7)], bulk_send.at[7])
    await_bytes(gout_ends.at[pl.ds(0, 7)], bulk_send.at[8])
    await_bytes(right_recv.at[pl.ds(0, 7)], bulk_send.at[9])
    await_bytes(right_ends.at[pl.ds(0, 3)], bulk_send.at[10])
    await_bytes(fin_in_send.at[pl.ds(0, 7)], last_send.at[0])
    await_bytes(fin_out_send.at[0], last_send.at[1])


def scratch():
    vmem = pltpu.VMEM
    dma = pltpu.SemaphoreType.DMA
    return [
        vmem((128, 1024), BF),
        vmem((128, 1024), BF),
        vmem((96, 2048), BF),
        vmem((1, 96), jnp.int32),
        vmem((1, 96), jnp.int32),
        vmem((1536, 128), F32),
        vmem((96, 16, 128), BF),
        vmem((1, 256), jnp.int32),
        pltpu.SMEM((1, 256), jnp.int32),
        vmem((64, 1, 128), F32),
        vmem((1024, 1024), BF),
        vmem((1024, 1024), BF),
        vmem((1024, 3072), BF),
        vmem((1024, 1024), BF),
        vmem((1024, 256), BF),
        vmem((256, 1024), BF),
        vmem((192, 16, 128), BF),
        vmem((192, 16, 128), BF),
        vmem((3072, 128), F32),
        vmem((64, 1, 128), F32),
        vmem((128, 1024), BF),
        vmem((128, 1024), BF),
        vmem((128, 1024), BF),
        vmem((128, 3072), BF),
        vmem((32, 16, 384), BF),
        vmem((32, 16, 256), BF),
        vmem((512, 128), F32),
        vmem((512, 128), F32),
        vmem((512, 128), F32),
        vmem((512, 128), F32),
        vmem((512, 128), F32),
        vmem((512, 128), F32),
        vmem((32, 16, 128), BF),
        vmem((128, 512), BF),
        vmem((128, 512), BF),
        vmem((128, 1024), F32),
        vmem((1024, 1024), BF),
        vmem((1024, 1024), BF),
        vmem((256, 1024), BF),
        vmem((256, 1024), BF),
        vmem((4, 8, 32, 128), BF),
        vmem((4, 8, 16, 512), BF),
        vmem((4, 8, 32, 128), BF),
        vmem((4, 8, 16, 512), BF),
        vmem((8, 32, 128), BF),
        vmem((8, 16, 512), BF),
        vmem((8, 32, 128), BF),
        vmem((8, 16, 512), BF),
        vmem((8, 4, 32, 128), BF),
        vmem((8, 4, 32, 128), BF),
        vmem((4, 32, 128), BF),
        vmem((4, 32, 128), BF),
        vmem((8, 4, 256), F32),
        vmem((8, 4, 256), F32),
        vmem((2, 8, 512), F32),
        vmem((2, 8, 512), F32),
        dma((13,)),
        dma((5, 4)),
        dma((5, 4)),
        dma((2,)),
        dma((2, 4)),
        dma((2,)),
        dma((2, 4)),
        dma((11,)),
        dma((11,)),
        dma((3,)),
        dma((1,)),
        dma((2,)),
        pltpu.SemaphoreType.REGULAR,
    ]


def local(
    grid_tokens,
    cotangent,
    obs_pairs,
    obs_route,
    obs_patch,
    w_query,
    w_cross_out,
    w_qkv,
    w_axial_out,
    w_in,
    w_out,
):
    vmem = pl.BlockSpec(memory_space=pltpu.VMEM)
    hbm = pl.BlockSpec(memory_space=pltpu.HBM)
    return pl.pallas_call(
        kernel,
        out_shape=(
            jax.ShapeDtypeStruct((4, 2048), F32),
            jax.ShapeDtypeStruct((8, 1024), F32),
        ),
        in_specs=[hbm] * 11,
        out_specs=(vmem, vmem),
        scratch_shapes=scratch(),
        compiler_params=pltpu.CompilerParams(
            collective_id=0, has_side_effects=True, vmem_limit_bytes=62 * 1024 * 1024
        ),
    )(
        grid_tokens.reshape(128, 1024),
        cotangent.reshape(128, 1024),
        obs_pairs.reshape(96, 2048),
        obs_route.reshape(1, 96),
        obs_patch.reshape(1, 96),
        w_query,
        w_cross_out,
        w_qkv,
        w_axial_out,
        w_in,
        w_out,
    )


def solution(mesh):
    return jax.shard_map(
        local,
        mesh=mesh,
        in_specs=(
            P("dp", "sp", None, None),
            P("dp", "sp", None, None),
            P("dp", "sp", None, None),
            P("dp", "sp", None, None),
            P("dp", "sp", None),
            P("dp", None),
            P("dp", None),
            P("dp", None),
            P("dp", None),
            P(),
            P(),
        ),
        out_specs=(P(("sp", "dp"), None), P(("sp", "dp"), None)),
        check_vma=False,
    )
```
